256 devices in a mesh: grp: 2 (over z_lo), dp: 32 (over z_hi, y, core), sp: 4 (over x).
Axes of the slice: x: 4, y: 4, z: 8 (z_hi: 4, z_lo: 2; z = z_hi * 2 + z_lo), core: 2. Of those that a mesh axis runs over, the one named last changes fastest.
Arguments:
- phase_mask: float32 [1024, 1024], P(None, 'sp'), may hold values from -3 to 3
- height_offsets: int32 [4, 1024, 1024], P(None, None, 'sp'), may hold values from -4 to 4
- sample_ids: int32 [32], P('dp'), may hold values from 0 to 3
- wavelength_ids: int32 [32], P('dp'), may hold values from 0 to 30
- scene: float32 [32, 1024, 1024], P('dp', 'sp'), may hold values from -6 to 6
- w_first: float32 [32, 9], replicated, may hold values from -2 to 2
- b_first: float32 [32], replicated, may hold values from -3 to 3
- w_second: float32 [9, 32], replicated, may hold values from -0.375 to 0.375
Outputs:
- mask_grad: float32 [1024, 1024], P(None, 'sp')
- w_first_grad: float32 [32, 9], replicated
- b_first_grad: float32 [32], replicated
- w_second_grad: float32 [9, 32], replicated
- loss: float32 [], replicated
The draws below stay inside these ranges and needn't reach their ends.
All inputs are finite; a program needn't handle non-finite values.
Results may differ from the reference program's by a relative error of at most 0.00018.
Values sent between devices are 32-bit elements; how exact they have to be, the bound alone decides.
No kernel may reach another device: no remote copies, remote signals or barrier semaphores. Data moves between devices by JAX's collectives and lax.ppermute only.
A program may use at most 128 MiB of HBM per device.

```python
import jax
import jax.numpy as jnp
import numpy as np
from jax import lax

GRID = 1024
CROP = 128
CHAN = 32
SAMPLES = 4
WAVES = 31
IMAGES = 32


def set_ends(drawn, rng, low, high):
    dims = drawn.shape
    spot = [jax.random.randint(jax.random.fold_in(rng, axis), (), 0, dims[axis]) for axis in range(len(dims))]
    drawn = drawn.at[tuple(spot)].set(low)
    longest = dims.index(max(dims))
    spot[longest] = (spot[longest] + 1) % dims[longest]
    return drawn.at[tuple(spot)].set(high)


def level_of(key, dims, shards, low, high):
    gain = 1.0
    for axis_at, parts in shards:
        steps = jax.random.uniform(jax.random.fold_in(jax.random.fold_in(key, 6), axis_at), (parts,), jnp.float32, low / len(shards), high / len(shards))
        gain = gain * jnp.repeat(jnp.exp(steps), dims[axis_at] // parts).reshape((-1,) + (1,) * (len(dims) - 1 - axis_at))
    return gain


def bell_draw(own_key, extent, deviation, limit, split=(), dtype=jnp.bfloat16):
    gain = level_of(own_key, extent, split, -0.22, 0.18) if split else 1.0
    entries = jax.random.normal(own_key, extent, jnp.float32) * deviation * gain
    return jnp.minimum(jnp.maximum(entries, -limit), limit).astype(dtype)


def setup_inputs(seed: int = 0) -> dict:
    key_of = jax.random.split(jax.random.key(seed), 9)
    return {
        "phase_mask": bell_draw(key_of[0], (GRID, GRID), 0.5, 3.0, ((1, 4),), jnp.float32),
        "height_offsets": set_ends(jax.random.randint(key_of[1], (SAMPLES, GRID, GRID), -4, 5), jax.random.fold_in(key_of[1], 1), -4, 4).astype(jnp.int32),
        "sample_ids": set_ends(jax.random.randint(key_of[2], (IMAGES,), 0, SAMPLES), jax.random.fold_in(key_of[2], 1), 0, SAMPLES - 1).astype(jnp.int32),
        "wavelength_ids": set_ends(jax.random.randint(key_of[3], (IMAGES,), 0, WAVES), jax.random.fold_in(key_of[3], 1), 0, WAVES - 1).astype(jnp.int32),
        "scene": bell_draw(key_of[4], (IMAGES, GRID, GRID), 1.0, 6.0, ((0, 32), (1, 4)), jnp.float32),
        "w_first": bell_draw(key_of[5], (CHAN, 9), 9 ** -0.5, 2.0, (), jnp.float32),
        "b_first": bell_draw(key_of[6], (CHAN,), 0.5, 3.0, (), jnp.float32),
        "w_second": bell_draw(key_of[7], (9, CHAN), (9 * CHAN) ** -0.5, 0.375, (), jnp.float32),
    }


highest = lax.Precision.HIGHEST
tap_shifts = ((-1, -1), (-1, 0), (-1, 1), (0, -1), (0, 0), (0, 1), (1, -1), (1, 0), (1, 1))

def contract(pattern, matrix, operand):
    return jnp.einsum(pattern, matrix, operand, precision=highest)

def pupil_count(size_grid):
    coords = np.arange(size_grid) * 2 - size_grid + 1
    inside = (coords[:, None] ** 2 + coords[None, :] ** 2) * 4 <= size_grid * size_grid
    return float(np.sum(inside))

def pupil_plane(size_grid, col_start, columns):
    row_ids = lax.broadcasted_iota(jnp.int32, (size_grid, columns), 0) * 2 - size_grid + 1
    col_ids = (lax.broadcasted_iota(jnp.int32, (size_grid, columns), 1) + col_start) * 2 - size_grid + 1
    return jnp.where((row_ids * row_ids + col_ids * col_ids) * 4 <= size_grid * size_grid, 1.0, 0.0).astype(jnp.float32)

def cross_taps(plane, rows_out):
    columns = plane.shape[-1]
    padded = jnp.pad(plane, ((0, 0), (1, 1)))
    return jnp.stack([padded[1 + row_step:1 + row_step + rows_out, 1 + col_step:1 + col_step + columns] for row_step, col_step in tap_shifts])

def gather_taps(stacked, rows_out):
    columns = stacked.shape[-1]
    padded = jnp.pad(stacked, ((0, 0), (0, 0), (1, 1)))
    summed = jnp.zeros((rows_out, columns), jnp.float32)
    for tap_index in range(9):
        row_step, col_step = tap_shifts[tap_index]
        summed = summed + padded[tap_index, 1 + row_step:1 + row_step + rows_out, 1 + col_step:1 + col_step + columns]
    return summed

def image_loss(phase_mask, w_first, b_first, w_second, offsets, ratio_wave, scene_image, aperture, pupils):
    phase_map = ratio_wave * (phase_mask + 0.1 * offsets)
    pupil_field = aperture * jnp.exp(1j * phase_map)
    far_field = jnp.fft.fft2(pupil_field)
    spread_psf = (jnp.real(far_field) ** 2 + jnp.imag(far_field) ** 2) / (GRID * GRID * pupils)
    blurred = jnp.real(jnp.fft.ifft2(jnp.fft.fft2(scene_image) * jnp.fft.fft2(spread_psf)))
    start_col = GRID // 4
    window = blurred[:, start_col:start_col + CROP]
    target = scene_image[:, start_col:start_col + CROP]
    window_taps = cross_taps(jnp.pad(window, ((1, 1), (0, 0))), GRID)
    pre_act = contract('ct,trw->crw', w_first, window_taps) + b_first[:, None, None]
    hidden = jax.nn.relu(pre_act)
    spread = contract('tc,crw->trw', w_second, hidden)
    restored = window + gather_taps(jnp.pad(spread, ((0, 0), (1, 1), (0, 0))), GRID)
    residual = restored - target
    return jnp.sum(residual * residual) / (IMAGES * GRID * CROP)

def reference(phase_mask, height_offsets, sample_ids, wavelength_ids, scene, w_first, b_first, w_second):
    aperture = pupil_plane(GRID, 0, GRID)
    pupils = pupil_count(GRID)
    measure = jax.value_and_grad(image_loss, argnums=(0, 1, 2, 3))

    def one_image(totals, picks):
        sample_id, wave_id, scene_image = picks
        offsets = lax.dynamic_index_in_dim(height_offsets, sample_id, 0, keepdims=False).astype(jnp.float32)
        ratio_wave = 550.0 / (400.0 + 10.0 * wave_id.astype(jnp.float32))
        loss_value, gradients = measure(phase_mask, w_first, b_first, w_second, offsets, ratio_wave, scene_image, aperture, pupils)
        return ((totals[0] + gradients[0], totals[1] + gradients[1], totals[2] + gradients[2], totals[3] + gradients[3], totals[4] + loss_value), None)
    zero_state = (jnp.zeros((GRID, GRID), jnp.float32), jnp.zeros((CHAN, 9), jnp.float32), jnp.zeros((CHAN,), jnp.float32), jnp.zeros((9, CHAN), jnp.float32), jnp.zeros((), jnp.float32))
    totals, unused = lax.scan(one_image, zero_state, (sample_ids, wavelength_ids, scene))
    return (GRID * GRID * totals[0], totals[1], totals[2], totals[3], totals[4])
```

```python
import functools
import itertools

import jax
import jax.numpy as jnp
import ml_dtypes
import numpy as np
from jax import lax
from jax.experimental import pallas as pl
from jax.experimental.pallas import tpu as pltpu
from jax.sharding import PartitionSpec as P

N = 1024
F32 = jnp.float32
BF16 = jnp.bfloat16
AXES = ("grp", "dp", "sp")
taps = ((-1, -1), (-1, 0), (-1, 1), (0, -1), (0, 0), (0, 1), (1, -1), (1, 0), (1, 1))


def halves(matrix):
    high = matrix.astype(ml_dtypes.bfloat16)
    low = (matrix - high.astype(np.float64)).astype(ml_dtypes.bfloat16)
    return high, low


def trig(rows, cols, length):
    angle = 2.0 * np.pi * (np.outer(rows, cols) % length) / length
    return np.cos(angle), np.sin(angle)


@functools.lru_cache(None)
def constants():
    half = np.arange(512)
    quarter = np.arange(256)
    fours = np.arange(4)
    cos_m, sin_m = trig(half, half, N)
    cos_f, sin_f = trig(quarter, quarter, 256)
    cos_w, sin_w = trig(half, np.arange(N), N)
    sin_w = -sin_w
    sin_w[0] = (-1.0) ** np.arange(N)
    packed = np.concatenate([cos_w, sin_w])
    weight = np.full((N,), 2.0)
    weight[0] = 1.0
    weight[512] = 1.0
    unpack = (packed * weight[:, None]).T / (N * N)
    rows_ext = (np.arange(N + 16) - 8) % N
    cos_t, sin_t = trig(quarter, fours, N)
    cos_c, sin_c = trig(256 + np.arange(128), fours, N)
    return {
        "m": halves(cos_m) + halves(sin_m),
        "f": halves(cos_f) + halves(sin_f),
        "pack": halves(packed),
        "unpack": halves(unpack[rows_ext]),
        "tw_col": np.concatenate([cos_t, sin_t], 1).astype(np.float32),
        "tw_row": np.concatenate([cos_t, sin_t], 1).T.astype(np.float32).copy(),
        "tw_win": np.concatenate([cos_c, sin_c], 1).T.astype(np.float32).copy(),
    }


def pupil_count(size_grid):
    coords = np.arange(size_grid) * 2 - size_grid + 1
    inside = (coords[:, None] ** 2 + coords[None, :] ** 2) * 4 <= size_grid * size_grid
    return float(np.sum(inside))


class Layout:
    def __init__(self, mesh):
        self.dp = mesh.shape["dp"]
        self.y = min(4, self.dp // 2)
        self.zh = self.dp // (2 * self.y)
        self.sp = mesh.shape["sp"]

    def move(self, x, where):
        pairs = []
        sizes = (2, self.zh, self.y, 2, self.sp)
        for spot in itertools.product(*[range(n) for n in sizes]):
            goal = where(*spot)
            if goal is not None:
                pairs.append((self.flat(spot), self.flat(goal)))
        return lax.ppermute(x, AXES, pairs)

    def flat(self, spot):
        g, zh, y, c, s = spot
        g, zh, y, c, s = g % 2, zh % self.zh, y % self.y, c % 2, s % self.sp
        return (g * self.dp + (zh * self.y + y) * 2 + c) * self.sp + s


def split(x):
    high = x.astype(BF16)
    return high, (x - high.astype(F32)).astype(BF16)


def dot(a, b):
    return lax.dot_general(a, b, (((1,), (0,)), ((), ())), preferred_element_type=F32)


def by_right(x, w_high, w_low):
    high, low = split(x)
    return dot(high, w_high) + (dot(high, w_low) + dot(low, w_high))


def by_left(w_high, w_low, x):
    high, low = split(x)
    return dot(w_high, high) + (dot(w_low, high) + dot(w_high, low))


def dft_right(re, im, mats, sign):
    rows = re.shape[0]
    both = jnp.concatenate([re, im], 0)
    by_cos = by_right(both, mats[0], mats[1])
    by_sin = by_right(both, mats[2], mats[3]) * sign
    return by_cos[:rows] - by_sin[rows:], by_cos[rows:] + by_sin[:rows]


def dft_left(re, im, mats, sign):
    cols = re.shape[1]
    both = jnp.concatenate([re, im], 1)
    by_cos = by_left(mats[0], mats[1], both)
    by_sin = by_left(mats[2], mats[3], both) * sign
    return by_cos[:, :cols] - by_sin[:, cols:], by_cos[:, cols:] + by_sin[:, :cols]


def turned(re, im, quarter_turns):
    quarter_turns %= 4
    if quarter_turns == 0:
        return re, im
    if quarter_turns == 1:
        return -im, re
    if quarter_turns == 2:
        return -re, -im
    return im, -re


def times(re, im, cos, sin):
    return re * cos - im * sin, re * sin + im * cos


def cos_sin(x):
    n = jnp.floor(x * (2.0 / np.pi) + 0.5)
    r = x - n * 1.5707963109016418
    r = r - n * 1.5893254712295857e-8
    q = n.astype(jnp.int32) & 3
    z = r * r
    sn = r + r * z * (-1.6666654611e-1 + z * (8.3321608736e-3 + z * -1.9515295891e-4))
    cs = 1.0 - 0.5 * z + z * z * (
        4.166664568298827e-2 + z * (-1.388731625493765e-3 + z * 2.443315711809948e-5)
    )
    odd = (q & 1) == 1
    c0 = jnp.where(odd, sn, cs)
    s0 = jnp.where(odd, cs, sn)
    cos = jnp.where((q == 1) | (q == 2), -c0, c0)
    sin = jnp.where(q >= 2, -s0, s0)
    return cos, sin


def spot_of(idx, d, e=0):
    return lax.rem(idx[0] + d, 4), lax.rem(idx[1] + e, 2)


def from_of(idx, d, e=0):
    return lax.rem(idx[0] + 4 - d, 4), lax.rem(idx[1] + 2 - e, 2)


def aligned(x, by):
    return pl.multiple_of(x * by, by)


def call(kernel, operands, in_smem, outs, scratch=(), spaces=None):
    specs = []
    for at in range(len(operands)):
        space = pltpu.SMEM if at in in_smem else pltpu.VMEM
        if spaces and at in spaces:
            space = spaces[at]
        specs.append(pl.BlockSpec(memory_space=space))
    return pl.pallas_call(
        kernel,
        out_shape=[jax.ShapeDtypeStruct(shape, F32) for shape in outs],
        in_specs=specs,
        out_specs=[pl.BlockSpec(memory_space=pltpu.VMEM) for _ in outs],
        scratch_shapes=list(scratch),
        compiler_params=pltpu.CompilerParams(vmem_limit_bytes=48 * 1024 * 1024),
    )(*operands)


relations = [(d, e) for e in range(2) for d in range(4)]


def phase_kernel(idx, ratio, mask, offsets, own, one, two, three, grabbed, phases, sem):
    copy = pltpu.make_async_copy(offsets.at[idx[2], pl.ds(256, 512), :], grabbed, sem)
    copy.start()
    copy.wait()
    phases[...] = ratio[0] * (mask[pl.ds(256, 512), :] + 0.1 * grabbed[...].astype(F32))
    s = idx[0]
    left = s == 1
    own[...] = phases[pl.ds(aligned(s, 128), 128), :]
    one[...] = phases[pl.ds(aligned(jnp.where(left, 0, 3), 128), 128), :]
    two[...] = phases[pl.ds(aligned(3 - s, 128), 128), :]
    three[...] = phases[pl.ds(aligned(jnp.where(left, 3, 0), 128), 128), :]


def scene_kernel(idx, scene, *outs):
    for (d, e), out in zip(relations, outs):
        s, c = spot_of(idx, d, e)
        out[...] = scene[0, :, pl.ds(aligned(4 * c + s, 128), 128)]


def pupil_kernel(idx, *refs):
    (x0, x1, x2, x3, y0, y1, y2, y3, ch, cl, sh, sl, o0, o1, o2, o3, pupil, grid) = refs
    s = idx[0]
    c = idx[1]
    owner = idx[3] == 1
    a0, a1, a2, a3 = [
        jnp.where(owner, x[...], y[...]) for x, y in ((x0, y0), (x1, y1), (x2, y2), (x3, y3))
    ]
    left = jnp.where(s == 0, a1, jnp.where(s == 1, a0, jnp.where(s == 2, a2, a3)))
    right = jnp.where(s == 0, a3, jnp.where(s == 1, a2, jnp.where(s == 2, a0, a1)))
    phase = jnp.concatenate([left, right], 1)
    rows = lax.broadcasted_iota(jnp.int32, (128, 512), 0) + s * 128
    cols = lax.broadcasted_iota(jnp.int32, (128, 512), 1)
    up = (rows + 256) * 2 - N + 1
    across = (cols + 256) * 2 - N + 1
    inside = (up * up + across * across) * 4 <= N * N
    cos, sin = cos_sin(phase)
    re = jnp.where(inside, cos, 0.0)
    im = jnp.where(inside, sin, 0.0)
    pupil[0] = re
    pupil[1] = im
    flip = jnp.where((cols & c) == 1, -1.0, 1.0)
    out_re, out_im = dft_right(
        re * flip, im * flip, (ch[...], cl[...], sh[...], sl[...]), -1.0
    )
    grid[0] = out_re
    grid[1] = out_im
    for d, out in enumerate((o0, o1, o2, o3)):
        to = spot_of(idx, d)[0]
        out[...] = grid[:, :, pl.ds(aligned(to, 128), 128)]


def optics_kernel(scale, idx, b0, b1, b2, b3, ch, cl, sh, sl, tw, far, *rest):
    outs = rest[:8]
    grid = rest[8]
    mats = (ch[...], cl[...], sh[...], sl[...])
    for d, block in enumerate((b0, b1, b2, b3)):
        grid[:, pl.ds(aligned(from_of(idx, d)[0], 128), 128), :] = block[...]
    low = (grid[0, :256, :], grid[1, :256, :])
    high = (grid[0, 256:, :], grid[1, 256:, :])
    twists = [(tw[:, r : r + 1], tw[:, 4 + r : 5 + r]) for r in range(4)]
    res, ims = [], []
    for r in range(4):
        add = turned(high[0], high[1], -r)
        re, im = low[0] + add[0], low[1] + add[1]
        if r:
            re, im = times(re, im, twists[r][0], -twists[r][1])
        res.append(re)
        ims.append(im)
    far_re, far_im = dft_left(
        jnp.concatenate(res, 1), jnp.concatenate(ims, 1), mats, -1.0
    )
    far[0] = far_re
    far[1] = far_im
    psf = scale * (far_re * far_re + far_im * far_im)
    psf_high, psf_low = split(psf)
    z_re = dot(mats[0], psf_high) + (dot(mats[1], psf_high) + dot(mats[0], psf_low))
    z_im = -(dot(mats[2], psf_high) + (dot(mats[3], psf_high) + dot(mats[2], psf_low)))
    first = [None, None]
    second = [None, None]
    nyquist = None
    for r in range(4):
        re = z_re[:, r * 128 : r * 128 + 128]
        im = z_im[:, r * 128 : r * 128 + 128]
        top = re[0:1, :]
        nyquist = top if r == 0 else (nyquist + top if r % 2 == 0 else nyquist - top)
        if r:
            re, im = times(re, im, twists[r][0], -twists[r][1])
        more = turned(re, im, -r)
        first = [re, im] if r == 0 else [first[0] + re, first[1] + im]
        second = list(more) if r == 0 else [second[0] + more[0], second[1] + more[1]]
    row = lax.broadcasted_iota(jnp.int32, (256, 128), 0)
    grid[0, :256, :] = first[0]
    grid[1, :256, :] = jnp.where(row == 0, nyquist, first[1])
    grid[0, 256:, :] = second[0]
    grid[1, 256:, :] = second[1]
    for (d, e), out in zip(relations, outs):
        s, c = spot_of(idx, d, e)
        out[...] = grid[:, pl.ds(aligned(2 * s + c, 64), 64), :]


def scene_columns_kernel(idx, b0, b1, b2, b3, wh, wl, *rest):
    outs = rest[:8]
    image, grid = rest[8:]
    for d, block in enumerate((b0, b1, b2, b3)):
        image[pl.ds(aligned(from_of(idx, d)[0], 256), 256), :] = block[...]
    spectrum = by_left(wh[...], wl[...], image[...])
    grid[0] = spectrum[:512]
    grid[1] = spectrum[512:]
    for (d, e), out in zip(relations, outs):
        s, c = spot_of(idx, d, e)
        out[...] = grid[:, pl.ds(aligned(2 * s + c, 64), 64), :]


def unpack_rows(idx, re, im, tail):
    rows = lax.broadcasted_iota(jnp.int32, re.shape, 0)
    first = (idx[0] + idx[1]) == 0
    nyquist = jnp.where(first, im[0:1, :], 0.0)
    tail_rows = lax.broadcasted_iota(jnp.int32, (tail, re.shape[1]), 0)
    extra = jnp.where(tail_rows == 0, nyquist, 0.0)
    im = jnp.where((rows == 0) & first, 0.0, im)
    return jnp.concatenate([re, extra], 0), jnp.concatenate([im, jnp.zeros_like(extra)], 0)


def repack_rows(idx, re, im):
    first = (idx[0] + idx[1]) == 0
    rows = lax.broadcasted_iota(jnp.int32, (64, re.shape[1]), 0)
    return re[:64], jnp.where((rows == 0) & first, re[64:65, :], im[:64])


def row_transform(idx, blocks, mats, tw, grid):
    for (d, e), block in zip(relations, blocks):
        s, c = from_of(idx, d, e)
        grid[:, :, pl.ds(aligned(4 * c + s, 128), 128)] = block[...]
    re, im = unpack_rows(idx, grid[0], grid[1], 8)
    quarters = [(re[:, q * 256 : q * 256 + 256], im[:, q * 256 : q * 256 + 256]) for q in range(4)]
    sum02 = [quarters[0][p] + quarters[2][p] for p in range(2)]
    dif02 = [quarters[0][p] - quarters[2][p] for p in range(2)]
    sum13 = [quarters[1][p] + quarters[3][p] for p in range(2)]
    dif13 = [quarters[1][p] - quarters[3][p] for p in range(2)]
    step = turned(dif13[0], dif13[1], -1)
    parts = [
        (sum02[0] + sum13[0], sum02[1] + sum13[1]),
        (dif02[0] + step[0], dif02[1] + step[1]),
        (sum02[0] - sum13[0], sum02[1] - sum13[1]),
        (dif02[0] - step[0], dif02[1] - step[1]),
    ]
    for r in range(1, 4):
        parts[r] = times(parts[r][0], parts[r][1], tw[r : r + 1, :], -tw[4 + r : 5 + r, :])
    return dft_right(
        jnp.concatenate([p[0] for p in parts], 0),
        jnp.concatenate([p[1] for p in parts], 0),
        mats,
        -1.0,
    )


def scene_rows_kernel(idx, *refs):
    blocks = refs[:8]
    ch, cl, sh, sl, tw, out, grid = refs[8:]
    re, im = row_transform(idx, blocks, (ch[...], cl[...], sh[...], sl[...]), tw, grid)
    out[0] = re
    out[1] = im


def blur_kernel(idx, *refs):
    blocks = refs[:8]
    ch, cl, sh, sl, tw, tw_win, spectrum, out, grid = refs[8:]
    re, im = row_transform(idx, blocks, (ch[...], cl[...], sh[...], sl[...]), tw, grid)
    re, im = times(re, im, spectrum[0], spectrum[1])
    mats = (ch[:, :128], cl[:, :128], sh[:, :128], sl[:, :128])
    re, im = dft_right(re, im, mats, 1.0)
    sum_re, sum_im = re[:72], im[:72]
    for r in range(1, 4):
        add = times(
            re[r * 72 : r * 72 + 72],
            im[r * 72 : r * 72 + 72],
            tw_win[r : r + 1, :],
            tw_win[4 + r : 5 + r, :],
        )
        sum_re = sum_re + add[0]
        sum_im = sum_im + add[1]
    re, im = repack_rows(idx, sum_re, sum_im)
    out[0] = re
    out[1] = im


def moved_lanes(x, e, lanes):
    if e == 0:
        return x
    rolled = pltpu.roll(x, (-e) % 128, 1)
    return jnp.where(lanes == (127 if e > 0 else 0), 0.0, rolled)


def moved_rows(x, a):
    if a == 0:
        return x
    return pltpu.roll(x, (-a) % x.shape[0], 0)


ROWS = 144


def net_kernel(pixel_count, idx, w1, b1, w2, *refs):
    blocks = refs[:8]
    vh, vl, target, g_out, acc, loss_out = refs[8:14]
    grid, win_taps, g_taps, hidden, sums = refs[14:]
    for (d, e), block in zip(relations, blocks):
        s, c = from_of(idx, d, e)
        at = 2 * s + c
        grid[pl.ds(aligned(at, 64), 64), :] = block[0]
        grid[pl.ds(aligned(at + 8, 64), 64), :] = block[1]
    rows = lax.broadcasted_iota(jnp.int32, (ROWS, 128), 0)
    lanes = lax.broadcasted_iota(jnp.int32, (ROWS, 128), 1)
    row_global = rows + (2 * idx[0] + idx[1]) * 128 - 8
    inside = (row_global >= 0) & (row_global < N)
    window = jnp.where(inside, by_right_const(vh[...], vl[...], grid[...]), 0.0)
    for e in (-1, 0, 1):
        side = moved_lanes(window, e, lanes)
        for a in (-1, 0, 1):
            win_taps[3 * (a + 1) + e + 1] = moved_rows(side, a)
    step = 16
    for k in range(ROWS // step):
        part = pl.ds(k * step, step)

        def forward(c, total, part=part):
            pre = jnp.full((step, 128), b1[c], F32)
            for t in range(9):
                pre = pre + w1[c, t] * win_taps[t, part, :]
            hid = jnp.maximum(pre, 0.0)
            hidden[c, part, :] = hid
            return tuple(total[t] + w2[t, c] * hid for t in range(9))

        total = lax.fori_loop(
            0, 32, forward, tuple(jnp.zeros((step, 128), F32) for _ in range(9))
        )
        for t in range(9):
            sums[t, part, :] = total[t]
    restored = window
    for e in (-1, 0, 1):
        side = None
        for a in (-1, 0, 1):
            part = moved_rows(jnp.where(inside, sums[3 * (a + 1) + e + 1], 0.0), a)
            side = part if side is None else side + part
        restored = restored + moved_lanes(side, e, lanes)
    residual = jnp.where(inside, restored - target[...], 0.0)
    own = (rows >= 8) & (rows < 136)
    own_residual = jnp.where(own, residual, 0.0)
    loss_out[...] = jnp.sum((own_residual * own_residual).reshape(ROWS // 8, 8, 128), 0)
    g_restored = (2.0 / pixel_count) * residual
    for e in (-1, 0, 1):
        side = moved_lanes(g_restored, -e, lanes)
        for a in (-1, 0, 1):
            g_taps[3 * (a + 1) + e + 1] = jnp.where(inside, moved_rows(side, -a), 0.0)
    acc[...] = jnp.zeros_like(acc)

    def folded(x):
        return x if x.shape[0] == 8 else x[:8] + x[8:]

    for start, step, mine in [(0, 8, False)] + [(8 + 16 * k, 16, True) for k in range(8)] + [
        (136, 8, False)
    ]:
        part = pl.ds(start, step)

        def backward(c, total, part=part, step=step, mine=mine):
            hid = hidden[c, part, :]
            gh = w2[0, c] * g_taps[0, part, :]
            for t in range(1, 9):
                gh = gh + w2[t, c] * g_taps[t, part, :]
            gp = jnp.where(hid > 0.0, gh, 0.0)
            if mine:
                for t in range(9):
                    acc[c, t] += folded(gp * win_taps[t, part, :])
                    acc[c, 9 + t] += folded(hid * g_taps[t, part, :])
                acc[c, 18] += folded(gp)
            return tuple(total[t] + w1[c, t] * gp for t in range(9))

        total = lax.fori_loop(
            0, 32, backward, tuple(jnp.zeros((step, 128), F32) for _ in range(9))
        )
        for t in range(9):
            sums[t, part, :] = total[t]
    g_window = g_restored
    for e in (-1, 0, 1):
        side = None
        for a in (-1, 0, 1):
            part = moved_rows(sums[3 * (a + 1) + e + 1], -a)
            side = part if side is None else side + part
        g_window = g_window + moved_lanes(side, -e, lanes)
    g_out[...] = g_window[8:136]


def by_right_const(w_high, w_low, x):
    return by_left(w_high, w_low, x)


def otf_grad_kernel(idx, *refs):
    blocks = refs[:8]
    wh, wl, ch, cl, sh, sl, tw, tw_win, spectrum = refs[8:17]
    outs = refs[17:25]
    window, grid = refs[25:]
    for (d, e), block in zip(relations, blocks):
        s, c = from_of(idx, d, e)
        window[pl.ds(aligned(2 * s + c, 128), 128), :] = block[...]
    packed = by_left(wh[...], wl[...], window[...])
    re, im = unpack_rows(idx, packed[:64], packed[64:], 8)
    res, ims = [re], [im]
    for r in range(1, 4):
        a, b = times(re, im, tw_win[r : r + 1, :], -tw_win[4 + r : 5 + r, :])
        res.append(a)
        ims.append(b)
    mats = (ch[...], cl[...], sh[...], sl[...])
    top = tuple(m[:128, :] for m in mats)
    re, im = dft_right(jnp.concatenate(res, 0), jnp.concatenate(ims, 0), top, -1.0)
    re, im = times(re, im, spectrum[0], -spectrum[1])
    re, im = dft_right(re, im, mats, 1.0)
    parts = []
    for r in range(4):
        a, b = re[r * 72 : r * 72 + 72], im[r * 72 : r * 72 + 72]
        if r:
            a, b = times(a, b, tw[r : r + 1, :], tw[4 + r : 5 + r, :])
        parts.append((a, b))
    for q in range(4):
        a, b = parts[0]
        for r in range(1, 4):
            more = turned(parts[r][0], parts[r][1], q * r)
            a = a + more[0]
            b = b + more[1]
        a, b = repack_rows(idx, a, b)
        grid[0, :, q * 256 : q * 256 + 256] = a
        grid[1, :, q * 256 : q * 256 + 256] = b
    for (d, e), out in zip(relations, outs):
        s, c = spot_of(idx, d, e)
        out[...] = grid[:, :, pl.ds(aligned(4 * c + s, 128), 128)]


def psf_grad_kernel(idx, *refs):
    blocks = refs[:8]
    far, ch, cl, sh, sl, tw, o0, o1, o2, o3, grid = refs[8:]
    mats = (ch[...], cl[...], sh[...], sl[...])
    for (d, e), block in zip(relations, blocks):
        s, c = from_of(idx, d, e)
        grid[:, pl.ds(aligned(2 * s + c, 64), 64), :] = block[...]
    row = lax.broadcasted_iota(jnp.int32, (256, 128), 0)
    zero_row = row == 0
    low_re, low_im = grid[0, :256, :], grid[1, :256, :]
    nyquist = jnp.where(zero_row, 0.5 * low_im, 0.0)
    low_re = jnp.where(zero_row, 0.5 * low_re, low_re)
    low_im = jnp.where(zero_row, 0.0, low_im)
    high = (grid[0, 256:, :], grid[1, 256:, :])
    twists = [(tw[:, r : r + 1], tw[:, 4 + r : 5 + r]) for r in range(4)]
    res, ims = [], []
    for r in range(4):
        add = turned(high[0], high[1], r)
        re, im = low_re + add[0], low_im + add[1]
        if r:
            re, im = times(re, im, twists[r][0], twists[r][1])
        re = re + nyquist if r % 2 == 0 else re - nyquist
        res.append(re)
        ims.append(im)
    g_psf = 2.0 * (
        by_left(mats[0], mats[1], jnp.concatenate(res, 1))
        - by_left(mats[2], mats[3], jnp.concatenate(ims, 1))
    )
    re, im = dft_left(g_psf * far[0], g_psf * far[1], mats, 1.0)
    first, second = None, None
    for r in range(4):
        a, b = re[:, r * 128 : r * 128 + 128], im[:, r * 128 : r * 128 + 128]
        if r:
            a, b = times(a, b, twists[r][0], twists[r][1])
        more = turned(a, b, r)
        first = [a, b] if r == 0 else [first[0] + a, first[1] + b]
        second = list(more) if r == 0 else [second[0] + more[0], second[1] + more[1]]
    for p in range(2):
        grid[p, :256, :] = first[p]
        grid[p, 256:, :] = second[p]
    for d, out in enumerate((o0, o1, o2, o3)):
        out[...] = grid[:, pl.ds(aligned(spot_of(idx, d)[0], 128), 128), :]


def mask_grad_kernel(scale, idx, ratio, *refs):
    blocks = refs[:4]
    ch, cl, sh, sl, pupil, keep, send, grid, whole = refs[4:]
    for d, block in enumerate(blocks):
        grid[:, :, pl.ds(aligned(from_of(idx, d)[0], 128), 128)] = block[...]
    re, im = dft_right(grid[0], grid[1], (ch[...], cl[...], sh[...], sl[...]), 1.0)
    cols = lax.broadcasted_iota(jnp.int32, (128, 512), 1)
    factor = ratio[0] * scale
    factor = jnp.where((cols & idx[1]) == 1, -factor, factor)
    whole[...] = factor * (im * pupil[0] - re * pupil[1])
    keep[...] = whole[:, pl.ds(aligned(idx[1], 256), 256)]
    send[...] = whole[:, pl.ds(aligned(1 - idx[1], 256), 256)]


def on_device(lay, phase_mask, height_offsets, sample_ids, wave_ids, scene, w1, b1, w2):
    con = constants()
    s = lax.axis_index("sp")
    dp = lax.axis_index("dp")
    c = dp % 2
    y = (dp // 2) % lay.y
    g = lax.axis_index("grp")
    owner = c == g
    pixel_count = float(lay.dp * N * 128)
    scale_psf = 1.0 / (N * N * pupil_count(N))
    idx = jnp.stack([s, c, sample_ids[0], owner.astype(jnp.int32)]).astype(jnp.int32)
    ids = jnp.stack([sample_ids[0], wave_ids[0]])
    ids_got = lay.move(ids, lambda g, zh, y, c, s: (g, zh, y, 1 - c, s) if c == g else None)
    wave_own = wave_ids[0]
    wave = jnp.where(owner, wave_own, ids_got[1])

    def ratio_of(w):
        return (550.0 / (400.0 + 10.0 * w.astype(F32))).reshape(1)

    mine, one, two, three = call(
        phase_kernel,
        (idx, ratio_of(wave_own), phase_mask, height_offsets),
        (0, 1),
        [(128, 256)] * 4,
        [pltpu.VMEM((512, 256), jnp.int32), pltpu.VMEM((512, 256), F32), pltpu.SemaphoreType.DMA],
        {3: pl.ANY},
    )

    def route(table, cross):
        return lambda g, zh, y, c, s: (
            (g, zh, y, c + cross, table[s]) if c == g and s in table else None
        )

    tables = ({1: 1, 2: 2}, {1: 0, 2: 3}, {1: 2, 2: 1}, {1: 3, 2: 0})
    pieces = [mine] + [
        lay.move(x, route(t, 0)) for x, t in zip((one, two, three), tables[1:])
    ]
    pieces += [lay.move(x, route(t, 1)) for x, t in zip((mine, one, two, three), tables)]

    scene_blocks = call(scene_kernel, (idx, scene), (0,), [(256, 128)] * 8)
    got = {}
    for (d, e), block in zip(relations, scene_blocks):
        if (d, e) == (0, 0):
            got[d, e] = block
        else:
            got[d, e] = lay.move(
                block,
                lambda g, zh, y, c, s, d=d, e=e: (g, zh, y, c + e, s + d) if c == g else None,
            )
    columns = [jnp.where(owner, got[d, 0], got[d, 1]) for d in range(4)]

    strip = scene[0, :, 256:384]
    before = lay.move(
        strip[248:], lambda g, zh, y, c, s: (g, zh, y, c, s + 1) if c == g and s < 3 else None
    )
    after = lay.move(
        strip[:8], lambda g, zh, y, c, s: (g, zh, y, c, s - 1) if c == g and s > 0 else None
    )
    strip = jnp.concatenate([before, strip, after], 0)
    strip_got = lay.move(
        lax.dynamic_slice_in_dim(strip, 128 * (1 - c), ROWS, 0),
        lambda g, zh, y, c, s: (g, zh, y, 1 - c, s) if c == g else None,
    )
    target = jnp.where(owner, lax.dynamic_slice_in_dim(strip, 128 * c, ROWS, 0), strip_got)

    def along_sp(blocks):
        return [blocks[0]] + [
            lay.move(blocks[d], lambda g, zh, y, c, s, d=d: (g, zh, y, c, s + d))
            for d in (1, 2, 3)
        ]

    def to_eight(blocks):
        out = []
        for (d, e), block in zip(relations, blocks):
            out.append(
                block
                if (d, e) == (0, 0)
                else lay.move(
                    block, lambda g, zh, y, c, s, d=d, e=e: (g, zh, y, c + e, s + d)
                )
            )
        return out

    m_mats = con["m"]
    f_mats = con["f"]
    slot = 2 * s + c
    unpack = [lax.dynamic_slice_in_dim(jnp.asarray(v), 128 * slot, ROWS, 0) for v in con["unpack"]]
    pack_rows = [
        jnp.concatenate(
            [
                lax.dynamic_slice_in_dim(jnp.asarray(v), 64 * slot, 64, 0),
                lax.dynamic_slice_in_dim(jnp.asarray(v), 512 + 64 * slot, 64, 0),
            ],
            0,
        )
        for v in con["pack"]
    ]

    *field, pupil = call(
        pupil_kernel,
        (idx, *pieces, *m_mats),
        (0,),
        [(2, 128, 128)] * 4 + [(2, 128, 512)],
        [pltpu.VMEM((2, 128, 512), F32)],
    )
    field = along_sp(field)
    scene_part = to_eight(
        call(
            scene_columns_kernel,
            (idx, *columns, *con["pack"]),
            (0,),
            [(2, 64, 128)] * 8,
            [pltpu.VMEM((N, 128), F32), pltpu.VMEM((2, 512, 128), F32)],
        )
    )
    far, *otf_part = call(
        functools.partial(optics_kernel, scale_psf),
        (idx, *field, *f_mats, con["tw_col"]),
        (0,),
        [(2, 256, 512)] + [(2, 64, 128)] * 8,
        [pltpu.VMEM((2, 512, 128), F32)],
    )
    otf_part = to_eight(otf_part)
    row_scratch = [pltpu.VMEM((2, 64, N), F32)]
    (spectrum,) = call(
        scene_rows_kernel,
        (idx, *scene_part, *f_mats, con["tw_row"]),
        (0,),
        [(2, 288, 256)],
        row_scratch,
    )
    (half_window,) = call(
        blur_kernel,
        (idx, *otf_part, *f_mats, con["tw_row"], con["tw_win"], spectrum),
        (0,),
        [(2, 64, 128)],
        row_scratch,
    )
    window_parts = to_eight([half_window] * 8)
    g_window, acc, loss_part = call(
        functools.partial(net_kernel, pixel_count),
        (idx, w1, b1, w2, *window_parts, *unpack, target),
        (0, 1, 2, 3),
        [(128, 128), (32, 19, 8, 128), (8, 128)],
        [
            pltpu.VMEM((N, 128), F32),
            pltpu.VMEM((9, ROWS, 128), F32),
            pltpu.VMEM((9, ROWS, 128), F32),
            pltpu.VMEM((32, ROWS, 128), F32),
            pltpu.VMEM((9, ROWS, 128), F32),
        ],
    )
    g_parts = to_eight([g_window] * 8)
    otf_grad = to_eight(
        call(
            otf_grad_kernel,
            (idx, *g_parts, *pack_rows, *f_mats, con["tw_row"], con["tw_win"], spectrum),
            (0,),
            [(2, 64, 128)] * 8,
            [pltpu.VMEM((N, 128), F32), pltpu.VMEM((2, 64, N), F32)],
        )
    )
    field_grad = along_sp(
        call(
            psf_grad_kernel,
            (idx, *otf_grad, far, *f_mats, con["tw_col"]),
            (0,),
            [(2, 128, 128)] * 4,
            [pltpu.VMEM((2, 512, 128), F32)],
        )
    )
    keep, send = call(
        functools.partial(mask_grad_kernel, 2.0 * scale_psf),
        (idx, ratio_of(wave), *field_grad, *m_mats, pupil),
        (0, 1),
        [(128, 256)] * 2,
        [pltpu.VMEM((2, 128, 512), F32), pltpu.VMEM((128, 512), F32)],
    )

    small = jnp.concatenate(
        [jnp.sum(acc, (2, 3)).reshape(-1), jnp.sum(loss_part).reshape(1), jnp.zeros((415,), F32)]
    ).reshape(8, 128)

    def summed(x, moves):
        total = x
        for where in moves:
            total = total + lay.move(x, where)
        return total

    y_moves = [
        lambda g, zh, y, c, s, d=d: (g, zh, y + d, c, s) for d in range(1, lay.y)
    ]

    def z_move(d):
        def where(g, zh, y, c, s):
            z = (2 * zh + g + d) % (2 * lay.zh)
            return (z % 2, z // 2, y, c, s)

        return where

    z_moves = [z_move(d) for d in range(1, 2 * lay.zh)]
    small = summed(small, [lambda g, zh, y, c, s: (g, zh, y, c + 1, s)])
    small = summed(small, [lambda g, zh, y, c, s, d=d: (g, zh, y, c, s + d) for d in (1, 2, 3)])
    small = summed(small, y_moves)
    small = summed(small, z_moves).reshape(-1)

    grad = keep + lay.move(send, lambda g, zh, y, c, s: (g, zh, y, c + 1, s))
    piece = 128 // lay.y
    total = lax.dynamic_slice_in_dim(grad, piece * y, piece, 0)
    for d in range(1, lay.y):
        block = lax.dynamic_slice_in_dim(grad, piece * ((y + d) % lay.y), piece, 0)
        total = total + lay.move(block, y_moves[d - 1])
    total = summed(total, z_moves)
    home = [
        lay.move(
            total, lambda g, zh, y, c, s, d=d: (g, zh, y, c, 1 + c) if (s + d - 1 - c) % 4 == 0 else None
        )
        for d in (1, 2, 3)
    ]
    home = [total] + home
    order = jnp.stack(home)
    order = jnp.stack([lax.dynamic_index_in_dim(order, (1 + c - q) % 4, 0, False) for q in range(4)])

    def at_home(c, s):
        return s == 1 + c

    sets = [order] + [
        lay.move(
            order,
            lambda g, zh, y, c, s, d=d: (g, zh, y + d, c, s) if at_home(c, s) else None,
        )
        for d in range(1, lay.y)
    ]
    sets = jnp.stack(sets)
    sets = jnp.stack(
        [lax.dynamic_index_in_dim(sets, (y - q) % lay.y, 0, False) for q in range(lay.y)], 1
    )
    middle = sets.reshape(512, 256)
    crossed = lay.move(
        middle,
        lambda g, zh, y, c, s: (g, zh, y, 1 - c, s) if at_home(c, s) else None,
    )
    middle = jnp.where(at_home(c, s), middle, crossed)
    mask_grad = jnp.pad(middle, ((256, 256), (0, 0)))
    table = small[:608].reshape(32, 19)
    return (
        mask_grad,
        table[:, :9],
        table[:, 18],
        table[:, 9:18].T,
        small[608] / pixel_count,
    )


def solution(mesh):
    placed = (
        P(None, "sp"),
        P(None, None, "sp"),
        P("dp"),
        P("dp"),
        P("dp", "sp", None),
        P(),
        P(),
        P(),
    )
    return jax.shard_map(
        functools.partial(on_device, Layout(mesh)),
        mesh=mesh,
        in_specs=placed,
        out_specs=(P(None, "sp"), P(), P(), P(), P()),
        check_vma=False,
    )
```

```python
import functools
import itertools

import jax
import jax.numpy as jnp
import ml_dtypes
import numpy as np
from jax import lax
from jax.experimental import pallas as pl
from jax.experimental.pallas import tpu as pltpu
from jax.sharding import PartitionSpec as P

N = 1024
F32 = jnp.float32
BF16 = jnp.bfloat16
AXES = ("grp", "zh", "y", "core", "sp")
taps = ((-1, -1), (-1, 0), (-1, 1), (0, -1), (0, 0), (0, 1), (1, -1), (1, 0), (1, 1))


def halves(matrix):
    high = matrix.astype(ml_dtypes.bfloat16)
    low = (matrix - high.astype(np.float64)).astype(ml_dtypes.bfloat16)
    return high, low


def trig(rows, cols, length):
    angle = 2.0 * np.pi * (np.outer(rows, cols) % length) / length
    return np.cos(angle), np.sin(angle)


@functools.lru_cache(None)
def constants():
    half = np.arange(512)
    quarter = np.arange(256)
    fours = np.arange(4)
    cos_m, sin_m = trig(half, half, N)
    cos_f, sin_f = trig(quarter, quarter, 256)
    cos_w, sin_w = trig(half, np.arange(N), N)
    sin_w = -sin_w
    sin_w[0] = (-1.0) ** np.arange(N)
    packed = np.concatenate([cos_w, sin_w])
    weight = np.full((N,), 2.0)
    weight[0] = 1.0
    weight[512] = 1.0
    unpack = (packed * weight[:, None]).T / (N * N)
    rows_ext = (np.arange(N + 16) - 8) % N
    cos_t, sin_t = trig(quarter, fours, N)
    cos_c, sin_c = trig(256 + np.arange(128), fours, N)
    return {
        "m": np.stack(halves(cos_m) + halves(sin_m)),
        "f": np.stack(halves(cos_f) + halves(sin_f)),
        "pack": np.stack(halves(packed)),
        "unpack": np.stack(halves(unpack[rows_ext])),
        "tw_col": np.concatenate([cos_t, sin_t], 1).astype(np.float32),
        "tw_row": np.concatenate(
            [
                np.concatenate([cos_t, sin_t], 1).T,
                np.pad(np.concatenate([cos_c, sin_c], 1).T, ((0, 0), (0, 128))),
            ]
        ).astype(np.float32),
    }


def pupil_count(size_grid):
    coords = np.arange(size_grid) * 2 - size_grid + 1
    inside = (coords[:, None] ** 2 + coords[None, :] ** 2) * 4 <= size_grid * size_grid
    return float(np.sum(inside))


class Layout:
    def __init__(self, mesh):
        self.dp = mesh.shape["dp"]
        self.y = min(4, self.dp // 2)
        self.zh = self.dp // (2 * self.y)
        self.sp = mesh.shape["sp"]
        self.sizes = (2, self.zh, self.y, 2, self.sp)
        self.mesh = jax.sharding.Mesh(mesh.devices.reshape(self.sizes), AXES)

    def move(self, x, where):
        pairs = []
        for spot in itertools.product(*[range(n) for n in self.sizes]):
            goal = where(*spot)
            if goal is not None:
                pairs.append((self.flat(spot), self.flat(goal)))
        return lax.ppermute(x, AXES, pairs)

    def flat(self, spot):
        at = 0
        for place, size in zip(spot, self.sizes):
            at = at * size + place % size
        return at


def split(x):
    high = x.astype(BF16)
    return high, (x - high.astype(F32)).astype(BF16)


def dot(a, b):
    return lax.dot_general(a, b, (((1,), (0,)), ((), ())), preferred_element_type=F32)


def by_right(x, w_high, w_low):
    high, low = split(x)
    return dot(high, w_high) + (dot(high, w_low) + dot(low, w_high))


def by_left(w_high, w_low, x):
    high, low = split(x)
    return dot(w_high, high) + (dot(w_low, high) + dot(w_high, low))


def dft_right(re, im, mats, sign):
    rows = re.shape[0]
    both = jnp.concatenate([re, im], 0)
    by_cos = by_right(both, mats[0], mats[1])
    by_sin = by_right(both, mats[2], mats[3]) * sign
    return by_cos[:rows] - by_sin[rows:], by_cos[rows:] + by_sin[:rows]


def dft_left(re, im, mats, sign):
    cols = re.shape[1]
    both = jnp.concatenate([re, im], 1)
    by_cos = by_left(mats[0], mats[1], both)
    by_sin = by_left(mats[2], mats[3], both) * sign
    return by_cos[:, :cols] - by_sin[:, cols:], by_cos[:, cols:] + by_sin[:, :cols]


def turned(re, im, quarter_turns):
    quarter_turns %= 4
    if quarter_turns == 0:
        return re, im
    if quarter_turns == 1:
        return -im, re
    if quarter_turns == 2:
        return -re, -im
    return im, -re


def times(re, im, cos, sin):
    return re * cos - im * sin, re * sin + im * cos


def cos_sin(x):
    n = jnp.floor(x * (2.0 / np.pi) + 0.5)
    r = x - n * 1.5707963109016418
    r = r - n * 1.5893254712295857e-8
    q = n.astype(jnp.int32) & 3
    z = r * r
    sn = r + r * z * (-1.6666654611e-1 + z * (8.3321608736e-3 + z * -1.9515295891e-4))
    cs = 1.0 - 0.5 * z + z * z * (
        4.166664568298827e-2 + z * (-1.388731625493765e-3 + z * 2.443315711809948e-5)
    )
    odd = (q & 1) == 1
    c0 = jnp.where(odd, sn, cs)
    s0 = jnp.where(odd, cs, sn)
    cos = jnp.where((q == 1) | (q == 2), -c0, c0)
    sin = jnp.where(q >= 2, -s0, s0)
    return cos, sin


def spot_of(idx, d, e=0):
    return lax.rem(idx[0] + d, 4), lax.rem(idx[1] + e, 2)


def from_of(idx, d, e=0):
    return lax.rem(idx[0] + 4 - d, 4), lax.rem(idx[1] + 2 - e, 2)


def aligned(x, by):
    return pl.multiple_of(x * by, by)


def call(kernel, operands, in_smem, outs, scratch=(), spaces=None):
    specs = []
    for at in range(len(operands)):
        space = pltpu.SMEM if at in in_smem else pltpu.VMEM
        if spaces and at in spaces:
            space = spaces[at]
        specs.append(pl.BlockSpec(memory_space=space))
    return pl.pallas_call(
        kernel,
        out_shape=[jax.ShapeDtypeStruct(shape, F32) for shape in outs],
        in_specs=specs,
        out_specs=[pl.BlockSpec(memory_space=pltpu.VMEM) for _ in outs],
        scratch_shapes=list(scratch),
        compiler_params=pltpu.CompilerParams(vmem_limit_bytes=48 * 1024 * 1024),
    )(*operands)


relations = [(d, e) for e in range(2) for d in range(4)]


def mats_of(ref):
    return ref[0], ref[1], ref[2], ref[3]


def phase_kernel(idx, ratio, mask, offsets, own, one, two, three, grabbed, phases, sem):
    copy = pltpu.make_async_copy(offsets.at[idx[2], pl.ds(256, 512), :], grabbed, sem)
    copy.start()
    copy.wait()
    phases[...] = ratio[0] * (mask[pl.ds(256, 512), :] + 0.1 * grabbed[...].astype(F32))
    s = idx[0]
    left = s == 1
    own[...] = phases[pl.ds(aligned(s, 128), 128), :]
    one[...] = phases[pl.ds(aligned(jnp.where(left, 0, 3), 128), 128), :]
    two[...] = phases[pl.ds(aligned(3 - s, 128), 128), :]
    three[...] = phases[pl.ds(aligned(jnp.where(left, 3, 0), 128), 128), :]


def scene_kernel(idx, scene, other, o0, o1, o2, o3, strip, edge):
    owner = idx[3] == 1
    c = idx[1]
    for d, out in enumerate((o0, o1, o2, o3)):
        s = spot_of(idx, d)[0]
        out[...] = jnp.where(
            owner,
            scene[0, :, pl.ds(aligned(4 * c + s, 128), 128)],
            other[:, pl.ds(aligned(s, 128), 128)],
        )
    strip[...] = jnp.where(owner, scene[0, :, 256:384], other[:, 512:640])
    edge[...] = jnp.where(c == 0, strip[248:256, :], strip[0:8, :])


def pupil_kernel(idx, a0, a1, a2, a3, m, o0, o1, o2, o3, pupil, grid):
    s = idx[0]
    c = idx[1]
    a0, a1, a2, a3 = a0[...], a1[...], a2[...], a3[...]
    left = jnp.where(s == 0, a1, jnp.where(s == 1, a0, jnp.where(s == 2, a2, a3)))
    right = jnp.where(s == 0, a3, jnp.where(s == 1, a2, jnp.where(s == 2, a0, a1)))
    phase = jnp.concatenate([left, right], 1)
    rows = lax.broadcasted_iota(jnp.int32, (128, 512), 0) + s * 128
    cols = lax.broadcasted_iota(jnp.int32, (128, 512), 1)
    up = (rows + 256) * 2 - N + 1
    across = (cols + 256) * 2 - N + 1
    inside = (up * up + across * across) * 4 <= N * N
    cos, sin = cos_sin(phase)
    re = jnp.where(inside, cos, 0.0)
    im = jnp.where(inside, sin, 0.0)
    pupil[0] = re
    pupil[1] = im
    flip = jnp.where((cols & c) == 1, -1.0, 1.0)
    out_re, out_im = dft_right(re * flip, im * flip, mats_of(m), -1.0)
    grid[0] = out_re
    grid[1] = out_im
    for d, out in enumerate((o0, o1, o2, o3)):
        to = spot_of(idx, d)[0]
        out[...] = grid[:, :, pl.ds(aligned(to, 128), 128)]


def eight_rows(out, grid):
    for c in range(2):
        for s in range(4):
            out[4 * c + s] = grid[:, 128 * s + 64 * c : 128 * s + 64 * c + 64, :]


def eight_columns(out, grid):
    for at in range(8):
        out[at] = grid[:, :, 128 * at : 128 * at + 128]


def optics_kernel(scale, idx, b0, b1, b2, b3, f, tw, far, out, grid):
    mats = mats_of(f)
    for d, block in enumerate((b0, b1, b2, b3)):
        grid[:, pl.ds(aligned(from_of(idx, d)[0], 128), 128), :] = block[...]
    low = (grid[0, :256, :], grid[1, :256, :])
    high = (grid[0, 256:, :], grid[1, 256:, :])
    twists = [(tw[:, r : r + 1], tw[:, 4 + r : 5 + r]) for r in range(4)]
    res, ims = [], []
    for r in range(4):
        add = turned(high[0], high[1], -r)
        re, im = low[0] + add[0], low[1] + add[1]
        if r:
            re, im = times(re, im, twists[r][0], -twists[r][1])
        res.append(re)
        ims.append(im)
    far_re, far_im = dft_left(
        jnp.concatenate(res, 1), jnp.concatenate(ims, 1), mats, -1.0
    )
    far[0] = far_re
    far[1] = far_im
    psf = scale * (far_re * far_re + far_im * far_im)
    psf_high, psf_low = split(psf)
    z_re = dot(mats[0], psf_high) + (dot(mats[1], psf_high) + dot(mats[0], psf_low))
    z_im = -(dot(mats[2], psf_high) + (dot(mats[3], psf_high) + dot(mats[2], psf_low)))
    first = [None, None]
    second = [None, None]
    nyquist = None
    for r in range(4):
        re = z_re[:, r * 128 : r * 128 + 128]
        im = z_im[:, r * 128 : r * 128 + 128]
        top = re[0:1, :]
        nyquist = top if r == 0 else (nyquist + top if r % 2 == 0 else nyquist - top)
        if r:
            re, im = times(re, im, twists[r][0], -twists[r][1])
        more = turned(re, im, -r)
        first = [re, im] if r == 0 else [first[0] + re, first[1] + im]
        second = list(more) if r == 0 else [second[0] + more[0], second[1] + more[1]]
    row = lax.broadcasted_iota(jnp.int32, (256, 128), 0)
    grid[0, :256, :] = first[0]
    grid[1, :256, :] = jnp.where(row == 0, nyquist, first[1])
    grid[0, 256:, :] = second[0]
    grid[1, 256:, :] = second[1]
    eight_rows(out, grid)


def scene_columns_kernel(idx, b0, b1, b2, b3, w, out, image, grid):
    for d, block in enumerate((b0, b1, b2, b3)):
        image[pl.ds(aligned(from_of(idx, d)[0], 256), 256), :] = block[...]
    spectrum = by_left(w[0], w[1], image[...])
    grid[0] = spectrum[:512]
    grid[1] = spectrum[512:]
    eight_rows(out, grid)


def unpack_rows(idx, re, im, tail):
    rows = lax.broadcasted_iota(jnp.int32, re.shape, 0)
    first = (idx[0] + idx[1]) == 0
    nyquist = jnp.where(first, im[0:1, :], 0.0)
    tail_rows = lax.broadcasted_iota(jnp.int32, (tail, re.shape[1]), 0)
    extra = jnp.where(tail_rows == 0, nyquist, 0.0)
    im = jnp.where((rows == 0) & first, 0.0, im)
    return jnp.concatenate([re, extra], 0), jnp.concatenate([im, jnp.zeros_like(extra)], 0)


def repack_rows(idx, re, im):
    first = (idx[0] + idx[1]) == 0
    rows = lax.broadcasted_iota(jnp.int32, (64, re.shape[1]), 0)
    return re[:64], jnp.where((rows == 0) & first, re[64:65, :], im[:64])


def row_transform(idx, blocks, mats, tw, grid):
    for at in range(8):
        grid[:, :, 128 * at : 128 * at + 128] = blocks[at]
    re, im = unpack_rows(idx, grid[0], grid[1], 8)
    quarters = [(re[:, q * 256 : q * 256 + 256], im[:, q * 256 : q * 256 + 256]) for q in range(4)]
    sum02 = [quarters[0][p] + quarters[2][p] for p in range(2)]
    dif02 = [quarters[0][p] - quarters[2][p] for p in range(2)]
    sum13 = [quarters[1][p] + quarters[3][p] for p in range(2)]
    dif13 = [quarters[1][p] - quarters[3][p] for p in range(2)]
    step = turned(dif13[0], dif13[1], -1)
    parts = [
        (sum02[0] + sum13[0], sum02[1] + sum13[1]),
        (dif02[0] + step[0], dif02[1] + step[1]),
        (sum02[0] - sum13[0], sum02[1] - sum13[1]),
        (dif02[0] - step[0], dif02[1] - step[1]),
    ]
    for r in range(1, 4):
        parts[r] = times(parts[r][0], parts[r][1], tw[r : r + 1, :], -tw[4 + r : 5 + r, :])
    return dft_right(
        jnp.concatenate([p[0] for p in parts], 0),
        jnp.concatenate([p[1] for p in parts], 0),
        mats,
        -1.0,
    )


def scene_rows_kernel(idx, blocks, f, tw, out, grid):
    re, im = row_transform(idx, blocks, mats_of(f), tw, grid)
    out[0] = re
    out[1] = im


def blur_kernel(idx, blocks, f, tw, spectrum, out, grid):
    mats = mats_of(f)
    re, im = row_transform(idx, blocks, mats, tw, grid)
    re, im = times(re, im, spectrum[0], spectrum[1])
    mats = tuple(m[:, :128] for m in mats)
    re, im = dft_right(re, im, mats, 1.0)
    sum_re, sum_im = re[:72], im[:72]
    for r in range(1, 4):
        add = times(
            re[r * 72 : r * 72 + 72],
            im[r * 72 : r * 72 + 72],
            tw[8 + r : 9 + r, :128],
            tw[12 + r : 13 + r, :128],
        )
        sum_re = sum_re + add[0]
        sum_im = sum_im + add[1]
    re, im = repack_rows(idx, sum_re, sum_im)
    out[0] = re
    out[1] = im


def moved_lanes(x, e, lanes):
    if e == 0:
        return x
    rolled = pltpu.roll(x, (-e) % 128, 1)
    return jnp.where(lanes == (127 if e > 0 else 0), 0.0, rolled)


def moved_rows(x, a):
    if a == 0:
        return x
    return pltpu.roll(x, (-a) % x.shape[0], 0)


ROWS = 144


def net_kernel(pixel_count, idx, w1, b1, w2, *refs):
    blocks = refs[:2]
    v, strip, edge, g_out, acc, loss_out = refs[2:8]
    grid, win_taps, g_taps, hidden, sums = refs[8:]
    for d, e in relations:
        s, c = from_of(idx, d, e)
        at = 2 * s + c
        grid[pl.ds(aligned(at, 64), 64), :] = blocks[e][d, 0]
        grid[pl.ds(aligned(at + 8, 64), 64), :] = blocks[e][d, 1]
    target = jnp.where(
        idx[1] == 0,
        jnp.concatenate([edge[...], strip[0:136, :]], 0),
        jnp.concatenate([strip[120:256, :], edge[...]], 0),
    )
    rows = lax.broadcasted_iota(jnp.int32, (ROWS, 128), 0)
    lanes = lax.broadcasted_iota(jnp.int32, (ROWS, 128), 1)
    row_global = rows + (2 * idx[0] + idx[1]) * 128 - 8
    inside = (row_global >= 0) & (row_global < N)
    window = jnp.where(inside, by_left(v[0], v[1], grid[...]), 0.0)
    for e in (-1, 0, 1):
        side = moved_lanes(window, e, lanes)
        for a in (-1, 0, 1):
            win_taps[3 * (a + 1) + e + 1] = moved_rows(side, a)
    step = 16
    for k in range(ROWS // step):
        part = pl.ds(k * step, step)

        def forward(c, total, part=part):
            pre = jnp.full((step, 128), b1[c], F32)
            for t in range(9):
                pre = pre + w1[c, t] * win_taps[t, part, :]
            hid = jnp.maximum(pre, 0.0)
            hidden[c, part, :] = hid
            return tuple(total[t] + w2[t, c] * hid for t in range(9))

        total = lax.fori_loop(
            0, 32, forward, tuple(jnp.zeros((step, 128), F32) for _ in range(9))
        )
        for t in range(9):
            sums[t, part, :] = total[t]
    restored = window
    for e in (-1, 0, 1):
        side = None
        for a in (-1, 0, 1):
            part = moved_rows(jnp.where(inside, sums[3 * (a + 1) + e + 1], 0.0), a)
            side = part if side is None else side + part
        restored = restored + moved_lanes(side, e, lanes)
    residual = jnp.where(inside, restored - target, 0.0)
    own = (rows >= 8) & (rows < 136)
    own_residual = jnp.where(own, residual, 0.0)
    loss_out[...] = jnp.sum((own_residual * own_residual).reshape(ROWS // 8, 8, 128), 0)
    g_restored = (2.0 / pixel_count) * residual
    for e in (-1, 0, 1):
        side = moved_lanes(g_restored, -e, lanes)
        for a in (-1, 0, 1):
            g_taps[3 * (a + 1) + e + 1] = jnp.where(inside, moved_rows(side, -a), 0.0)
    acc[...] = jnp.zeros_like(acc)

    def folded(x):
        return x if x.shape[0] == 8 else x[:8] + x[8:]

    for start, step, mine in [(0, 8, False)] + [(8 + 16 * k, 16, True) for k in range(8)] + [
        (136, 8, False)
    ]:
        part = pl.ds(start, step)

        def backward(c, total, part=part, step=step, mine=mine):
            hid = hidden[c, part, :]
            gh = w2[0, c] * g_taps[0, part, :]
            for t in range(1, 9):
                gh = gh + w2[t, c] * g_taps[t, part, :]
            gp = jnp.where(hid > 0.0, gh, 0.0)
            if mine:
                for t in range(9):
                    acc[c, t] += folded(gp * win_taps[t, part, :])
                    acc[c, 9 + t] += folded(hid * g_taps[t, part, :])
                acc[c, 18] += folded(gp)
            return tuple(total[t] + w1[c, t] * gp for t in range(9))

        total = lax.fori_loop(
            0, 32, backward, tuple(jnp.zeros((step, 128), F32) for _ in range(9))
        )
        for t in range(9):
            sums[t, part, :] = total[t]
    g_window = g_restored
    for e in (-1, 0, 1):
        side = None
        for a in (-1, 0, 1):
            part = moved_rows(sums[3 * (a + 1) + e + 1], -a)
            side = part if side is None else side + part
        g_window = g_window + moved_lanes(side, -e, lanes)
    g_out[...] = g_window[8:136]


def otf_grad_kernel(idx, *refs):
    blocks = refs[:2]
    w, f, tw, spectrum, out, window, grid = refs[2:]
    for d, e in relations:
        s, c = from_of(idx, d, e)
        window[pl.ds(aligned(2 * s + c, 128), 128), :] = blocks[e][d]
    packed = by_left(w[0], w[1], window[...])
    re, im = unpack_rows(idx, packed[:64], packed[64:], 8)
    res, ims = [re], [im]
    for r in range(1, 4):
        a, b = times(re, im, tw[8 + r : 9 + r, :128], -tw[12 + r : 13 + r, :128])
        res.append(a)
        ims.append(b)
    mats = mats_of(f)
    top = tuple(m[:128, :] for m in mats)
    re, im = dft_right(jnp.concatenate(res, 0), jnp.concatenate(ims, 0), top, -1.0)
    re, im = times(re, im, spectrum[0], -spectrum[1])
    re, im = dft_right(re, im, mats, 1.0)
    parts = []
    for r in range(4):
        a, b = re[r * 72 : r * 72 + 72], im[r * 72 : r * 72 + 72]
        if r:
            a, b = times(a, b, tw[r : r + 1, :], tw[4 + r : 5 + r, :])
        parts.append((a, b))
    for q in range(4):
        a, b = parts[0]
        for r in range(1, 4):
            more = turned(parts[r][0], parts[r][1], q * r)
            a = a + more[0]
            b = b + more[1]
        a, b = repack_rows(idx, a, b)
        grid[0, :, q * 256 : q * 256 + 256] = a
        grid[1, :, q * 256 : q * 256 + 256] = b
    eight_columns(out, grid)


def psf_grad_kernel(idx, blocks, far, f, tw, small, o0, o1, o2, o3, grid):
    mats = mats_of(f)
    for c in range(2):
        for s in range(4):
            grid[:, 128 * s + 64 * c : 128 * s + 64 * c + 64, :] = blocks[4 * c + s]
    row = lax.broadcasted_iota(jnp.int32, (256, 128), 0)
    zero_row = row == 0
    low_re, low_im = grid[0, :256, :], grid[1, :256, :]
    nyquist = jnp.where(zero_row, 0.5 * low_im, 0.0)
    low_re = jnp.where(zero_row, 0.5 * low_re, low_re)
    low_im = jnp.where(zero_row, 0.0, low_im)
    high = (grid[0, 256:, :], grid[1, 256:, :])
    twists = [(tw[:, r : r + 1], tw[:, 4 + r : 5 + r]) for r in range(4)]
    res, ims = [], []
    for r in range(4):
        add = turned(high[0], high[1], r)
        re, im = low_re + add[0], low_im + add[1]
        if r:
            re, im = times(re, im, twists[r][0], twists[r][1])
        re = re + nyquist if r % 2 == 0 else re - nyquist
        res.append(re)
        ims.append(im)
    g_psf = 2.0 * (
        by_left(mats[0], mats[1], jnp.concatenate(res, 1))
        - by_left(mats[2], mats[3], jnp.concatenate(ims, 1))
    )
    re, im = dft_left(g_psf * far[0], g_psf * far[1], mats, 1.0)
    first, second = None, None
    for r in range(4):
        a, b = re[:, r * 128 : r * 128 + 128], im[:, r * 128 : r * 128 + 128]
        if r:
            a, b = times(a, b, twists[r][0], twists[r][1])
        more = turned(a, b, r)
        first = [a, b] if r == 0 else [first[0] + a, first[1] + b]
        second = list(more) if r == 0 else [second[0] + more[0], second[1] + more[1]]
    for p in range(2):
        grid[p, :256, :] = first[p]
        grid[p, 256:, :] = second[p]
    for d, out in enumerate((o0, o1, o2, o3)):
        out[:, 0:128, :] = grid[:, pl.ds(aligned(spot_of(idx, d)[0], 128), 128), :]
        out[0, 128:136, :] = small[...]
        out[1, 128:136, :] = jnp.zeros((8, 128), F32)


def mask_grad_kernel(scale, idx, ratio, b0, b1, b2, b3, m, pupil, keep, send, grid, whole):
    small = None
    for d, block in enumerate((b0, b1, b2, b3)):
        grid[:, :, pl.ds(aligned(from_of(idx, d)[0], 128), 128)] = block[:, 0:128, :]
        part = block[0, 128:136, :]
        small = part if small is None else small + part
    re, im = dft_right(grid[0], grid[1], mats_of(m), 1.0)
    cols = lax.broadcasted_iota(jnp.int32, (128, 512), 1)
    factor = ratio[0] * scale
    factor = jnp.where((cols & idx[1]) == 1, -factor, factor)
    whole[...] = factor * (im * pupil[0] - re * pupil[1])
    both = jnp.concatenate([small, small], 1)
    keep[0:128, :] = whole[:, pl.ds(aligned(idx[1], 256), 256)]
    send[0:128, :] = whole[:, pl.ds(aligned(1 - idx[1], 256), 256)]
    keep[128:136, :] = both
    send[128:136, :] = both


def cut_kernel(ways, idx, keep, other, *refs):
    outs = refs[:ways]
    whole = refs[ways]
    whole[...] = keep[...] + other[...]
    piece = 128 // ways
    for d, out in enumerate(outs):
        to = lax.rem(idx[4] + d, ways)
        out[0:piece, :] = whole[pl.ds(aligned(to, piece), piece), :]
        out[piece : piece + 8, :] = whole[128:136, :]


def home_kernel(ways, idx, *refs):
    near = refs[:ways]
    far = refs[ways : 2 * ways]
    out = refs[2 * ways]
    piece = 128 // ways
    at_home = idx[0] == 1 + idx[1]
    central = (idx[0] == 1) | (idx[0] == 2)
    out[0:256, :] = jnp.zeros((256, 256), F32)
    out[768:1024, :] = jnp.zeros((256, 256), F32)
    for back in range(ways):
        y = lax.rem(idx[4] + ways - back, ways)
        for d in range(4):
            s = from_of(idx, d)[0]
            row = 256 + 128 * s + piece * y
            block = jnp.where(at_home, near[back][d], far[back][d])
            out[pl.ds(aligned(8 + 4 * s + y, 32) if ways == 4 else row, piece), :] = jnp.where(
                central, block, 0.0
            )


def on_device(lay, phase_mask, height_offsets, sample_ids, wave_ids, scene, w1, b1, w2):
    con = constants()
    s = lax.axis_index("sp")
    c = lax.axis_index("core")
    y = lax.axis_index("y")
    owner = c == lax.axis_index("grp")
    pixel_count = float(lay.dp * N * 128)
    scale_psf = 1.0 / (N * N * pupil_count(N))

    def swap(g, zh, y, c, s):
        return (g, zh, y, 1 - c, s)

    def along_sp(blocks):
        return [blocks[0]] + [
            lay.move(blocks[d], lambda g, zh, y, c, s, d=d: (g, zh, y, c, s + d))
            for d in (1, 2, 3)
        ]

    def to_eight(blocks):
        return lax.all_to_all(blocks, ("core", "sp"), 0, 0, tiled=True)

    def gathered(block):
        near = jnp.stack(along_sp([block] * 4))
        return near, lay.move(near, swap)

    ids = jnp.concatenate([sample_ids, wave_ids])
    ids = jnp.where(owner, ids, lay.move(ids, swap))
    idx = jnp.stack([s, c, ids[0], owner.astype(jnp.int32), y]).astype(jnp.int32)
    ratio = (550.0 / (400.0 + 10.0 * ids[1].astype(F32))).reshape(1)
    other = lay.move(
        jnp.concatenate(
            [lax.dynamic_slice_in_dim(scene[0], 512 * (1 - c), 512, 1), scene[0, :, 256:384]], 1
        ),
        swap,
    )

    mine, *sent = call(
        phase_kernel,
        (idx, ratio, phase_mask, height_offsets),
        (0, 1),
        [(128, 256)] * 4,
        [pltpu.VMEM((512, 256), jnp.int32), pltpu.VMEM((512, 256), F32), pltpu.SemaphoreType.DMA],
        {3: pl.ANY},
    )
    tables = ({1: 0, 2: 3}, {1: 2, 2: 1}, {1: 3, 2: 0})
    pieces = [mine] + [
        lay.move(
            block,
            lambda g, zh, y, c, s, to=to: (g, zh, y, c, to[s]) if s in to else None,
        )
        for block, to in zip(sent, tables)
    ]

    *columns, strip, edge = call(
        scene_kernel,
        (idx, scene, other),
        (0,),
        [(256, 128)] * 4 + [(256, 128), (8, 128)],
    )
    columns = along_sp(columns)
    edge = lay.move(edge, lambda g, zh, y, c, s: (g, zh, y, c, s + 1 - 2 * c))

    slot = 2 * s + c
    unpack = lax.dynamic_slice_in_dim(jnp.asarray(con["unpack"]), 128 * slot, ROWS, 1)
    pack = jnp.asarray(con["pack"])
    pack_rows = jnp.concatenate(
        [
            lax.dynamic_slice_in_dim(pack, 64 * slot, 64, 1),
            lax.dynamic_slice_in_dim(pack, 512 + 64 * slot, 64, 1),
        ],
        1,
    )

    *field, pupil = call(
        pupil_kernel,
        (idx, *pieces, con["m"]),
        (0,),
        [(2, 128, 128)] * 4 + [(2, 128, 512)],
        [pltpu.VMEM((2, 128, 512), F32)],
    )
    field = along_sp(field)
    (scene_part,) = call(
        scene_columns_kernel,
        (idx, *columns, con["pack"]),
        (0,),
        [(8, 2, 64, 128)],
        [pltpu.VMEM((N, 128), F32), pltpu.VMEM((2, 512, 128), F32)],
    )
    scene_part = to_eight(scene_part)
    far, otf_part = call(
        functools.partial(optics_kernel, scale_psf),
        (idx, *field, con["f"], con["tw_col"]),
        (0,),
        [(2, 256, 512), (8, 2, 64, 128)],
        [pltpu.VMEM((2, 512, 128), F32)],
    )
    otf_part = to_eight(otf_part)
    row_scratch = [pltpu.VMEM((2, 64, N), F32)]
    (spectrum,) = call(
        scene_rows_kernel,
        (idx, scene_part, con["f"], con["tw_row"]),
        (0,),
        [(2, 288, 256)],
        row_scratch,
    )
    (half_window,) = call(
        blur_kernel,
        (idx, otf_part, con["f"], con["tw_row"], spectrum),
        (0,),
        [(2, 64, 128)],
        row_scratch,
    )
    window_parts = gathered(half_window)
    g_window, acc, loss_part = call(
        functools.partial(net_kernel, pixel_count),
        (idx, w1, b1, w2, *window_parts, unpack, strip, edge),
        (0, 1, 2, 3),
        [(128, 128), (32, 19, 8, 128), (8, 128)],
        [
            pltpu.VMEM((N, 128), F32),
            pltpu.VMEM((9, ROWS, 128), F32),
            pltpu.VMEM((9, ROWS, 128), F32),
            pltpu.VMEM((32, ROWS, 128), F32),
            pltpu.VMEM((9, ROWS, 128), F32),
        ],
    )
    small = jnp.concatenate(
        [jnp.sum(acc, (2, 3)).reshape(-1), jnp.sum(loss_part).reshape(1), jnp.zeros((415,), F32)]
    ).reshape(8, 128)
    g_parts = gathered(g_window)
    (otf_grad,) = call(
        otf_grad_kernel,
        (idx, *g_parts, pack_rows, con["f"], con["tw_row"], spectrum),
        (0,),
        [(8, 2, 64, 128)],
        [pltpu.VMEM((N, 128), F32), pltpu.VMEM((2, 64, N), F32)],
    )
    otf_grad = to_eight(otf_grad)
    field_grad = along_sp(
        call(
            psf_grad_kernel,
            (idx, otf_grad, far, con["f"], con["tw_col"], small),
            (0,),
            [(2, 136, 128)] * 4,
            [pltpu.VMEM((2, 512, 128), F32)],
        )
    )
    keep, send = call(
        functools.partial(mask_grad_kernel, 2.0 * scale_psf),
        (idx, ratio, *field_grad, con["m"], pupil),
        (0, 1),
        [(136, 256)] * 2,
        [pltpu.VMEM((2, 128, 512), F32), pltpu.VMEM((128, 512), F32)],
    )

    piece = 128 // lay.y
    blocks = call(
        functools.partial(cut_kernel, lay.y),
        (idx, keep, lay.move(send, swap)),
        (0,),
        [(piece + 8, 256)] * lay.y,
        [pltpu.VMEM((136, 256), F32)],
    )
    total = blocks[0]
    for d in range(1, lay.y):
        total = total + lay.move(
            blocks[d], lambda g, zh, y, c, s, d=d: (g, zh, y + d, c, s)
        )
    total = total + lay.move(total, lambda g, zh, y, c, s: (1 - g, zh, y, c, s))
    part = total
    for d in range(1, lay.zh):
        total = total + lay.move(part, lambda g, zh, y, c, s, d=d: (g, zh + d, y, c, s))
    small = total[piece:, :128].reshape(-1)
    total = total[:piece]
    home = jnp.stack(
        [total]
        + [
            lay.move(
                total,
                lambda g, zh, y, c, s, d=d: (
                    (g, zh, y, c, 1 + c) if (s + d - 1 - c) % 4 == 0 else None
                ),
            )
            for d in (1, 2, 3)
        ]
    )
    near = [home] + [
        lay.move(
            home,
            lambda g, zh, y, c, s, d=d: (g, zh, y + d, c, s) if s == 1 + c else None,
        )
        for d in range(1, lay.y)
    ]
    across = [
        lay.move(
            block, lambda g, zh, y, c, s: (g, zh, y, 1 - c, s) if s == 1 + c else None
        )
        for block in near
    ]
    (mask_grad,) = call(
        functools.partial(home_kernel, lay.y), (idx, *near, *across), (0,), [(N, 256)]
    )
    table = small[:608].reshape(32, 19)
    return (
        mask_grad,
        table[:, :9],
        table[:, 18],
        table[:, 9:18].T,
        small[608] / pixel_count,
    )


def solution(mesh):
    lay = Layout(mesh)
    images = ("zh", "y", "core")
    placed = (
        P(None, "sp"),
        P(None, None, "sp"),
        P(images),
        P(images),
        P(images, "sp", None),
        P(),
        P(),
        P(),
    )
    return jax.shard_map(
        functools.partial(on_device, lay),
        mesh=lay.mesh,
        in_specs=placed,
        out_specs=(P(None, "sp"), P(), P(), P(), P()),
        check_vma=False,
    )
```

```python
import functools
import itertools

import jax
import jax.numpy as jnp
import ml_dtypes
import numpy as np
from jax import lax
from jax.experimental import pallas as pl
from jax.experimental.pallas import tpu as pltpu
from jax.sharding import PartitionSpec as P

N = 1024
F32 = jnp.float32
BF16 = jnp.bfloat16
AXES = ("grp", "zh", "y", "core", "sp")
taps = ((-1, -1), (-1, 0), (-1, 1), (0, -1), (0, 0), (0, 1), (1, -1), (1, 0), (1, 1))


def halves(matrix):
    high = matrix.astype(ml_dtypes.bfloat16)
    low = (matrix - high.astype(np.float64)).astype(ml_dtypes.bfloat16)
    return high, low


def trig(rows, cols, length):
    angle = 2.0 * np.pi * (np.outer(rows, cols) % length) / length
    return np.cos(angle), np.sin(angle)


@functools.lru_cache(None)
def constants():
    half = np.arange(512)
    quarter = np.arange(256)
    fours = np.arange(4)
    cos_m, sin_m = trig(half, half, N)
    cos_f, sin_f = trig(quarter, quarter, 256)
    cos_w, sin_w = trig(half, np.arange(N), N)
    sin_w = -sin_w
    sin_w[0] = (-1.0) ** np.arange(N)
    packed = np.concatenate([cos_w, sin_w])
    weight = np.full((N,), 2.0)
    weight[0] = 1.0
    weight[512] = 1.0
    unpack = (packed * weight[:, None]).T / (N * N)
    rows_ext = (np.arange(N + 16) - 8) % N
    cos_t, sin_t = trig(quarter, fours, N)
    cos_c, sin_c = trig(256 + np.arange(128), fours, N)
    return {
        "m": np.stack(halves(cos_m) + halves(sin_m)),
        "f": np.stack(halves(cos_f) + halves(sin_f)),
        "pack": np.stack(halves(packed)),
        "unpack": np.stack(halves(unpack[rows_ext])),
        "tw_col": np.concatenate([cos_t, sin_t], 1).astype(np.float32),
        "tw_row": np.concatenate(
            [
                np.concatenate([cos_t, sin_t], 1).T,
                np.pad(np.concatenate([cos_c, sin_c], 1).T, ((0, 0), (0, 128))),
            ]
        ).astype(np.float32),
    }


def pupil_count(size_grid):
    coords = np.arange(size_grid) * 2 - size_grid + 1
    inside = (coords[:, None] ** 2 + coords[None, :] ** 2) * 4 <= size_grid * size_grid
    return float(np.sum(inside))


class Layout:
    def __init__(self, mesh):
        self.dp = mesh.shape["dp"]
        self.y = min(4, self.dp // 2)
        self.zh = self.dp // (2 * self.y)
        self.sp = mesh.shape["sp"]
        self.sizes = (2, self.zh, self.y, 2, self.sp)
        self.mesh = jax.sharding.Mesh(mesh.devices.reshape(self.sizes), AXES)

    def move(self, x, where):
        pairs = []
        for spot in itertools.product(*[range(n) for n in self.sizes]):
            goal = where(*spot)
            if goal is not None:
                pairs.append((self.flat(spot), self.flat(goal)))
        return lax.ppermute(x, AXES, pairs)

    def flat(self, spot):
        at = 0
        for place, size in zip(spot, self.sizes):
            at = at * size + place % size
        return at


def split(x):
    high = x.astype(BF16)
    return high, (x - high.astype(F32)).astype(BF16)


def dot(a, b):
    return lax.dot_general(a, b, (((1,), (0,)), ((), ())), preferred_element_type=F32)


def by_right(x, w_high, w_low):
    high, low = split(x)
    return dot(high, w_high) + (dot(high, w_low) + dot(low, w_high))


def by_left(w_high, w_low, x):
    high, low = split(x)
    return dot(w_high, high) + (dot(w_low, high) + dot(w_high, low))


def dft_right(re, im, mats, sign):
    rows = re.shape[0]
    both = jnp.concatenate([re, im], 0)
    by_cos = by_right(both, mats[0], mats[1])
    by_sin = by_right(both, mats[2], mats[3]) * sign
    return by_cos[:rows] - by_sin[rows:], by_cos[rows:] + by_sin[:rows]


def dft_left(re, im, mats, sign):
    cols = re.shape[1]
    both = jnp.concatenate([re, im], 1)
    by_cos = by_left(mats[0], mats[1], both)
    by_sin = by_left(mats[2], mats[3], both) * sign
    return by_cos[:, :cols] - by_sin[:, cols:], by_cos[:, cols:] + by_sin[:, :cols]


def turned(re, im, quarter_turns):
    quarter_turns %= 4
    if quarter_turns == 0:
        return re, im
    if quarter_turns == 1:
        return -im, re
    if quarter_turns == 2:
        return -re, -im
    return im, -re


def times(re, im, cos, sin):
    return re * cos - im * sin, re * sin + im * cos


def cos_sin(x):
    n = jnp.floor(x * (2.0 / np.pi) + 0.5)
    r = x - n * 1.5707963109016418
    r = r - n * 1.5893254712295857e-8
    q = n.astype(jnp.int32) & 3
    z = r * r
    sn = r + r * z * (-1.6666654611e-1 + z * (8.3321608736e-3 + z * -1.9515295891e-4))
    cs = 1.0 - 0.5 * z + z * z * (
        4.166664568298827e-2 + z * (-1.388731625493765e-3 + z * 2.443315711809948e-5)
    )
    odd = (q & 1) == 1
    c0 = jnp.where(odd, sn, cs)
    s0 = jnp.where(odd, cs, sn)
    cos = jnp.where((q == 1) | (q == 2), -c0, c0)
    sin = jnp.where(q >= 2, -s0, s0)
    return cos, sin


def spot_of(idx, d, e=0):
    return lax.rem(idx[0] + d, 4), lax.rem(idx[1] + e, 2)


def from_of(idx, d, e=0):
    return lax.rem(idx[0] + 4 - d, 4), lax.rem(idx[1] + 2 - e, 2)


def aligned(x, by):
    return pl.multiple_of(x * by, by)


def call(kernel, operands, in_smem, outs, scratch=(), apart=()):
    specs = []
    for at in range(len(operands)):
        space = pltpu.SMEM if at in in_smem else pltpu.VMEM
        specs.append(pl.BlockSpec(memory_space=pl.ANY if at in apart else space))
    return pl.pallas_call(
        kernel,
        out_shape=[jax.ShapeDtypeStruct(shape, F32) for shape in outs],
        in_specs=specs,
        out_specs=[pl.BlockSpec(memory_space=pltpu.VMEM) for _ in outs],
        scratch_shapes=list(scratch),
        compiler_params=pltpu.CompilerParams(vmem_limit_bytes=60 * 1024 * 1024),
    )(*operands)


relations = [(d, e) for e in range(2) for d in range(4)]


class Fetch:
    def __init__(self, sems, *pairs):
        self.copies = [
            pltpu.make_async_copy(src, dst, sems.at[at]) for at, (src, dst) in enumerate(pairs)
        ]
        for copy in self.copies:
            copy.start()

    def wait(self, at):
        self.copies[at].wait()


def bf16_buffer(*shape):
    return pltpu.VMEM(shape, BF16)


def fetch_sems(count):
    return pltpu.SemaphoreType.DMA((count,))


def ratio_of(wave):
    return 550.0 / (400.0 + 10.0 * jnp.full((8, 128), wave, jnp.int32).astype(F32))


def mats_of(ref):
    return ref[0], ref[1], ref[2], ref[3]


def phase_kernel(idx, ids, got, mask, offsets, own, one, two, three, slab, grabbed, phases, sems):
    owner = idx[2] == 1
    sample = jnp.where(owner, ids[0], got[0])
    fetch = Fetch(
        sems,
        (offsets.at[sample, pl.ds(256, 512), :], grabbed),
        (mask.at[pl.ds(256, 512), :], slab),
    )
    ratio = ratio_of(jnp.where(owner, ids[1], got[1]))[0:1, 0:1]
    fetch.wait(0)
    fetch.wait(1)
    phases[...] = ratio * (slab[...] + 0.1 * grabbed[...].astype(F32))
    s = idx[0]
    left = s == 1
    own[...] = phases[pl.ds(aligned(s, 128), 128), :]
    one[...] = phases[pl.ds(aligned(jnp.where(left, 0, 3), 128), 128), :]
    two[...] = phases[pl.ds(aligned(3 - s, 128), 128), :]
    three[...] = phases[pl.ds(aligned(jnp.where(left, 3, 0), 128), 128), :]


def scene_kernel(idx, scene, other, o0, o1, o2, o3, strip, edge):
    owner = idx[2] == 1
    c = idx[1]
    for d, out in enumerate((o0, o1, o2, o3)):
        s = spot_of(idx, d)[0]
        out[...] = jnp.where(
            owner,
            scene[0, :, pl.ds(aligned(4 * c + s, 128), 128)],
            other[:, pl.ds(aligned(s, 128), 128)],
        )
    strip[...] = jnp.where(owner, scene[0, :, 256:384], other[:, 512:640])
    edge[...] = jnp.where(c == 0, strip[248:256, :], strip[0:8, :])


def pupil_kernel(idx, a0, a1, a2, a3, m_far, o0, o1, o2, o3, pupil, grid, m, sems):
    fetch = Fetch(sems, (m_far, m))
    s = idx[0]
    c = idx[1]
    a0, a1, a2, a3 = a0[...], a1[...], a2[...], a3[...]
    left = jnp.where(s == 0, a1, jnp.where(s == 1, a0, jnp.where(s == 2, a2, a3)))
    right = jnp.where(s == 0, a3, jnp.where(s == 1, a2, jnp.where(s == 2, a0, a1)))
    phase = jnp.concatenate([left, right], 1)
    rows = lax.broadcasted_iota(jnp.int32, (128, 512), 0) + s * 128
    cols = lax.broadcasted_iota(jnp.int32, (128, 512), 1)
    up = (rows + 256) * 2 - N + 1
    across = (cols + 256) * 2 - N + 1
    inside = (up * up + across * across) * 4 <= N * N
    cos, sin = cos_sin(phase)
    re = jnp.where(inside, cos, 0.0)
    im = jnp.where(inside, sin, 0.0)
    pupil[0] = re
    pupil[1] = im
    flip = jnp.where((cols & c) == 1, -1.0, 1.0)
    fetch.wait(0)
    out_re, out_im = dft_right(re * flip, im * flip, mats_of(m), -1.0)
    grid[0] = out_re
    grid[1] = out_im
    for d, out in enumerate((o0, o1, o2, o3)):
        to = spot_of(idx, d)[0]
        out[...] = grid[:, :, pl.ds(aligned(to, 128), 128)]


def eight_rows(out, grid):
    for c in range(2):
        for s in range(4):
            out[4 * c + s] = grid[:, 128 * s + 64 * c : 128 * s + 64 * c + 64, :]


def eight_columns(out, grid):
    for at in range(8):
        out[at] = grid[:, :, 128 * at : 128 * at + 128]


def optics_kernel(scale, idx, b0, b1, b2, b3, f_far, tw, far, out, grid, f, sems):
    fetch = Fetch(sems, (f_far, f))
    for d, block in enumerate((b0, b1, b2, b3)):
        grid[:, pl.ds(aligned(from_of(idx, d)[0], 128), 128), :] = block[...]
    low = (grid[0, :256, :], grid[1, :256, :])
    high = (grid[0, 256:, :], grid[1, 256:, :])
    twists = [(tw[:, r : r + 1], tw[:, 4 + r : 5 + r]) for r in range(4)]
    res, ims = [], []
    for r in range(4):
        add = turned(high[0], high[1], -r)
        re, im = low[0] + add[0], low[1] + add[1]
        if r:
            re, im = times(re, im, twists[r][0], -twists[r][1])
        res.append(re)
        ims.append(im)
    fetch.wait(0)
    mats = mats_of(f)
    far_re, far_im = dft_left(
        jnp.concatenate(res, 1), jnp.concatenate(ims, 1), mats, -1.0
    )
    far[0] = far_re
    far[1] = far_im
    psf = scale * (far_re * far_re + far_im * far_im)
    psf_high, psf_low = split(psf)
    z_re = dot(mats[0], psf_high) + (dot(mats[1], psf_high) + dot(mats[0], psf_low))
    z_im = -(dot(mats[2], psf_high) + (dot(mats[3], psf_high) + dot(mats[2], psf_low)))
    first = [None, None]
    second = [None, None]
    nyquist = None
    for r in range(4):
        re = z_re[:, r * 128 : r * 128 + 128]
        im = z_im[:, r * 128 : r * 128 + 128]
        top = re[0:1, :]
        nyquist = top if r == 0 else (nyquist + top if r % 2 == 0 else nyquist - top)
        if r:
            re, im = times(re, im, twists[r][0], -twists[r][1])
        more = turned(re, im, -r)
        first = [re, im] if r == 0 else [first[0] + re, first[1] + im]
        second = list(more) if r == 0 else [second[0] + more[0], second[1] + more[1]]
    row = lax.broadcasted_iota(jnp.int32, (256, 128), 0)
    grid[0, :256, :] = first[0]
    grid[1, :256, :] = jnp.where(row == 0, nyquist, first[1])
    grid[0, 256:, :] = second[0]
    grid[1, 256:, :] = second[1]
    eight_rows(out, grid)


def scene_columns_kernel(idx, b0, b1, b2, b3, w_far, out, image, grid, w, sems):
    fetch = Fetch(sems, (w_far, w))
    for d, block in enumerate((b0, b1, b2, b3)):
        image[pl.ds(aligned(from_of(idx, d)[0], 256), 256), :] = block[...]
    fetch.wait(0)
    spectrum = by_left(w[0], w[1], image[...])
    grid[0] = spectrum[:512]
    grid[1] = spectrum[512:]
    eight_rows(out, grid)


def unpack_rows(idx, re, im, tail):
    rows = lax.broadcasted_iota(jnp.int32, re.shape, 0)
    first = (idx[0] + idx[1]) == 0
    nyquist = jnp.where(first, im[0:1, :], 0.0)
    tail_rows = lax.broadcasted_iota(jnp.int32, (tail, re.shape[1]), 0)
    extra = jnp.where(tail_rows == 0, nyquist, 0.0)
    im = jnp.where((rows == 0) & first, 0.0, im)
    return jnp.concatenate([re, extra], 0), jnp.concatenate([im, jnp.zeros_like(extra)], 0)


def repack_rows(idx, re, im):
    first = (idx[0] + idx[1]) == 0
    rows = lax.broadcasted_iota(jnp.int32, (64, re.shape[1]), 0)
    return re[:64], jnp.where((rows == 0) & first, re[64:65, :], im[:64])


def row_transform(idx, blocks, fetch, f, tw, grid):
    for at in range(8):
        grid[:, :, 128 * at : 128 * at + 128] = blocks[at]
    re, im = unpack_rows(idx, grid[0], grid[1], 8)
    quarters = [(re[:, q * 256 : q * 256 + 256], im[:, q * 256 : q * 256 + 256]) for q in range(4)]
    sum02 = [quarters[0][p] + quarters[2][p] for p in range(2)]
    dif02 = [quarters[0][p] - quarters[2][p] for p in range(2)]
    sum13 = [quarters[1][p] + quarters[3][p] for p in range(2)]
    dif13 = [quarters[1][p] - quarters[3][p] for p in range(2)]
    step = turned(dif13[0], dif13[1], -1)
    parts = [
        (sum02[0] + sum13[0], sum02[1] + sum13[1]),
        (dif02[0] + step[0], dif02[1] + step[1]),
        (sum02[0] - sum13[0], sum02[1] - sum13[1]),
        (dif02[0] - step[0], dif02[1] - step[1]),
    ]
    for r in range(1, 4):
        parts[r] = times(parts[r][0], parts[r][1], tw[r : r + 1, :], -tw[4 + r : 5 + r, :])
    fetch.wait(0)
    mats = mats_of(f)
    return dft_right(
        jnp.concatenate([p[0] for p in parts], 0),
        jnp.concatenate([p[1] for p in parts], 0),
        mats,
        -1.0,
    )


def scene_rows_kernel(idx, blocks, f_far, tw, out, grid, f, sems):
    re, im = row_transform(idx, blocks, Fetch(sems, (f_far, f)), f, tw, grid)
    out[0] = re
    out[1] = im


def blur_kernel(idx, blocks, f_far, tw, spectrum, out, grid, f, sems):
    re, im = row_transform(idx, blocks, Fetch(sems, (f_far, f)), f, tw, grid)
    mats = mats_of(f)
    re, im = times(re, im, spectrum[0], spectrum[1])
    mats = tuple(m[:, :128] for m in mats)
    re, im = dft_right(re, im, mats, 1.0)
    sum_re, sum_im = re[:72], im[:72]
    for r in range(1, 4):
        add = times(
            re[r * 72 : r * 72 + 72],
            im[r * 72 : r * 72 + 72],
            tw[8 + r : 9 + r, :128],
            tw[12 + r : 13 + r, :128],
        )
        sum_re = sum_re + add[0]
        sum_im = sum_im + add[1]
    re, im = repack_rows(idx, sum_re, sum_im)
    out[0] = re
    out[1] = im


def moved_lanes(x, e, lanes):
    if e == 0:
        return x
    rolled = pltpu.roll(x, (-e) % 128, 1)
    return jnp.where(lanes == (127 if e > 0 else 0), 0.0, rolled)


def moved_rows(x, a):
    if a == 0:
        return x
    return pltpu.roll(x, (-a) % x.shape[0], 0)


ROWS = 144


def net_kernel(pixel_count, idx, w1, b1, w2, *refs):
    blocks = refs[:2]
    v_far, strip, edge, g_out, sums_out = refs[2:7]
    grid, win_taps, g_taps, hidden, sums, acc, v, sems = refs[7:]
    slot = 2 * idx[0] + idx[1]
    fetch = Fetch(sems, (v_far.at[:, pl.ds(aligned(slot, 128), ROWS), :], v))
    for d, e in relations:
        s, c = from_of(idx, d, e)
        at = 2 * s + c
        grid[pl.ds(aligned(at, 64), 64), :] = blocks[e][d, 0]
        grid[pl.ds(aligned(at + 8, 64), 64), :] = blocks[e][d, 1]
    target = jnp.where(
        idx[1] == 0,
        jnp.concatenate([edge[...], strip[0:136, :]], 0),
        jnp.concatenate([strip[120:256, :], edge[...]], 0),
    )
    rows = lax.broadcasted_iota(jnp.int32, (ROWS, 128), 0)
    lanes = lax.broadcasted_iota(jnp.int32, (ROWS, 128), 1)
    row_global = rows + (2 * idx[0] + idx[1]) * 128 - 8
    inside = (row_global >= 0) & (row_global < N)
    fetch.wait(0)
    window = jnp.where(inside, by_left(v[0], v[1], grid[...]), 0.0)
    for e in (-1, 0, 1):
        side = moved_lanes(window, e, lanes)
        for a in (-1, 0, 1):
            win_taps[3 * (a + 1) + e + 1] = moved_rows(side, a)
    step = 24
    for k in range(ROWS // step):
        part = pl.ds(k * step, step)

        def forward(c, total, part=part):
            pre = w1[c, 0] * win_taps[0, part, :]
            for t in range(1, 9):
                pre = pre + w1[c, t] * win_taps[t, part, :]
            hid = jnp.maximum(pre + b1[c], 0.0)
            hidden[c, part, :] = hid
            return tuple(total[t] + w2[t, c] * hid for t in range(9))

        total = lax.fori_loop(
            0, 32, forward, tuple(jnp.zeros((step, 128), F32) for _ in range(9)), unroll=4
        )
        for t in range(9):
            sums[t, part, :] = total[t]
    restored = window
    for e in (-1, 0, 1):
        side = None
        for a in (-1, 0, 1):
            part = moved_rows(jnp.where(inside, sums[3 * (a + 1) + e + 1], 0.0), a)
            side = part if side is None else side + part
        restored = restored + moved_lanes(side, e, lanes)
    residual = jnp.where(inside, restored - target, 0.0)
    own = (rows >= 8) & (rows < 136)
    own_residual = jnp.where(own, residual, 0.0)
    loss = jnp.sum(own_residual * own_residual, 0, keepdims=True)
    g_restored = (2.0 / pixel_count) * residual
    for e in (-1, 0, 1):
        side = moved_lanes(g_restored, -e, lanes)
        for a in (-1, 0, 1):
            g_taps[3 * (a + 1) + e + 1] = jnp.where(inside, moved_rows(side, -a), 0.0)
    acc[...] = jnp.zeros_like(acc)

    def folded(x):
        total = x[:8]
        for row in range(8, x.shape[0], 8):
            total = total + x[row : row + 8]
        return total

    for start, step, mine in [(0, 8, False)] + [(8 + 32 * k, 32, True) for k in range(4)] + [
        (136, 8, False)
    ]:
        part = pl.ds(start, step)

        def backward(c, total, part=part, step=step, mine=mine):
            hid = hidden[c, part, :]
            gh = w2[0, c] * g_taps[0, part, :]
            for t in range(1, 9):
                gh = gh + w2[t, c] * g_taps[t, part, :]
            gp = jnp.where(hid > 0.0, gh, 0.0)
            if mine:
                for t in range(9):
                    acc[c, t] += folded(gp * win_taps[t, part, :])
                    acc[c, 9 + t] += folded(hid * g_taps[t, part, :])
                acc[c, 18] += folded(gp)
            return tuple(total[t] + w1[c, t] * gp for t in range(9))

        total = lax.fori_loop(
            0, 32, backward, tuple(jnp.zeros((step, 128), F32) for _ in range(9)), unroll=4
        )
        for t in range(9):
            sums[t, part, :] = total[t]
    g_window = g_restored
    for e in (-1, 0, 1):
        side = None
        for a in (-1, 0, 1):
            part = moved_rows(sums[3 * (a + 1) + e + 1], -a)
            side = part if side is None else side + part
        g_window = g_window + moved_lanes(side, -e, lanes)
    g_out[...] = g_window[8:136]
    for c in range(32):
        sums_out[c, 0:19, :] = jnp.sum(acc[c], 1)
        sums_out[c, 19:24, :] = jnp.broadcast_to(loss, (5, 128))


def otf_grad_kernel(idx, *refs):
    blocks = refs[:2]
    w_far, f_far, tw, spectrum, out, window, grid, w, f, sems = refs[2:]
    slot = 2 * idx[0] + idx[1]
    fetch = Fetch(
        sems,
        (w_far.at[:, pl.ds(aligned(slot, 64), 64), :], w.at[:, pl.ds(0, 64), :]),
        (w_far.at[:, pl.ds(aligned(slot + 8, 64), 64), :], w.at[:, pl.ds(64, 64), :]),
        (f_far, f),
    )
    for d, e in relations:
        s, c = from_of(idx, d, e)
        window[pl.ds(aligned(2 * s + c, 128), 128), :] = blocks[e][d]
    fetch.wait(0)
    fetch.wait(1)
    packed = by_left(w[0], w[1], window[...])
    re, im = unpack_rows(idx, packed[:64], packed[64:], 8)
    res, ims = [re], [im]
    for r in range(1, 4):
        a, b = times(re, im, tw[8 + r : 9 + r, :128], -tw[12 + r : 13 + r, :128])
        res.append(a)
        ims.append(b)
    fetch.wait(2)
    mats = mats_of(f)
    top = tuple(m[:128, :] for m in mats)
    re, im = dft_right(jnp.concatenate(res, 0), jnp.concatenate(ims, 0), top, -1.0)
    re, im = times(re, im, spectrum[0], -spectrum[1])
    re, im = dft_right(re, im, mats, 1.0)
    parts = []
    for r in range(4):
        a, b = re[r * 72 : r * 72 + 72], im[r * 72 : r * 72 + 72]
        if r:
            a, b = times(a, b, tw[r : r + 1, :], tw[4 + r : 5 + r, :])
        parts.append((a, b))
    for q in range(4):
        a, b = parts[0]
        for r in range(1, 4):
            more = turned(parts[r][0], parts[r][1], q * r)
            a = a + more[0]
            b = b + more[1]
        a, b = repack_rows(idx, a, b)
        grid[0, :, q * 256 : q * 256 + 256] = a
        grid[1, :, q * 256 : q * 256 + 256] = b
    eight_columns(out, grid)


def psf_grad_kernel(idx, blocks, far_far, f_far, tw, small, o0, o1, o2, o3, grid, far, f, sems):
    fetch = Fetch(sems, (f_far, f), (far_far, far))
    for c in range(2):
        for s in range(4):
            grid[:, 128 * s + 64 * c : 128 * s + 64 * c + 64, :] = blocks[4 * c + s]
    row = lax.broadcasted_iota(jnp.int32, (256, 128), 0)
    zero_row = row == 0
    low_re, low_im = grid[0, :256, :], grid[1, :256, :]
    nyquist = jnp.where(zero_row, 0.5 * low_im, 0.0)
    low_re = jnp.where(zero_row, 0.5 * low_re, low_re)
    low_im = jnp.where(zero_row, 0.0, low_im)
    high = (grid[0, 256:, :], grid[1, 256:, :])
    twists = [(tw[:, r : r + 1], tw[:, 4 + r : 5 + r]) for r in range(4)]
    res, ims = [], []
    for r in range(4):
        add = turned(high[0], high[1], r)
        re, im = low_re + add[0], low_im + add[1]
        if r:
            re, im = times(re, im, twists[r][0], twists[r][1])
        re = re + nyquist if r % 2 == 0 else re - nyquist
        res.append(re)
        ims.append(im)
    fetch.wait(0)
    mats = mats_of(f)
    g_psf = 2.0 * (
        by_left(mats[0], mats[1], jnp.concatenate(res, 1))
        - by_left(mats[2], mats[3], jnp.concatenate(ims, 1))
    )
    fetch.wait(1)
    re, im = dft_left(g_psf * far[0], g_psf * far[1], mats, 1.0)
    first, second = None, None
    for r in range(4):
        a, b = re[:, r * 128 : r * 128 + 128], im[:, r * 128 : r * 128 + 128]
        if r:
            a, b = times(a, b, twists[r][0], twists[r][1])
        more = turned(a, b, r)
        first = [a, b] if r == 0 else [first[0] + a, first[1] + b]
        second = list(more) if r == 0 else [second[0] + more[0], second[1] + more[1]]
    for p in range(2):
        grid[p, :256, :] = first[p]
        grid[p, 256:, :] = second[p]
    for d, out in enumerate((o0, o1, o2, o3)):
        out[:, 0:128, :] = grid[:, pl.ds(aligned(spot_of(idx, d)[0], 128), 128), :]
        out[0, 128:136, :] = small[...]
        out[1, 128:136, :] = jnp.zeros((8, 128), F32)


def mask_grad_kernel(scale, idx, ids, got, *refs):
    b0, b1, b2, b3, m_far, pupil_far, keep, send, grid, whole, m, pupil, sems = refs
    fetch = Fetch(sems, (m_far, m), (pupil_far, pupil))
    small = None
    for d, block in enumerate((b0, b1, b2, b3)):
        grid[:, :, pl.ds(aligned(from_of(idx, d)[0], 128), 128)] = block[:, 0:128, :]
        part = block[0, 128:136, :]
        small = part if small is None else small + part
    fetch.wait(0)
    re, im = dft_right(grid[0], grid[1], mats_of(m), 1.0)
    fetch.wait(1)
    cols = lax.broadcasted_iota(jnp.int32, (128, 512), 1)
    factor = ratio_of(jnp.where(idx[2] == 1, ids[1], got[1]))[0:1, 0:1] * scale
    factor = jnp.where((cols & idx[1]) == 1, -factor, factor)
    whole[...] = factor * (im * pupil[0] - re * pupil[1])
    both = jnp.concatenate([small, small], 1)
    keep[0:128, :] = whole[:, pl.ds(aligned(idx[1], 256), 256)]
    send[0:128, :] = whole[:, pl.ds(aligned(1 - idx[1], 256), 256)]
    keep[128:136, :] = both
    send[128:136, :] = both


def cut_kernel(ways, idx, keep, other, *refs):
    outs = refs[:ways]
    whole = refs[ways]
    whole[...] = keep[...] + other[...]
    piece = 128 // ways
    for d, out in enumerate(outs):
        to = lax.rem(idx[3] + d, ways)
        out[0:piece, :] = whole[pl.ds(aligned(to, piece), piece), :]
        out[piece : piece + 8, :] = whole[128:136, :]


def home_kernel(ways, idx, *refs):
    blocks = refs[:ways]
    out = refs[ways]
    piece = 128 // ways
    central = (idx[0] == 1) | (idx[0] == 2)
    out[0:256, :] = jnp.zeros((256, 256), F32)
    out[768:1024, :] = jnp.zeros((256, 256), F32)
    for back in range(ways):
        y = lax.rem(idx[3] + ways - back, ways)
        for d in range(4):
            s = from_of(idx, d)[0]
            at = (2 + s) * ways + y
            out[pl.ds(aligned(at, piece), piece), :] = jnp.where(
                central, blocks[back][d], 0.0
            )


def on_device(lay, phase_mask, height_offsets, sample_ids, wave_ids, scene, w1, b1, w2):
    con = constants()
    s = lax.axis_index("sp")
    c = lax.axis_index("core")
    y = lax.axis_index("y")
    owner = c == lax.axis_index("grp")
    pixel_count = float(lay.dp * N * 128)
    scale_psf = 1.0 / (N * N * pupil_count(N))
    idx = jnp.stack([s, c, owner.astype(jnp.int32), y]).astype(jnp.int32)

    def swap(g, zh, y, c, s):
        return (g, zh, y, 1 - c, s)

    def along_sp(blocks):
        return [blocks[0]] + [
            lay.move(blocks[d], lambda g, zh, y, c, s, d=d: (g, zh, y, c, s + d))
            for d in (1, 2, 3)
        ]

    def to_eight(blocks):
        return lax.all_to_all(blocks, ("core", "sp"), 0, 0, tiled=True)

    def gathered(block):
        near = jnp.stack(along_sp([block] * 4))
        return near, lay.move(near, swap)

    ids = jnp.concatenate([sample_ids, wave_ids])
    got = lay.move(ids, swap)

    mine, *sent = call(
        phase_kernel,
        (idx, ids, got, phase_mask, height_offsets),
        (0, 1, 2),
        [(128, 256)] * 4,
        [
            pltpu.VMEM((512, 256), F32),
            pltpu.VMEM((512, 256), jnp.int32),
            pltpu.VMEM((512, 256), F32),
            fetch_sems(2),
        ],
        (3, 4),
    )
    tables = ({1: 0, 2: 3}, {1: 2, 2: 1}, {1: 3, 2: 0})
    pieces = [mine] + [
        lay.move(
            block,
            lambda g, zh, y, c, s, to=to: (g, zh, y, c, to[s]) if s in to else None,
        )
        for block, to in zip(sent, tables)
    ]

    scene, mine = lax.optimization_barrier((scene, mine))
    pieces[0] = mine
    other = lay.move(
        jnp.concatenate(
            [lax.dynamic_slice_in_dim(scene[0], 512 * (1 - c), 512, 1), scene[0, :, 256:384]], 1
        ),
        swap,
    )
    *columns, strip, edge = call(
        scene_kernel,
        (idx, scene, other),
        (0,),
        [(256, 128)] * 4 + [(256, 128), (8, 128)],
    )
    columns = along_sp(columns)
    edge = lay.move(edge, lambda g, zh, y, c, s: (g, zh, y, c, s + 1 - 2 * c))

    *field, pupil = call(
        pupil_kernel,
        (idx, *pieces, con["m"]),
        (0,),
        [(2, 128, 128)] * 4 + [(2, 128, 512)],
        [pltpu.VMEM((2, 128, 512), F32), bf16_buffer(4, 512, 512), fetch_sems(1)],
        (5,),
    )
    field = along_sp(field)
    (scene_part,) = call(
        scene_columns_kernel,
        (idx, *columns, con["pack"]),
        (0,),
        [(8, 2, 64, 128)],
        [
            pltpu.VMEM((N, 128), F32),
            pltpu.VMEM((2, 512, 128), F32),
            bf16_buffer(2, N, N),
            fetch_sems(1),
        ],
        (5,),
    )
    scene_part = to_eight(scene_part)
    far, otf_part = call(
        functools.partial(optics_kernel, scale_psf),
        (idx, *field, con["f"], con["tw_col"]),
        (0,),
        [(2, 256, 512), (8, 2, 64, 128)],
        [pltpu.VMEM((2, 512, 128), F32), bf16_buffer(4, 256, 256), fetch_sems(1)],
        (5,),
    )
    otf_part = to_eight(otf_part)
    row_scratch = [pltpu.VMEM((2, 64, N), F32), bf16_buffer(4, 256, 256), fetch_sems(1)]
    (spectrum,) = call(
        scene_rows_kernel,
        (idx, scene_part, con["f"], con["tw_row"]),
        (0,),
        [(2, 288, 256)],
        row_scratch,
        (2,),
    )
    (half_window,) = call(
        blur_kernel,
        (idx, otf_part, con["f"], con["tw_row"], spectrum),
        (0,),
        [(2, 64, 128)],
        row_scratch,
        (2,),
    )
    window_parts = gathered(half_window)
    g_window, sums = call(
        functools.partial(net_kernel, pixel_count),
        (idx, w1, b1, w2, *window_parts, con["unpack"], strip, edge),
        (0, 1, 2, 3),
        [(128, 128), (32, 24, 128)],
        [
            pltpu.VMEM((N, 128), F32),
            pltpu.VMEM((9, ROWS, 128), F32),
            pltpu.VMEM((9, ROWS, 128), F32),
            pltpu.VMEM((32, ROWS, 128), F32),
            pltpu.VMEM((9, ROWS, 128), F32),
            pltpu.VMEM((32, 19, 8, 128), F32),
            bf16_buffer(2, ROWS, N),
            fetch_sems(1),
        ],
        (6,),
    )
    small = jnp.pad(jnp.sum(sums, 2).reshape(6, 128), ((0, 2), (0, 0)))
    g_parts = gathered(g_window)
    (otf_grad,) = call(
        otf_grad_kernel,
        (idx, *g_parts, con["pack"], con["f"], con["tw_row"], spectrum),
        (0,),
        [(8, 2, 64, 128)],
        [
            pltpu.VMEM((N, 128), F32),
            pltpu.VMEM((2, 64, N), F32),
            bf16_buffer(2, 128, N),
            bf16_buffer(4, 256, 256),
            fetch_sems(3),
        ],
        (3, 4),
    )
    otf_grad = to_eight(otf_grad)
    field_grad = along_sp(
        call(
            psf_grad_kernel,
            (idx, otf_grad, far, con["f"], con["tw_col"], small),
            (0,),
            [(2, 136, 128)] * 4,
            [
                pltpu.VMEM((2, 512, 128), F32),
                pltpu.VMEM((2, 256, 512), F32),
                bf16_buffer(4, 256, 256),
                fetch_sems(2),
            ],
            (2, 3),
        )
    )
    keep, send = call(
        functools.partial(mask_grad_kernel, 2.0 * scale_psf),
        (idx, ids, got, *field_grad, con["m"], pupil),
        (0, 1, 2),
        [(136, 256)] * 2,
        [
            pltpu.VMEM((2, 128, 512), F32),
            pltpu.VMEM((128, 512), F32),
            bf16_buffer(4, 512, 512),
            pltpu.VMEM((2, 128, 512), F32),
            fetch_sems(2),
        ],
        (7, 8),
    )

    piece = 128 // lay.y
    blocks = call(
        functools.partial(cut_kernel, lay.y),
        (idx, keep, lay.move(send, swap)),
        (0,),
        [(piece + 8, 256)] * lay.y,
        [pltpu.VMEM((136, 256), F32)],
    )
    total = blocks[0]
    for d in range(1, lay.y):
        total = total + lay.move(
            blocks[d], lambda g, zh, y, c, s, d=d: (g, zh, y + d, c, s)
        )
    total = total + lay.move(total, lambda g, zh, y, c, s: (1 - g, zh, y, c, s))
    part = total
    for d in range(1, lay.zh):
        total = total + lay.move(part, lambda g, zh, y, c, s, d=d: (g, zh + d, y, c, s))
    small = total[piece:, :128].reshape(-1)
    total = total[:piece]
    home = jnp.stack(
        [total]
        + [
            lay.move(
                total,
                lambda g, zh, y, c, s, d=d: (
                    (g, zh, y, c, 1 + c) if (s + d - 1 - c) % 4 == 0 else None
                ),
            )
            for d in (1, 2, 3)
        ]
    )
    at_home = s == 1 + c
    crossed = lay.move(home, lambda g, zh, y, c, s: (g, zh, y, 1 - c, s) if s == 1 + c else None)
    home = jnp.where(at_home, home, crossed)
    near = [home] + [
        lay.move(
            home, lambda g, zh, y, c, s, d=d: (g, zh, y + d, c, s) if s in (1, 2) else None
        )
        for d in range(1, lay.y)
    ]
    (mask_grad,) = call(functools.partial(home_kernel, lay.y), (idx, *near), (0,), [(N, 256)])
    table = small[:768].reshape(32, 24)
    return (
        mask_grad,
        table[:, :9],
        table[:, 18],
        table[:, 9:18].T,
        table[0, 19] / pixel_count,
    )


def solution(mesh):
    lay = Layout(mesh)
    images = ("zh", "y", "core")
    placed = (
        P(None, "sp"),
        P(None, None, "sp"),
        P(images),
        P(images),
        P(images, "sp", None),
        P(),
        P(),
        P(),
    )
    return jax.shard_map(
        functools.partial(on_device, lay),
        mesh=lay.mesh,
        in_specs=placed,
        out_specs=(P(None, "sp"), P(), P(), P(), P()),
        check_vma=False,
    )
```

```python
import functools
import itertools

import jax
import jax.numpy as jnp
import ml_dtypes
import numpy as np
from jax import lax
from jax.experimental import pallas as pl
from jax.experimental.pallas import tpu as pltpu
from jax.sharding import PartitionSpec as P

N = 1024
F32 = jnp.float32
BF16 = jnp.bfloat16
AXES = ("grp", "zh", "y", "core", "sp")
taps = ((-1, -1), (-1, 0), (-1, 1), (0, -1), (0, 0), (0, 1), (1, -1), (1, 0), (1, 1))


def halves(matrix):
    high = matrix.astype(ml_dtypes.bfloat16)
    low = (matrix - high.astype(np.float64)).astype(ml_dtypes.bfloat16)
    return high, low


def trig(rows, cols, length):
    angle = 2.0 * np.pi * (np.outer(rows, cols) % length) / length
    return np.cos(angle), np.sin(angle)


@functools.lru_cache(None)
def constants():
    half = np.arange(512)
    quarter = np.arange(256)
    fours = np.arange(4)
    cos_m, sin_m = trig(half, half, N)
    cos_f, sin_f = trig(quarter, quarter, 256)
    cos_w, sin_w = trig(half, np.arange(N), N)
    sin_w = -sin_w
    sin_w[0] = (-1.0) ** np.arange(N)
    packed = np.concatenate([cos_w, sin_w])
    weight = np.full((N,), 2.0)
    weight[0] = 1.0
    weight[512] = 1.0
    unpack = (packed * weight[:, None]).T / (N * N)
    rows_ext = (np.arange(N + 16) - 8) % N
    cos_t, sin_t = trig(quarter, fours, N)
    cos_c, sin_c = trig(256 + np.arange(128), fours, N)
    return {
        "m": np.stack(halves(cos_m) + halves(sin_m)),
        "f": np.stack(halves(cos_f) + halves(sin_f)),
        "pack": np.stack(halves(packed)),
        "unpack": np.stack(halves(unpack[rows_ext])),
        "tw_col": np.concatenate([cos_t, sin_t], 1).astype(np.float32),
        "tw_row": np.concatenate(
            [
                np.concatenate([cos_t, sin_t], 1).T,
                np.pad(np.concatenate([cos_c, sin_c], 1).T, ((0, 0), (0, 128))),
            ]
        ).astype(np.float32),
    }


def pupil_count(size_grid):
    coords = np.arange(size_grid) * 2 - size_grid + 1
    inside = (coords[:, None] ** 2 + coords[None, :] ** 2) * 4 <= size_grid * size_grid
    return float(np.sum(inside))


class Layout:
    def __init__(self, mesh):
        self.dp = mesh.shape["dp"]
        self.y = min(4, self.dp // 2)
        self.zh = self.dp // (2 * self.y)
        self.sp = mesh.shape["sp"]
        self.sizes = (2, self.zh, self.y, 2, self.sp)
        self.mesh = jax.sharding.Mesh(mesh.devices.reshape(self.sizes), AXES)

    def move(self, x, where):
        pairs = []
        for spot in itertools.product(*[range(n) for n in self.sizes]):
            goal = where(*spot)
            if goal is not None:
                pairs.append((self.flat(spot), self.flat(goal)))
        return lax.ppermute(x, AXES, pairs)

    def flat(self, spot):
        at = 0
        for place, size in zip(spot, self.sizes):
            at = at * size + place % size
        return at


def split(x):
    high = x.astype(BF16)
    return high, (x - high.astype(F32)).astype(BF16)


def dot(a, b):
    return lax.dot_general(a, b, (((1,), (0,)), ((), ())), preferred_element_type=F32)


def by_right(x, w_high, w_low):
    high, low = split(x)
    return dot(high, w_high) + (dot(high, w_low) + dot(low, w_high))


def by_left(w_high, w_low, x):
    high, low = split(x)
    return dot(w_high, high) + (dot(w_low, high) + dot(w_high, low))


def dft_right(re, im, mats, sign):
    rows = re.shape[0]
    both = jnp.concatenate([re, im], 0)
    by_cos = by_right(both, mats[0], mats[1])
    by_sin = by_right(both, mats[2], mats[3]) * sign
    return by_cos[:rows] - by_sin[rows:], by_cos[rows:] + by_sin[:rows]


def dft_left(re, im, mats, sign):
    cols = re.shape[1]
    both = jnp.concatenate([re, im], 1)
    by_cos = by_left(mats[0], mats[1], both)
    by_sin = by_left(mats[2], mats[3], both) * sign
    return by_cos[:, :cols] - by_sin[:, cols:], by_cos[:, cols:] + by_sin[:, :cols]


def turned(re, im, quarter_turns):
    quarter_turns %= 4
    if quarter_turns == 0:
        return re, im
    if quarter_turns == 1:
        return -im, re
    if quarter_turns == 2:
        return -re, -im
    return im, -re


def times(re, im, cos, sin):
    return re * cos - im * sin, re * sin + im * cos


def cos_sin(x):
    n = jnp.floor(x * (2.0 / np.pi) + 0.5)
    r = x - n * 1.5707963109016418
    r = r - n * 1.5893254712295857e-8
    q = n.astype(jnp.int32) & 3
    z = r * r
    sn = r + r * z * (-1.6666654611e-1 + z * (8.3321608736e-3 + z * -1.9515295891e-4))
    cs = 1.0 - 0.5 * z + z * z * (
        4.166664568298827e-2 + z * (-1.388731625493765e-3 + z * 2.443315711809948e-5)
    )
    odd = (q & 1) == 1
    c0 = jnp.where(odd, sn, cs)
    s0 = jnp.where(odd, cs, sn)
    cos = jnp.where((q == 1) | (q == 2), -c0, c0)
    sin = jnp.where(q >= 2, -s0, s0)
    return cos, sin


def spot_of(idx, d, e=0):
    return lax.rem(idx[0] + d, 4), lax.rem(idx[1] + e, 2)


def from_of(idx, d, e=0):
    return lax.rem(idx[0] + 4 - d, 4), lax.rem(idx[1] + 2 - e, 2)


def aligned(x, by):
    return pl.multiple_of(x * by, by)


def call(kernel, operands, in_smem, outs, scratch=(), apart=()):
    specs = []
    for at in range(len(operands)):
        space = pltpu.SMEM if at in in_smem else pltpu.VMEM
        specs.append(pl.BlockSpec(memory_space=pltpu.HBM if at in apart else space))
    return pl.pallas_call(
        kernel,
        out_shape=[jax.ShapeDtypeStruct(shape, F32) for shape in outs],
        in_specs=specs,
        out_specs=[pl.BlockSpec(memory_space=pltpu.VMEM) for _ in outs],
        scratch_shapes=list(scratch),
        compiler_params=pltpu.CompilerParams(vmem_limit_bytes=20 * 1024 * 1024),
    )(*operands)


relations = [(d, e) for e in range(2) for d in range(4)]


class Fetch:
    def __init__(self, sems, *pairs):
        self.copies = [
            pltpu.make_async_copy(src, dst, sems.at[at]) for at, (src, dst) in enumerate(pairs)
        ]
        for copy in self.copies:
            copy.start()

    def wait(self, at):
        self.copies[at].wait()


def bf16_buffer(*shape):
    return pltpu.VMEM(shape, BF16)


def fetch_sems(count):
    return pltpu.SemaphoreType.DMA((count,))


def ratio_of(wave):
    return 550.0 / (400.0 + 10.0 * jnp.full((8, 128), wave, jnp.int32).astype(F32))


def mats_of(ref):
    return ref[0], ref[1], ref[2], ref[3]


def phase_kernel(idx, phases, own, one, two, three):
    s = idx[0]
    left = s == 1
    own[...] = phases[pl.ds(aligned(s, 128), 128), :]
    one[...] = phases[pl.ds(aligned(jnp.where(left, 0, 3), 128), 128), :]
    two[...] = phases[pl.ds(aligned(3 - s, 128), 128), :]
    three[...] = phases[pl.ds(aligned(jnp.where(left, 3, 0), 128), 128), :]


def scene_kernel(idx, scene, other, o0, o1, o2, o3, strip, edge):
    owner = idx[2] == 1
    c = idx[1]
    for d, out in enumerate((o0, o1, o2, o3)):
        s = spot_of(idx, d)[0]
        out[...] = jnp.where(
            owner,
            scene[0, :, pl.ds(aligned(4 * c + s, 128), 128)],
            other[:, pl.ds(aligned(s, 128), 128)],
        )
    strip[...] = jnp.where(owner, scene[0, :, 256:384], other[:, 512:640])
    edge[...] = jnp.where(c == 0, strip[248:256, :], strip[0:8, :])


def pupil_kernel(idx, *refs):
    m_far, o0, o1, o2, o3, pupil, grid, m, sems = refs[8:]
    fetch = Fetch(sems, (m_far, m))
    s = idx[0]
    c = idx[1]
    owner = idx[2] == 1
    a0, a1, a2, a3 = [jnp.where(owner, refs[at][...], refs[at + 4][...]) for at in range(4)]
    left = jnp.where(s == 0, a1, jnp.where(s == 1, a0, jnp.where(s == 2, a2, a3)))
    right = jnp.where(s == 0, a3, jnp.where(s == 1, a2, jnp.where(s == 2, a0, a1)))
    phase = jnp.concatenate([left, right], 1)
    rows = lax.broadcasted_iota(jnp.int32, (128, 512), 0) + s * 128
    cols = lax.broadcasted_iota(jnp.int32, (128, 512), 1)
    up = (rows + 256) * 2 - N + 1
    across = (cols + 256) * 2 - N + 1
    inside = (up * up + across * across) * 4 <= N * N
    cos, sin = cos_sin(phase)
    re = jnp.where(inside, cos, 0.0)
    im = jnp.where(inside, sin, 0.0)
    pupil[0] = re
    pupil[1] = im
    flip = jnp.where((cols & c) == 1, -1.0, 1.0)
    fetch.wait(0)
    out_re, out_im = dft_right(re * flip, im * flip, mats_of(m), -1.0)
    grid[0] = out_re
    grid[1] = out_im
    for d, out in enumerate((o0, o1, o2, o3)):
        to = spot_of(idx, d)[0]
        out[...] = grid[:, :, pl.ds(aligned(to, 128), 128)]


def eight_rows(out, grid, at):
    for c in range(2):
        for s in range(4):
            row = 128 * s + 64 * c
            out[4 * c + s, at : at + 2] = grid[:, row : row + 64, :]


def eight_columns(out, grid):
    for at in range(8):
        out[at] = grid[:, :, 128 * at : 128 * at + 128]


def optics_kernel(scale, idx, b0, b1, b2, b3, *refs):
    i0, i1, i2, i3, f_far, tw_far, w_far, far, out, grid, image, f, tw, w, sems = refs
    fetch = Fetch(sems, (tw_far, tw), (f_far, f), (w_far, w))
    for d, block in enumerate((b0, b1, b2, b3)):
        grid[:, pl.ds(aligned(from_of(idx, d)[0], 128), 128), :] = block[...]
    low = (grid[0, :256, :], grid[1, :256, :])
    high = (grid[0, 256:, :], grid[1, 256:, :])
    fetch.wait(0)
    twists = [(tw[:, r : r + 1], tw[:, 4 + r : 5 + r]) for r in range(4)]
    res, ims = [], []
    for r in range(4):
        add = turned(high[0], high[1], -r)
        re, im = low[0] + add[0], low[1] + add[1]
        if r:
            re, im = times(re, im, twists[r][0], -twists[r][1])
        res.append(re)
        ims.append(im)
    fetch.wait(1)
    mats = mats_of(f)
    far_re, far_im = dft_left(
        jnp.concatenate(res, 1), jnp.concatenate(ims, 1), mats, -1.0
    )
    far[0] = far_re
    far[1] = far_im
    psf = scale * (far_re * far_re + far_im * far_im)
    psf_high, psf_low = split(psf)
    z_re = dot(mats[0], psf_high) + (dot(mats[1], psf_high) + dot(mats[0], psf_low))
    z_im = -(dot(mats[2], psf_high) + (dot(mats[3], psf_high) + dot(mats[2], psf_low)))
    first = [None, None]
    second = [None, None]
    nyquist = None
    for r in range(4):
        re = z_re[:, r * 128 : r * 128 + 128]
        im = z_im[:, r * 128 : r * 128 + 128]
        top = re[0:1, :]
        nyquist = top if r == 0 else (nyquist + top if r % 2 == 0 else nyquist - top)
        if r:
            re, im = times(re, im, twists[r][0], -twists[r][1])
        more = turned(re, im, -r)
        first = [re, im] if r == 0 else [first[0] + re, first[1] + im]
        second = list(more) if r == 0 else [second[0] + more[0], second[1] + more[1]]
    row = lax.broadcasted_iota(jnp.int32, (256, 128), 0)
    grid[0, :256, :] = first[0]
    grid[1, :256, :] = jnp.where(row == 0, nyquist, first[1])
    grid[0, 256:, :] = second[0]
    grid[1, 256:, :] = second[1]
    eight_rows(out, grid, 0)
    for d, block in enumerate((i0, i1, i2, i3)):
        image[pl.ds(aligned(from_of(idx, d)[0], 256), 256), :] = block[...]
    fetch.wait(2)
    spectrum = by_left(w[0], w[1], image[...])
    grid[0] = spectrum[:512]
    grid[1] = spectrum[512:]
    eight_rows(out, grid, 2)


def unpack_rows(idx, re, im, tail):
    rows = lax.broadcasted_iota(jnp.int32, re.shape, 0)
    first = (idx[0] + idx[1]) == 0
    nyquist = jnp.where(first, im[0:1, :], 0.0)
    tail_rows = lax.broadcasted_iota(jnp.int32, (tail, re.shape[1]), 0)
    extra = jnp.where(tail_rows == 0, nyquist, 0.0)
    im = jnp.where((rows == 0) & first, 0.0, im)
    return jnp.concatenate([re, extra], 0), jnp.concatenate([im, jnp.zeros_like(extra)], 0)


def repack_rows(idx, re, im):
    first = (idx[0] + idx[1]) == 0
    rows = lax.broadcasted_iota(jnp.int32, (64, re.shape[1]), 0)
    return re[:64], jnp.where((rows == 0) & first, re[64:65, :], im[:64])


def row_transform(idx, blocks, first, mats, tw, grid):
    for at in range(8):
        grid[:, :, 128 * at : 128 * at + 128] = blocks[at, first : first + 2]
    re, im = unpack_rows(idx, grid[0], grid[1], 8)
    quarters = [(re[:, q * 256 : q * 256 + 256], im[:, q * 256 : q * 256 + 256]) for q in range(4)]
    sum02 = [quarters[0][p] + quarters[2][p] for p in range(2)]
    dif02 = [quarters[0][p] - quarters[2][p] for p in range(2)]
    sum13 = [quarters[1][p] + quarters[3][p] for p in range(2)]
    dif13 = [quarters[1][p] - quarters[3][p] for p in range(2)]
    step = turned(dif13[0], dif13[1], -1)
    parts = [
        (sum02[0] + sum13[0], sum02[1] + sum13[1]),
        (dif02[0] + step[0], dif02[1] + step[1]),
        (sum02[0] - sum13[0], sum02[1] - sum13[1]),
        (dif02[0] - step[0], dif02[1] - step[1]),
    ]
    for r in range(1, 4):
        parts[r] = times(parts[r][0], parts[r][1], tw[r : r + 1, :], -tw[4 + r : 5 + r, :])
    return dft_right(
        jnp.concatenate([p[0] for p in parts], 0),
        jnp.concatenate([p[1] for p in parts], 0),
        mats,
        -1.0,
    )


def blur_kernel(idx, blocks, f_far, tw_far, out, spectrum, grid, f, tw, sems):
    fetch = Fetch(sems, (tw_far, tw), (f_far, f))
    fetch.wait(0)
    fetch.wait(1)
    mats = mats_of(f)
    scene_re, scene_im = row_transform(idx, blocks, 2, mats, tw, grid)
    spectrum[0] = scene_re
    spectrum[1] = scene_im
    re, im = row_transform(idx, blocks, 0, mats, tw, grid)
    re, im = times(re, im, scene_re, scene_im)
    mats = tuple(m[:, :128] for m in mats)
    re, im = dft_right(re, im, mats, 1.0)
    sum_re, sum_im = re[:72], im[:72]
    for r in range(1, 4):
        add = times(
            re[r * 72 : r * 72 + 72],
            im[r * 72 : r * 72 + 72],
            tw[8 + r : 9 + r, :128],
            tw[12 + r : 13 + r, :128],
        )
        sum_re = sum_re + add[0]
        sum_im = sum_im + add[1]
    re, im = repack_rows(idx, sum_re, sum_im)
    out[0] = re
    out[1] = im


def moved_lanes(x, e, lanes):
    if e == 0:
        return x
    rolled = pltpu.roll(x, (-e) % 128, 1)
    return jnp.where(lanes == (127 if e > 0 else 0), 0.0, rolled)


def moved_rows(x, a):
    if a == 0:
        return x
    return pltpu.roll(x, (-a) % x.shape[0], 0)


ROWS = 144


def net_kernel(pixel_count, idx, w1, b1, w2, *refs):
    blocks = refs[:2]
    v, strip, edge, g_out, sums_out = refs[2:7]
    grid, win_taps, g_taps, hidden, sums, acc = refs[7:]
    for d, e in relations:
        s, c = from_of(idx, d, e)
        at = 2 * s + c
        grid[pl.ds(aligned(at, 64), 64), :] = blocks[e][d, 0]
        grid[pl.ds(aligned(at + 8, 64), 64), :] = blocks[e][d, 1]
    target = jnp.where(
        idx[1] == 0,
        jnp.concatenate([edge[...], strip[0:136, :]], 0),
        jnp.concatenate([strip[120:256, :], edge[...]], 0),
    )
    rows = lax.broadcasted_iota(jnp.int32, (ROWS, 128), 0)
    lanes = lax.broadcasted_iota(jnp.int32, (ROWS, 128), 1)
    row_global = rows + (2 * idx[0] + idx[1]) * 128 - 8
    inside = (row_global >= 0) & (row_global < N)
    window = jnp.where(inside, by_left(v[0], v[1], grid[...]), 0.0)
    for e in (-1, 0, 1):
        side = moved_lanes(window, e, lanes)
        for a in (-1, 0, 1):
            win_taps[3 * (a + 1) + e + 1] = moved_rows(side, a)
    step = 24
    for k in range(ROWS // step):
        part = pl.ds(k * step, step)

        def forward(c, total, part=part):
            pre = w1[c, 0] * win_taps[0, part, :]
            for t in range(1, 9):
                pre = pre + w1[c, t] * win_taps[t, part, :]
            hid = jnp.maximum(pre + b1[c], 0.0)
            hidden[c, part, :] = hid
            return tuple(total[t] + w2[t, c] * hid for t in range(9))

        total = lax.fori_loop(
            0, 32, forward, tuple(jnp.zeros((step, 128), F32) for _ in range(9)), unroll=4
        )
        for t in range(9):
            sums[t, part, :] = total[t]
    restored = window
    for e in (-1, 0, 1):
        side = None
        for a in (-1, 0, 1):
            part = moved_rows(jnp.where(inside, sums[3 * (a + 1) + e + 1], 0.0), a)
            side = part if side is None else side + part
        restored = restored + moved_lanes(side, e, lanes)
    residual = jnp.where(inside, restored - target, 0.0)
    own = (rows >= 8) & (rows < 136)
    own_residual = jnp.where(own, residual, 0.0)
    loss = jnp.sum(own_residual * own_residual, 0, keepdims=True)
    g_restored = (2.0 / pixel_count) * residual
    for e in (-1, 0, 1):
        side = moved_lanes(g_restored, -e, lanes)
        for a in (-1, 0, 1):
            g_taps[3 * (a + 1) + e + 1] = jnp.where(inside, moved_rows(side, -a), 0.0)
    acc[...] = jnp.zeros_like(acc)

    def folded(x):
        total = x[:8]
        for row in range(8, x.shape[0], 8):
            total = total + x[row : row + 8]
        return total

    for start, step, mine in [(0, 8, False)] + [(8 + 32 * k, 32, True) for k in range(4)] + [
        (136, 8, False)
    ]:
        part = pl.ds(start, step)

        def backward(c, total, part=part, step=step, mine=mine):
            hid = hidden[c, part, :]
            gh = w2[0, c] * g_taps[0, part, :]
            for t in range(1, 9):
                gh = gh + w2[t, c] * g_taps[t, part, :]
            gp = jnp.where(hid > 0.0, gh, 0.0)
            if mine:
                for t in range(9):
                    acc[c, t] += folded(gp * win_taps[t, part, :])
                    acc[c, 9 + t] += folded(hid * g_taps[t, part, :])
                acc[c, 18] += folded(gp)
            return tuple(total[t] + w1[c, t] * gp for t in range(9))

        total = lax.fori_loop(
            0, 32, backward, tuple(jnp.zeros((step, 128), F32) for _ in range(9)), unroll=4
        )
        for t in range(9):
            sums[t, part, :] = total[t]
    g_window = g_restored
    for e in (-1, 0, 1):
        side = None
        for a in (-1, 0, 1):
            part = moved_rows(sums[3 * (a + 1) + e + 1], -a)
            side = part if side is None else side + part
        g_window = g_window + moved_lanes(side, -e, lanes)
    g_out[...] = g_window[8:136]
    for c in range(32):
        sums_out[c, 0:19, :] = jnp.sum(acc[c], 1)
        sums_out[c, 19:24, :] = jnp.broadcast_to(loss, (5, 128))


def otf_grad_kernel(idx, *refs):
    blocks = refs[:2]
    w, f_far, tw_far, spectrum, out, window, grid, f, tw, sems = refs[2:]
    fetch = Fetch(sems, (f_far, f), (tw_far, tw))
    for d, e in relations:
        s, c = from_of(idx, d, e)
        window[pl.ds(aligned(2 * s + c, 128), 128), :] = blocks[e][d]
    packed = by_left(w[0], w[1], window[...])
    fetch.wait(0)
    fetch.wait(1)
    re, im = unpack_rows(idx, packed[:64], packed[64:], 8)
    res, ims = [re], [im]
    for r in range(1, 4):
        a, b = times(re, im, tw[8 + r : 9 + r, :128], -tw[12 + r : 13 + r, :128])
        res.append(a)
        ims.append(b)
    mats = mats_of(f)
    top = tuple(m[:128, :] for m in mats)
    re, im = dft_right(jnp.concatenate(res, 0), jnp.concatenate(ims, 0), top, -1.0)
    re, im = times(re, im, spectrum[0], -spectrum[1])
    re, im = dft_right(re, im, mats, 1.0)
    parts = []
    for r in range(4):
        a, b = re[r * 72 : r * 72 + 72], im[r * 72 : r * 72 + 72]
        if r:
            a, b = times(a, b, tw[r : r + 1, :], tw[4 + r : 5 + r, :])
        parts.append((a, b))
    for q in range(4):
        a, b = parts[0]
        for r in range(1, 4):
            more = turned(parts[r][0], parts[r][1], q * r)
            a = a + more[0]
            b = b + more[1]
        a, b = repack_rows(idx, a, b)
        grid[0, :, q * 256 : q * 256 + 256] = a
        grid[1, :, q * 256 : q * 256 + 256] = b
    eight_columns(out, grid)


def psf_grad_kernel(idx, blocks, far, f_far, tw_far, small, o0, o1, o2, o3, grid, f, tw, sems):
    fetch = Fetch(sems, (f_far, f), (tw_far, tw))
    for c in range(2):
        for s in range(4):
            grid[:, 128 * s + 64 * c : 128 * s + 64 * c + 64, :] = blocks[4 * c + s]
    row = lax.broadcasted_iota(jnp.int32, (256, 128), 0)
    zero_row = row == 0
    low_re, low_im = grid[0, :256, :], grid[1, :256, :]
    nyquist = jnp.where(zero_row, 0.5 * low_im, 0.0)
    low_re = jnp.where(zero_row, 0.5 * low_re, low_re)
    low_im = jnp.where(zero_row, 0.0, low_im)
    high = (grid[0, 256:, :], grid[1, 256:, :])
    fetch.wait(1)
    twists = [(tw[:, r : r + 1], tw[:, 4 + r : 5 + r]) for r in range(4)]
    res, ims = [], []
    for r in range(4):
        add = turned(high[0], high[1], r)
        re, im = low_re + add[0], low_im + add[1]
        if r:
            re, im = times(re, im, twists[r][0], twists[r][1])
        re = re + nyquist if r % 2 == 0 else re - nyquist
        res.append(re)
        ims.append(im)
    fetch.wait(0)
    mats = mats_of(f)
    g_psf = 2.0 * (
        by_left(mats[0], mats[1], jnp.concatenate(res, 1))
        - by_left(mats[2], mats[3], jnp.concatenate(ims, 1))
    )
    re, im = dft_left(g_psf * far[0], g_psf * far[1], mats, 1.0)
    first, second = None, None
    for r in range(4):
        a, b = re[:, r * 128 : r * 128 + 128], im[:, r * 128 : r * 128 + 128]
        if r:
            a, b = times(a, b, twists[r][0], twists[r][1])
        more = turned(a, b, r)
        first = [a, b] if r == 0 else [first[0] + a, first[1] + b]
        second = list(more) if r == 0 else [second[0] + more[0], second[1] + more[1]]
    for p in range(2):
        grid[p, :256, :] = first[p]
        grid[p, 256:, :] = second[p]
    for d, out in enumerate((o0, o1, o2, o3)):
        out[:, 0:128, :] = grid[:, pl.ds(aligned(spot_of(idx, d)[0], 128), 128), :]
        out[0, 128:136, :] = small[...]
        out[1, 128:136, :] = jnp.zeros((8, 128), F32)


def mask_grad_kernel(scale, idx, ids, got, *refs):
    b0, b1, b2, b3, m_far, pupil, keep, send, grid, whole, m, sems = refs
    fetch = Fetch(sems, (m_far, m))
    small = None
    for d, block in enumerate((b0, b1, b2, b3)):
        grid[:, :, pl.ds(aligned(from_of(idx, d)[0], 128), 128)] = block[:, 0:128, :]
        part = block[0, 128:136, :]
        small = part if small is None else small + part
    fetch.wait(0)
    re, im = dft_right(grid[0], grid[1], mats_of(m), 1.0)
    cols = lax.broadcasted_iota(jnp.int32, (128, 512), 1)
    factor = ratio_of(jnp.where(idx[2] == 1, ids[1], got[1]))[0:1, 0:1] * scale
    factor = jnp.where((cols & idx[1]) == 1, -factor, factor)
    whole[...] = factor * (im * pupil[0] - re * pupil[1])
    both = jnp.concatenate([small, small], 1)
    keep[0:128, :] = whole[:, pl.ds(aligned(idx[1], 256), 256)]
    send[0:128, :] = whole[:, pl.ds(aligned(1 - idx[1], 256), 256)]
    keep[128:136, :] = both
    send[128:136, :] = both


def cut_kernel(ways, idx, keep, other, *refs):
    outs = refs[:ways]
    whole = refs[ways]
    whole[...] = keep[...] + other[...]
    piece = 128 // ways
    for d, out in enumerate(outs):
        to = lax.rem(idx[3] + d, ways)
        out[0:piece, :] = whole[pl.ds(aligned(to, piece), piece), :]
        out[piece : piece + 8, :] = whole[128:136, :]


def home_kernel(ways, idx, near, far, out):
    piece = 128 // ways
    at_home = idx[0] == 1 + idx[1]
    central = (idx[0] == 1) | (idx[0] == 2)
    out[0:256, :] = jnp.zeros((256, 256), F32)
    out[768:1024, :] = jnp.zeros((256, 256), F32)
    for y in range(ways):
        for s in range(4):
            row = 256 + 128 * s + piece * y
            block = jnp.where(at_home, near[4 * y + s], far[4 * y + s])
            out[row : row + piece, :] = jnp.where(central, block, 0.0)


def on_device(lay, phase_mask, height_offsets, sample_ids, wave_ids, scene, w1, b1, w2):
    con = constants()
    s = lax.axis_index("sp")
    c = lax.axis_index("core")
    y = lax.axis_index("y")
    owner = c == lax.axis_index("grp")
    pixel_count = float(lay.dp * N * 128)
    scale_psf = 1.0 / (N * N * pupil_count(N))
    idx = jnp.stack([s, c, owner.astype(jnp.int32), y]).astype(jnp.int32)

    def swap(g, zh, y, c, s):
        return (g, zh, y, 1 - c, s)

    def along_sp(blocks):
        return [blocks[0]] + [
            lay.move(blocks[d], lambda g, zh, y, c, s, d=d: (g, zh, y, c, s + d))
            for d in (1, 2, 3)
        ]

    def to_eight(blocks):
        return lax.all_to_all(blocks, ("core", "sp"), 0, 0, tiled=True)

    def gathered(block):
        near = jnp.stack(along_sp([block] * 4))
        return near, lay.move(near, swap)

    ids = jnp.concatenate([sample_ids, wave_ids])
    got = lay.move(ids, swap)
    grabbed = lax.dynamic_slice(height_offsets, (ids[0], 256, 0), (1, 512, 256))[0]
    ratio = 550.0 / (400.0 + 10.0 * ids[1].astype(F32))
    phases = ratio * (phase_mask[256:768] + 0.1 * grabbed.astype(F32))

    mine, *sent = call(
        phase_kernel,
        (idx, phases),
        (0,),
        [(128, 256)] * 4,
    )
    tables = ({1: 0, 2: 3}, {1: 2, 2: 1}, {1: 3, 2: 0})
    pieces = [mine] + [
        lay.move(
            block,
            lambda g, zh, y, c, s, to=to: (
                (g, zh, y, c, to[s]) if s in to and c == g else None
            ),
        )
        for block, to in zip(sent, tables)
    ]
    pieces += [
        lay.move(block, lambda g, zh, y, c, s: (g, zh, y, 1 - c, s) if c == g else None)
        for block in pieces
    ]

    other = lay.move(
        jnp.concatenate(
            [lax.dynamic_slice_in_dim(scene[0], 512 * (1 - c), 512, 1), scene[0, :, 256:384]], 1
        ),
        swap,
    )
    *columns, strip, edge = call(
        scene_kernel,
        (idx, scene, other),
        (0,),
        [(256, 128)] * 4 + [(256, 128), (8, 128)],
    )
    columns = along_sp(columns)
    edge = lay.move(edge, lambda g, zh, y, c, s: (g, zh, y, c, s + 1 - 2 * c))

    unpack = lax.dynamic_slice_in_dim(jnp.asarray(con["unpack"]), 128 * (2 * s + c), ROWS, 1)
    pack = jnp.asarray(con["pack"]).reshape(4, 512, N)
    pack_rows = lax.dynamic_slice_in_dim(pack, 64 * (2 * s + c), 64, 1).reshape(2, 128, N)
    *field, pupil = call(
        pupil_kernel,
        (idx, *pieces, con["m"]),
        (0,),
        [(2, 128, 128)] * 4 + [(2, 128, 512)],
        [pltpu.VMEM((2, 128, 512), F32), bf16_buffer(4, 512, 512), fetch_sems(1)],
        (9,),
    )
    field = along_sp(field)
    far, parts = call(
        functools.partial(optics_kernel, scale_psf),
        (idx, *field, *columns, con["f"], con["tw_col"], con["pack"]),
        (0,),
        [(2, 256, 512), (8, 4, 64, 128)],
        [
            pltpu.VMEM((2, 512, 128), F32),
            pltpu.VMEM((N, 128), F32),
            bf16_buffer(4, 256, 256),
            pltpu.VMEM((256, 8), F32),
            bf16_buffer(2, N, N),
            fetch_sems(3),
        ],
        (9, 10, 11),
    )
    half_window, spectrum = call(
        blur_kernel,
        (idx, to_eight(parts), con["f"], con["tw_row"]),
        (0,),
        [(2, 288, 256), (2, 64, 128)][::-1],
        [
            pltpu.VMEM((2, 64, N), F32),
            bf16_buffer(4, 256, 256),
            pltpu.VMEM((16, 256), F32),
            fetch_sems(2),
        ],
        (2, 3),
    )
    window_parts = gathered(half_window)
    g_window, sums = call(
        functools.partial(net_kernel, pixel_count),
        (idx, w1, b1, w2, *window_parts, unpack, strip, edge),
        (0, 1, 2, 3),
        [(128, 128), (32, 24, 128)],
        [
            pltpu.VMEM((N, 128), F32),
            pltpu.VMEM((9, ROWS, 128), F32),
            pltpu.VMEM((9, ROWS, 128), F32),
            pltpu.VMEM((32, ROWS, 128), F32),
            pltpu.VMEM((9, ROWS, 128), F32),
            pltpu.VMEM((32, 19, 8, 128), F32),
        ],
    )
    small = jnp.pad(jnp.sum(sums, 2).reshape(6, 128), ((0, 2), (0, 0)))
    g_parts = gathered(g_window)
    (otf_grad,) = call(
        otf_grad_kernel,
        (idx, *g_parts, pack_rows, con["f"], con["tw_row"], spectrum),
        (0,),
        [(8, 2, 64, 128)],
        [
            pltpu.VMEM((N, 128), F32),
            pltpu.VMEM((2, 64, N), F32),
            bf16_buffer(4, 256, 256),
            pltpu.VMEM((16, 256), F32),
            fetch_sems(2),
        ],
        (4, 5),
    )
    otf_grad = to_eight(otf_grad)
    field_grad = along_sp(
        call(
            psf_grad_kernel,
            (idx, otf_grad, far, con["f"], con["tw_col"], small),
            (0,),
            [(2, 136, 128)] * 4,
            [
                pltpu.VMEM((2, 512, 128), F32),
                bf16_buffer(4, 256, 256),
                pltpu.VMEM((256, 8), F32),
                fetch_sems(2),
            ],
            (3, 4),
        )
    )
    keep, send = call(
        functools.partial(mask_grad_kernel, 2.0 * scale_psf),
        (idx, ids, got, *field_grad, con["m"], pupil),
        (0, 1, 2),
        [(136, 256)] * 2,
        [
            pltpu.VMEM((2, 128, 512), F32),
            pltpu.VMEM((128, 512), F32),
            bf16_buffer(4, 512, 512),
            fetch_sems(1),
        ],
        (7,),
    )

    piece = 128 // lay.y
    blocks = call(
        functools.partial(cut_kernel, lay.y),
        (idx, keep, lay.move(send, swap)),
        (0,),
        [(piece + 8, 256)] * lay.y,
        [pltpu.VMEM((136, 256), F32)],
    )
    total = blocks[0]
    for d in range(1, lay.y):
        total = total + lay.move(
            blocks[d], lambda g, zh, y, c, s, d=d: (g, zh, y + d, c, s)
        )
    total = total + lay.move(total, lambda g, zh, y, c, s: (1 - g, zh, y, c, s))
    part = total
    for d in range(1, lay.zh):
        total = total + lay.move(part, lambda g, zh, y, c, s, d=d: (g, zh + d, y, c, s))
    small = total[piece:, :128].reshape(-1)
    total = total[:piece]
    ways = 4 * lay.y
    near = lax.all_to_all(
        jnp.broadcast_to(total, (ways, piece, 256)), ("y", "sp"), 0, 0, tiled=True
    )
    far = lay.move(near, lambda g, zh, y, c, s: (g, zh, y, 1 - c, s) if s == 1 + c else None)
    (mask_grad,) = call(functools.partial(home_kernel, lay.y), (idx, near, far), (0,), [(N, 256)])
    table = small[:768].reshape(32, 24)
    return (
        mask_grad,
        table[:, :9],
        table[:, 18],
        table[:, 9:18].T,
        table[0, 19] / pixel_count,
    )


def solution(mesh):
    lay = Layout(mesh)
    images = ("zh", "y", "core")
    placed = (
        P(None, "sp"),
        P(None, None, "sp"),
        P(images),
        P(images),
        P(images, "sp", None),
        P(),
        P(),
        P(),
    )
    return jax.shard_map(
        functools.partial(on_device, lay),
        mesh=lay.mesh,
        in_specs=placed,
        out_specs=(P(None, "sp"), P(), P(), P(), P()),
        check_vma=False,
    )
```

```python
import functools
import itertools

import jax
import jax.numpy as jnp
import ml_dtypes
import numpy as np
from jax import lax
from jax.experimental import pallas as pl
from jax.experimental.pallas import tpu as pltpu
from jax.sharding import PartitionSpec as P

N = 1024
F32 = jnp.float32
BF16 = jnp.bfloat16
AXES = ("grp", "zh", "y", "core", "sp")
taps = ((-1, -1), (-1, 0), (-1, 1), (0, -1), (0, 0), (0, 1), (1, -1), (1, 0), (1, 1))


def halves(matrix):
    high = matrix.astype(ml_dtypes.bfloat16)
    low = (matrix - high.astype(np.float64)).astype(ml_dtypes.bfloat16)
    return high, low


def trig(rows, cols, length):
    angle = 2.0 * np.pi * (np.outer(rows, cols) % length) / length
    return np.cos(angle), np.sin(angle)


@functools.lru_cache(None)
def constants():
    half = np.arange(512)
    quarter = np.arange(256)
    fours = np.arange(4)
    spread = (np.arange(4)[:, None] * 256 + np.arange(128)).reshape(-1)
    cos_m, sin_m = trig(half, spread, N)
    cos_f, sin_f = trig(quarter, quarter, 256)
    cos_w, sin_w = trig(half, np.arange(N), N)
    sin_w = -sin_w
    sin_w[0] = (-1.0) ** np.arange(N)
    packed = np.concatenate([cos_w, sin_w])
    weight = np.full((N,), 2.0)
    weight[0] = 1.0
    weight[512] = 1.0
    unpack = (packed * weight[:, None]).T / (N * N)
    blocks = [np.r_[64 * q : 64 * q + 64, 512 + 64 * q : 576 + 64 * q] for q in range(8)]
    by_at = np.concatenate([blocks[2 * s + c] for c in range(2) for s in range(4)])
    near = packed[np.concatenate(blocks), 256:384].reshape(8, 128, 128).transpose(0, 2, 1)
    cos_e, sin_e = trig([0, 1], half, 8)
    cos_t, sin_t = trig(quarter, fours, N)
    return {
        "m": np.stack(halves(cos_m) + halves(sin_m)),
        "m_back": np.stack(halves(cos_m.T) + halves(sin_m.T)),
        "f": np.stack(halves(cos_f) + halves(sin_f)),
        "pack": np.stack(halves(packed)),
        "window": np.stack(halves(unpack[256:384, by_at].T)),
        "near": np.stack(halves(near)),
        "eighth": np.stack([cos_e, sin_e], 1).astype(np.float32),
        "tw_col": np.concatenate([cos_t, sin_t], 1).astype(np.float32),
        "tw_row": np.concatenate([cos_t, sin_t], 1).T.astype(np.float32).copy(),
    }


def pupil_count(size_grid):
    coords = np.arange(size_grid) * 2 - size_grid + 1
    inside = (coords[:, None] ** 2 + coords[None, :] ** 2) * 4 <= size_grid * size_grid
    return float(np.sum(inside))


class Layout:
    def __init__(self, mesh):
        self.dp = mesh.shape["dp"]
        self.y = min(4, self.dp // 2)
        self.zh = self.dp // (2 * self.y)
        self.sp = mesh.shape["sp"]
        self.sizes = (2, self.zh, self.y, 2, self.sp)
        self.mesh = jax.sharding.Mesh(mesh.devices.reshape(self.sizes), AXES)

    def move(self, x, where):
        pairs = []
        for spot in itertools.product(*[range(n) for n in self.sizes]):
            goal = where(*spot)
            if goal is not None:
                pairs.append((self.flat(spot), self.flat(goal)))
        return lax.ppermute(x, AXES, pairs)

    def flat(self, spot):
        at = 0
        for place, size in zip(spot, self.sizes):
            at = at * size + place % size
        return at


def split(x):
    high = x.astype(BF16)
    return high, (x - high.astype(F32)).astype(BF16)


def dot(a, b):
    return lax.dot_general(a, b, (((1,), (0,)), ((), ())), preferred_element_type=F32)


def by_right(x, w_high, w_low):
    high, low = split(x)
    return dot(high, w_high) + (dot(high, w_low) + dot(low, w_high))


def by_left(w_high, w_low, x):
    high, low = split(x)
    return dot(w_high, high) + (dot(w_low, high) + dot(w_high, low))


def dft_right(re, im, mats, sign):
    rows = re.shape[0]
    both = jnp.concatenate([re, im], 0)
    by_cos = by_right(both, mats[0], mats[1])
    by_sin = by_right(both, mats[2], mats[3]) * sign
    return by_cos[:rows] - by_sin[rows:], by_cos[rows:] + by_sin[:rows]


def dft_left(re, im, mats, sign):
    cols = re.shape[1]
    both = jnp.concatenate([re, im], 1)
    by_cos = by_left(mats[0], mats[1], both)
    by_sin = by_left(mats[2], mats[3], both) * sign
    return by_cos[:, :cols] - by_sin[:, cols:], by_cos[:, cols:] + by_sin[:, :cols]


def turned(re, im, quarter_turns):
    quarter_turns %= 4
    if quarter_turns == 0:
        return re, im
    if quarter_turns == 1:
        return -im, re
    if quarter_turns == 2:
        return -re, -im
    return im, -re


def times(re, im, cos, sin):
    return re * cos - im * sin, re * sin + im * cos


def cos_sin(x):
    n = jnp.floor(x * (2.0 / np.pi) + 0.5)
    r = x - n * 1.5707963109016418
    r = r - n * 1.5893254712295857e-8
    q = n.astype(jnp.int32) & 3
    z = r * r
    sn = r + r * z * (-1.6666654611e-1 + z * (8.3321608736e-3 + z * -1.9515295891e-4))
    cs = 1.0 - 0.5 * z + z * z * (
        4.166664568298827e-2 + z * (-1.388731625493765e-3 + z * 2.443315711809948e-5)
    )
    odd = (q & 1) == 1
    c0 = jnp.where(odd, sn, cs)
    s0 = jnp.where(odd, cs, sn)
    cos = jnp.where((q == 1) | (q == 2), -c0, c0)
    sin = jnp.where(q >= 2, -s0, s0)
    return cos, sin


def spot_of(idx, d, e=0):
    return lax.rem(idx[0] + d, 4), lax.rem(idx[1] + e, 2)


def from_of(idx, d, e=0):
    return lax.rem(idx[0] + 4 - d, 4), lax.rem(idx[1] + 2 - e, 2)


def aligned(x, by):
    return pl.multiple_of(x * by, by)


def call(kernel, operands, in_smem, outs, scratch=(), apart=()):
    specs = []
    for at in range(len(operands)):
        space = pltpu.SMEM if at in in_smem else pltpu.VMEM
        specs.append(pl.BlockSpec(memory_space=pltpu.HBM if at in apart else space))
    return pl.pallas_call(
        kernel,
        out_shape=[jax.ShapeDtypeStruct(shape, F32) for shape in outs],
        in_specs=specs,
        out_specs=[pl.BlockSpec(memory_space=pltpu.VMEM) for _ in outs],
        scratch_shapes=list(scratch),
        compiler_params=pltpu.CompilerParams(vmem_limit_bytes=20 * 1024 * 1024),
    )(*operands)


relations = [(d, e) for e in range(2) for d in range(4)]


class Fetch:
    def __init__(self, sems, *pairs):
        self.copies = [
            pltpu.make_async_copy(src, dst, sems.at[at]) for at, (src, dst) in enumerate(pairs)
        ]
        for copy in self.copies:
            copy.start()

    def wait(self, at):
        self.copies[at].wait()


def bf16_buffer(*shape):
    return pltpu.VMEM(shape, BF16)


def fetch_sems(count):
    return pltpu.SemaphoreType.DMA((count,))


def ratio_of(wave):
    return 550.0 / (400.0 + 10.0 * jnp.full((8, 128), wave, jnp.int32).astype(F32))


def mats_of(ref):
    return ref[0], ref[1], ref[2], ref[3]


def phase_kernel(idx, phases, own0, own1, sent0, sent1, grid):
    grid[...] = jnp.transpose(phases[...])
    kept = aligned(jnp.where(idx[0] == 1, 1, 0), 128)
    given = aligned(jnp.where(idx[0] == 1, 0, 1), 128)
    own0[...] = grid[pl.ds(kept, 128), 0:256]
    own1[...] = grid[pl.ds(kept, 128), 256:512]
    sent0[...] = grid[pl.ds(given, 128), 0:256]
    sent1[...] = grid[pl.ds(given, 128), 256:512]


def scene_kernel(idx, scene, other, w_far, out, strip, edge, image, grid, w, sems):
    fetch = Fetch(sems, (w_far, w))
    owner = idx[2] == 1
    c = idx[1]
    rows = jnp.where(
        owner,
        scene[0, pl.ds(aligned(15 * c, 8), 136), :],
        other[...],
    )
    strip[...] = rows[:, 256:384]
    edge[...] = jnp.where(c == 0, rows[0:8, 256:384], rows[128:136, 256:384])
    image[...] = jnp.transpose(jnp.where(c == 0, rows[0:128], rows[8:136]))
    fetch.wait(0)
    spectrum = by_left(w[0], w[1], image[...])
    grid[0] = spectrum[:512]
    grid[1] = spectrum[512:]
    eight_rows(out, grid)


def pupil_kernel(idx, *refs):
    m_far, e, o0, o1, o2, o3, pupil, grid, m, sems = refs[8:]
    fetch = Fetch(sems, (m_far, m))
    s = idx[0]
    c = idx[1]
    owner = idx[2] == 1
    central = (s == 1) | (s == 2)
    own = jnp.concatenate([refs[0][...], refs[1][...]], 1)
    got = jnp.concatenate([refs[2][...], refs[3][...]], 1)
    own_far = jnp.concatenate([refs[4][...], refs[5][...]], 1)
    got_far = jnp.concatenate([refs[6][...], refs[7][...]], 1)
    phase = jnp.where(central, jnp.where(owner, own, own_far), jnp.where(owner, got, got_far))
    rows = lax.broadcasted_iota(jnp.int32, (128, 512), 0) + s * 128
    cols = lax.broadcasted_iota(jnp.int32, (128, 512), 1)
    across = (rows + 256) * 2 - N + 1
    down = (cols + 256) * 2 - N + 1
    inside = (down * down + across * across) * 4 <= N * N
    cos, sin = cos_sin(phase)
    re = jnp.where(inside, cos, 0.0)
    im = jnp.where(inside, sin, 0.0)
    pupil[0] = re
    pupil[1] = im
    re, im = times(re, im, e[c, 0:1, :], -e[c, 1:2, :])
    fetch.wait(0)
    out_re, out_im = dft_right(re, im, mats_of(m), -1.0)
    grid[0] = out_re
    grid[1] = out_im
    for d, out in enumerate((o0, o1, o2, o3)):
        to = spot_of(idx, d)[0]
        out[...] = grid[:, :, pl.ds(aligned(to, 128), 128)]


def eight_rows(out, grid):
    for c in range(2):
        for s in range(4):
            row = 128 * s + 64 * c
            out[4 * c + s, 0:2] = grid[:, row : row + 64, :]


def eight_columns(out, grid):
    for c in range(2):
        for s in range(4):
            col = 128 * (2 * s + c)
            out[4 * c + s] = grid[:, :, col : col + 128]


def optics_kernel(scale, idx, b0, b1, b2, b3, scene, *refs):
    f_far, tw_far, far, out, grid, f, tw, sems = refs
    fetch = Fetch(sems, (tw_far, tw), (f_far, f))
    for d, block in enumerate((b0, b1, b2, b3)):
        grid[:, pl.ds(aligned(from_of(idx, d)[0], 128), 128), :] = block[...]
    low = (grid[0, :256, :], grid[1, :256, :])
    high = (grid[0, 256:, :], grid[1, 256:, :])
    fetch.wait(0)
    twists = [(tw[:, r : r + 1], tw[:, 4 + r : 5 + r]) for r in range(4)]
    res, ims = [], []
    for r in range(4):
        add = turned(high[0], high[1], -r)
        re, im = low[0] + add[0], low[1] + add[1]
        if r:
            re, im = times(re, im, twists[r][0], -twists[r][1])
        res.append(re)
        ims.append(im)
    fetch.wait(1)
    mats = mats_of(f)
    far_re, far_im = dft_left(
        jnp.concatenate(res, 1), jnp.concatenate(ims, 1), mats, -1.0
    )
    far[0] = far_re
    far[1] = far_im
    psf = scale * (far_re * far_re + far_im * far_im)
    psf_high, psf_low = split(psf)
    z_re = dot(mats[0], psf_high) + (dot(mats[1], psf_high) + dot(mats[0], psf_low))
    z_im = -(dot(mats[2], psf_high) + (dot(mats[3], psf_high) + dot(mats[2], psf_low)))
    first = [None, None]
    second = [None, None]
    nyquist = None
    for r in range(4):
        re = z_re[:, r * 128 : r * 128 + 128]
        im = z_im[:, r * 128 : r * 128 + 128]
        top = re[0:1, :]
        nyquist = top if r == 0 else (nyquist + top if r % 2 == 0 else nyquist - top)
        if r:
            re, im = times(re, im, twists[r][0], -twists[r][1])
        more = turned(re, im, -r)
        first = [re, im] if r == 0 else [first[0] + re, first[1] + im]
        second = list(more) if r == 0 else [second[0] + more[0], second[1] + more[1]]
    row = lax.broadcasted_iota(jnp.int32, (256, 128), 0)
    grid[0, :256, :] = first[0]
    grid[1, :256, :] = jnp.where(row == 0, nyquist, first[1])
    grid[0, 256:, :] = second[0]
    grid[1, 256:, :] = second[1]
    eight_rows(out, grid)
    for at in range(8):
        out[at, 2:4] = scene[at]


def unpack_rows(idx, re, im, tail):
    rows = lax.broadcasted_iota(jnp.int32, re.shape, 0)
    first = (idx[0] + idx[1]) == 0
    nyquist = jnp.where(first, im[0:1, :], 0.0)
    tail_rows = lax.broadcasted_iota(jnp.int32, (tail, re.shape[1]), 0)
    extra = jnp.where(tail_rows == 0, nyquist, 0.0)
    im = jnp.where((rows == 0) & first, 0.0, im)
    return jnp.concatenate([re, extra], 0), jnp.concatenate([im, jnp.zeros_like(extra)], 0)


def repack_rows(idx, re, im):
    first = (idx[0] + idx[1]) == 0
    rows = lax.broadcasted_iota(jnp.int32, (64, re.shape[1]), 0)
    return re[:64], jnp.where((rows == 0) & first, re[64:65, :], im[:64])


def row_transform(idx, blocks, first, mats, tw, grid):
    for c in range(2):
        for s in range(4):
            col = 128 * (2 * s + c)
            grid[:, :, col : col + 128] = blocks[4 * c + s, first : first + 2]
    return rows_out(idx, grid[0], grid[1], mats, tw)


def rows_back(idx, re, im, mats, tw, grid):
    re, im = dft_right(re, im, mats, 1.0)
    parts = []
    for r in range(4):
        a, b = re[r * 72 : r * 72 + 72], im[r * 72 : r * 72 + 72]
        if r:
            a, b = times(a, b, tw[r : r + 1, :], tw[4 + r : 5 + r, :])
        parts.append((a, b))
    for q in range(4):
        a, b = parts[0]
        for r in range(1, 4):
            more = turned(parts[r][0], parts[r][1], q * r)
            a = a + more[0]
            b = b + more[1]
        a, b = repack_rows(idx, a, b)
        grid[0, :, q * 256 : q * 256 + 256] = a
        grid[1, :, q * 256 : q * 256 + 256] = b


def rows_out(idx, re, im, mats, tw):
    re, im = unpack_rows(idx, re, im, 8)
    quarters = [(re[:, q * 256 : q * 256 + 256], im[:, q * 256 : q * 256 + 256]) for q in range(4)]
    sum02 = [quarters[0][p] + quarters[2][p] for p in range(2)]
    dif02 = [quarters[0][p] - quarters[2][p] for p in range(2)]
    sum13 = [quarters[1][p] + quarters[3][p] for p in range(2)]
    dif13 = [quarters[1][p] - quarters[3][p] for p in range(2)]
    step = turned(dif13[0], dif13[1], -1)
    parts = [
        (sum02[0] + sum13[0], sum02[1] + sum13[1]),
        (dif02[0] + step[0], dif02[1] + step[1]),
        (sum02[0] - sum13[0], sum02[1] - sum13[1]),
        (dif02[0] - step[0], dif02[1] - step[1]),
    ]
    for r in range(1, 4):
        parts[r] = times(parts[r][0], parts[r][1], tw[r : r + 1, :], -tw[4 + r : 5 + r, :])
    return dft_right(
        jnp.concatenate([p[0] for p in parts], 0),
        jnp.concatenate([p[1] for p in parts], 0),
        mats,
        -1.0,
    )


def blur_kernel(idx, blocks, f_far, tw_far, out, spectrum, grid, turned_grid, f, tw, sems):
    fetch = Fetch(sems, (tw_far, tw), (f_far, f))
    fetch.wait(0)
    fetch.wait(1)
    mats = mats_of(f)
    re, im = row_transform(idx, blocks, 2, mats, tw, grid)
    spectrum[0] = re
    spectrum[1] = im
    re, im = row_transform(idx, blocks, 0, mats, tw, grid)
    re, im = times(re, im, spectrum[0], spectrum[1])
    rows_back(idx, re, im, mats, tw, grid)
    both = jnp.transpose(jnp.concatenate([grid[0], grid[1]], 0))
    turned_grid[8 : N + 8, :] = both
    turned_grid[0:8, :] = both[N - 8 :, :]
    turned_grid[N + 8 :, :] = both[:8, :]
    for c in range(2):
        for s in range(4):
            row = 128 * (2 * s + c)
            out[4 * c + s] = turned_grid[row : row + ROWS, :]


def moved_lanes(x, e, lanes):
    if e == 0:
        return x
    rolled = pltpu.roll(x, (-e) % 128, 1)
    return jnp.where(lanes == (127 if e > 0 else 0), 0.0, rolled)


def moved_rows(x, a):
    if a == 0:
        return x
    return pltpu.roll(x, (-a) % x.shape[0], 0)


ROWS = 144


def net_kernel(pixel_count, idx, w1, b1, w2, *refs):
    blocks, v_far, strip, edge, g_out, sums_out = refs[:6]
    win_taps, g_taps, hidden, sums, acc, v, sems = refs[6:]
    fetch = Fetch(sems, (v_far, v))
    target = jnp.where(
        idx[1] == 0,
        jnp.concatenate([edge[...], strip[...]], 0),
        jnp.concatenate([strip[...], edge[...]], 0),
    )
    spectra = jnp.concatenate([blocks[at] for at in range(8)], 1)
    fetch.wait(0)
    rows = lax.broadcasted_iota(jnp.int32, (ROWS, 128), 0)
    lanes = lax.broadcasted_iota(jnp.int32, (ROWS, 128), 1)
    row_global = rows + (2 * idx[0] + idx[1]) * 128 - 8
    inside = (row_global >= 0) & (row_global < N)
    window = jnp.where(inside, by_right(spectra, v[0], v[1]), 0.0)
    for e in (-1, 0, 1):
        side = moved_lanes(window, e, lanes)
        for a in (-1, 0, 1):
            win_taps[3 * (a + 1) + e + 1] = moved_rows(side, a)
    step = 24
    for k in range(ROWS // step):
        part = pl.ds(k * step, step)

        def forward(c, total, part=part):
            pre = w1[c, 0] * win_taps[0, part, :]
            for t in range(1, 9):
                pre = pre + w1[c, t] * win_taps[t, part, :]
            hid = jnp.maximum(pre + b1[c], 0.0)
            hidden[c, part, :] = hid
            return tuple(total[t] + w2[t, c] * hid for t in range(9))

        total = lax.fori_loop(
            0, 32, forward, tuple(jnp.zeros((step, 128), F32) for _ in range(9)), unroll=4
        )
        for t in range(9):
            sums[t, part, :] = total[t]
    restored = window
    for e in (-1, 0, 1):
        side = None
        for a in (-1, 0, 1):
            part = moved_rows(jnp.where(inside, sums[3 * (a + 1) + e + 1], 0.0), a)
            side = part if side is None else side + part
        restored = restored + moved_lanes(side, e, lanes)
    residual = jnp.where(inside, restored - target, 0.0)
    own = (rows >= 8) & (rows < 136)
    own_residual = jnp.where(own, residual, 0.0)
    loss = jnp.sum(own_residual * own_residual, 0, keepdims=True)
    g_restored = (2.0 / pixel_count) * residual
    for e in (-1, 0, 1):
        side = moved_lanes(g_restored, -e, lanes)
        for a in (-1, 0, 1):
            g_taps[3 * (a + 1) + e + 1] = jnp.where(inside, moved_rows(side, -a), 0.0)
    acc[...] = jnp.zeros_like(acc)

    def folded(x):
        total = x[:8]
        for row in range(8, x.shape[0], 8):
            total = total + x[row : row + 8]
        return total

    for start, step, mine in [(0, 8, False)] + [(8 + 32 * k, 32, True) for k in range(4)] + [
        (136, 8, False)
    ]:
        part = pl.ds(start, step)

        def backward(c, total, part=part, step=step, mine=mine):
            hid = hidden[c, part, :]
            gh = w2[0, c] * g_taps[0, part, :]
            for t in range(1, 9):
                gh = gh + w2[t, c] * g_taps[t, part, :]
            gp = jnp.where(hid > 0.0, gh, 0.0)
            if mine:
                for t in range(9):
                    acc[c, t] += folded(gp * win_taps[t, part, :])
                    acc[c, 9 + t] += folded(hid * g_taps[t, part, :])
                acc[c, 18] += folded(gp)
            return tuple(total[t] + w1[c, t] * gp for t in range(9))

        total = lax.fori_loop(
            0, 32, backward, tuple(jnp.zeros((step, 128), F32) for _ in range(9)), unroll=4
        )
        for t in range(9):
            sums[t, part, :] = total[t]
    g_window = g_restored
    for e in (-1, 0, 1):
        side = None
        for a in (-1, 0, 1):
            part = moved_rows(sums[3 * (a + 1) + e + 1], -a)
            side = part if side is None else side + part
        g_window = g_window + moved_lanes(side, -e, lanes)
    g_out[...] = g_window[8:136]
    for c in range(32):
        sums_out[c, 0:19, :] = jnp.sum(acc[c], 1)
        sums_out[c, 19:24, :] = jnp.broadcast_to(loss, (5, 128))


def otf_grad_kernel(idx, *refs):
    blocks = refs[:8]
    w_far, f_far, tw_far, spectrum, out, window, grid, f, tw, w, sems = refs[8:]
    fetch = Fetch(
        sems, (f_far, f), (tw_far, tw), (w_far.at[:, 2 * idx[0] + idx[1]], w)
    )
    for d, e in relations:
        s, c = from_of(idx, d, e)
        window[pl.ds(aligned(2 * s + c, 128), 128), :] = blocks[4 * e + d][...]
    for at in range(3):
        fetch.wait(at)
    packed = jnp.transpose(by_right(window[...], w[0], w[1]))
    mats = mats_of(f)
    re, im = rows_out(idx, packed[:64], packed[64:], mats, tw)
    re, im = times(re, im, spectrum[0], -spectrum[1])
    rows_back(idx, re, im, mats, tw, grid)
    eight_columns(out, grid)


def psf_grad_kernel(idx, blocks, far, f_far, tw_far, small, o0, o1, o2, o3, grid, f, tw, sems):
    fetch = Fetch(sems, (f_far, f), (tw_far, tw))
    for c in range(2):
        for s in range(4):
            grid[:, 128 * s + 64 * c : 128 * s + 64 * c + 64, :] = blocks[4 * c + s]
    row = lax.broadcasted_iota(jnp.int32, (256, 128), 0)
    zero_row = row == 0
    low_re, low_im = grid[0, :256, :], grid[1, :256, :]
    nyquist = jnp.where(zero_row, 0.5 * low_im, 0.0)
    low_re = jnp.where(zero_row, 0.5 * low_re, low_re)
    low_im = jnp.where(zero_row, 0.0, low_im)
    high = (grid[0, 256:, :], grid[1, 256:, :])
    fetch.wait(1)
    twists = [(tw[:, r : r + 1], tw[:, 4 + r : 5 + r]) for r in range(4)]
    res, ims = [], []
    for r in range(4):
        add = turned(high[0], high[1], r)
        re, im = low_re + add[0], low_im + add[1]
        if r:
            re, im = times(re, im, twists[r][0], twists[r][1])
        re = re + nyquist if r % 2 == 0 else re - nyquist
        res.append(re)
        ims.append(im)
    fetch.wait(0)
    mats = mats_of(f)
    g_psf = 2.0 * (
        by_left(mats[0], mats[1], jnp.concatenate(res, 1))
        - by_left(mats[2], mats[3], jnp.concatenate(ims, 1))
    )
    re, im = dft_left(g_psf * far[0], g_psf * far[1], mats, 1.0)
    first, second = None, None
    for r in range(4):
        a, b = re[:, r * 128 : r * 128 + 128], im[:, r * 128 : r * 128 + 128]
        if r:
            a, b = times(a, b, twists[r][0], twists[r][1])
        more = turned(a, b, r)
        first = [a, b] if r == 0 else [first[0] + a, first[1] + b]
        second = list(more) if r == 0 else [second[0] + more[0], second[1] + more[1]]
    for p in range(2):
        grid[p, :256, :] = first[p]
        grid[p, 256:, :] = second[p]
    for d, out in enumerate((o0, o1, o2, o3)):
        out[:, 0:128, :] = grid[:, pl.ds(aligned(spot_of(idx, d)[0], 128), 128), :]
        out[0, 128:144, :] = small[0:16, :]
        out[1, 128:144, :] = small[16:32, :]


def mask_grad_kernel(scale, idx, ids, got, *refs):
    b0, b1, b2, b3, m_far, e, pupil, keep, send, grid, whole, m, sems = refs
    fetch = Fetch(sems, (m_far, m))
    small = None
    for d, block in enumerate((b0, b1, b2, b3)):
        grid[:, :, pl.ds(aligned(from_of(idx, d)[0], 128), 128)] = block[:, 0:128, :]
        part = jnp.concatenate([block[0, 128:144, :], block[1, 128:144, :]], 1)
        small = part if small is None else small + part
    fetch.wait(0)
    re, im = dft_right(grid[0], grid[1], mats_of(m), 1.0)
    re, im = times(re, im, e[idx[1], 0:1, :], e[idx[1], 1:2, :])
    factor = ratio_of(jnp.where(idx[2] == 1, ids[1], got[1]))[0:1, 0:1] * scale
    whole[...] = factor * (im * pupil[0] - re * pupil[1])
    keep[0:128, :] = whole[:, pl.ds(aligned(idx[1], 256), 256)]
    send[0:128, :] = whole[:, pl.ds(aligned(1 - idx[1], 256), 256)]
    keep[128:144, :] = small
    send[128:144, :] = small


def cut_kernel(ways, idx, keep, other, *refs):
    outs = refs[:ways]
    whole = refs[ways]
    whole[...] = keep[...] + other[...]
    piece = 128 // ways
    for d, out in enumerate(outs):
        to = lax.rem(idx[3] + d, ways)
        out[0:piece, :] = whole[pl.ds(aligned(to, piece), piece), :]
        out[piece : piece + 16, :] = whole[128:144, :]


def home_kernel(ways, pixel_count, idx, small, *refs):
    near, far, out, w1_out, b1_out, w2_out, loss_out, grid = refs
    piece = 128 // ways
    first = idx[1] == 0
    for y in range(ways):
        for h in range(2):
            row = 128 * h + piece * y
            a, b = near[y, h], far[y, h]
            grid[row : row + piece, 0:256] = jnp.where(first, a, b)
            grid[row : row + piece, 256:512] = jnp.where(first, b, a)
    central = (idx[0] == 1) | (idx[0] == 2)
    out[0:256, :] = jnp.zeros((256, 256), F32)
    out[768:1024, :] = jnp.zeros((256, 256), F32)
    out[256:768, :] = jnp.where(central, jnp.transpose(grid[...]), 0.0)
    table = jnp.concatenate([small[:, :128], small[:, 128:]], 0)
    flat = jnp.transpose(table)
    w1_out[...] = table[:, 0:9]
    w2_out[...] = flat[9:18, :]
    b1_out[...] = flat[18:19, :]
    loss_out[...] = table[0:1, 19:20] / pixel_count


def on_device(lay, phase_mask, height_offsets, sample_ids, wave_ids, scene, w1, b1, w2):
    con = constants()
    s = lax.axis_index("sp")
    c = lax.axis_index("core")
    y = lax.axis_index("y")
    owner = c == lax.axis_index("grp")
    pixel_count = float(lay.dp * N * 128)
    scale_psf = 1.0 / (N * N * pupil_count(N))
    idx = jnp.stack([s, c, owner.astype(jnp.int32), y]).astype(jnp.int32)

    def swap(g, zh, y, c, s):
        return (g, zh, y, 1 - c, s)

    def along_sp(blocks):
        return [blocks[0]] + [
            lay.move(blocks[d], lambda g, zh, y, c, s, d=d: (g, zh, y, c, s + d))
            for d in (1, 2, 3)
        ]

    def to_eight(blocks):
        return lax.all_to_all(blocks, ("core", "sp"), 0, 0, tiled=True)

    def gathered(block):
        near = along_sp([block] * 4)
        return near + [lay.move(part, swap) for part in near]

    ids = jnp.concatenate([sample_ids, wave_ids])
    got = lay.move(ids, swap)
    grabbed = lax.dynamic_slice(height_offsets, (ids[0], 256, 0), (1, 512, 256))[0]
    ratio = 550.0 / (400.0 + 10.0 * ids[1].astype(F32))
    phases = ratio * (phase_mask[256:768] + 0.1 * grabbed.astype(F32))

    mine = call(
        phase_kernel,
        (idx, phases),
        (0,),
        [(128, 256)] * 4,
        [pltpu.VMEM((256, 512), F32)],
    )
    pieces = list(mine[:2]) + [
        lay.move(
            block,
            lambda g, zh, y, c, s: (
                (g, zh, y, c, {1: 0, 2: 3}[s]) if s in (1, 2) and c == g else None
            ),
        )
        for block in mine[2:]
    ]
    pieces += [
        lay.move(
            block,
            lambda g, zh, y, c, s, inner=inner: (
                (g, zh, y, 1 - c, s) if c == g and (s in (1, 2)) == inner else None
            ),
        )
        for block, inner in zip(pieces, (True, True, False, False))
    ]

    scene, pieces[0] = lax.optimization_barrier((scene, pieces[0]))
    other = lay.move(lax.dynamic_slice_in_dim(scene[0], 120 * (1 - c), 136, 0), swap)

    *field, pupil = call(
        pupil_kernel,
        (idx, *pieces, con["m"], con["eighth"]),
        (0,),
        [(2, 128, 128)] * 4 + [(2, 128, 512)],
        [pltpu.VMEM((2, 128, 512), F32), bf16_buffer(4, 512, 512), fetch_sems(1)],
        (9,),
    )
    field = along_sp(field)

    scene_part, strip, edge = call(
        scene_kernel,
        (idx, scene, other, con["pack"]),
        (0,),
        [(8, 2, 64, 128), (136, 128), (8, 128)],
        [
            pltpu.VMEM((N, 128), F32),
            pltpu.VMEM((2, 512, 128), F32),
            bf16_buffer(2, N, N),
            fetch_sems(1),
        ],
        (3,),
    )
    edge = lay.move(
        edge,
        lambda g, zh, y, c, s: (
            (g, zh, y, 1 - c, s - 1 + 2 * c) if 0 <= s - 1 + 2 * c < 4 else None
        ),
    )
    far, parts = call(
        functools.partial(optics_kernel, scale_psf),
        (idx, *field, scene_part, con["f"], con["tw_col"]),
        (0,),
        [(2, 256, 512), (8, 4, 64, 128)],
        [
            pltpu.VMEM((2, 512, 128), F32),
            bf16_buffer(4, 256, 256),
            pltpu.VMEM((256, 8), F32),
            fetch_sems(2),
        ],
        (6, 7),
    )
    parts, edge = lax.optimization_barrier((to_eight(parts), edge))
    fourier = [bf16_buffer(4, 256, 256), pltpu.VMEM((8, 256), F32)]
    blurred, spectrum = call(
        blur_kernel,
        (idx, parts, con["f"], con["tw_row"]),
        (0,),
        [(8, ROWS, 128), (2, 288, 256)],
        [
            pltpu.VMEM((2, 64, N), F32),
            pltpu.VMEM((N + 16, 128), F32),
            *fourier,
            fetch_sems(2),
        ],
        (2, 3),
    )
    blurred = to_eight(blurred)
    g_window, sums = call(
        functools.partial(net_kernel, pixel_count),
        (idx, w1, b1, w2, blurred, con["window"], strip, edge),
        (0, 1, 2, 3),
        [(128, 128), (32, 24, 128)],
        [
            pltpu.VMEM((9, ROWS, 128), F32),
            pltpu.VMEM((9, ROWS, 128), F32),
            pltpu.VMEM((32, ROWS, 128), F32),
            pltpu.VMEM((9, ROWS, 128), F32),
            pltpu.VMEM((32, 19, 8, 128), F32),
            bf16_buffer(2, N, 128),
            fetch_sems(1),
        ],
        (5,),
    )
    small = jnp.pad(jnp.sum(sums, 2), ((0, 0), (0, 104)))
    g_parts = gathered(g_window)
    (otf_grad,) = call(
        otf_grad_kernel,
        (idx, *g_parts, con["near"], con["f"], con["tw_row"], spectrum),
        (0,),
        [(8, 2, 64, 128)],
        [
            pltpu.VMEM((N, 128), F32),
            pltpu.VMEM((2, 64, N), F32),
            *fourier,
            bf16_buffer(2, 128, 128),
            fetch_sems(3),
        ],
        (9, 10, 11),
    )
    otf_grad = to_eight(otf_grad)
    field_grad = along_sp(
        call(
            psf_grad_kernel,
            (idx, otf_grad, far, con["f"], con["tw_col"], small),
            (0,),
            [(2, 144, 128)] * 4,
            [
                pltpu.VMEM((2, 512, 128), F32),
                bf16_buffer(4, 256, 256),
                pltpu.VMEM((256, 8), F32),
                fetch_sems(2),
            ],
            (3, 4),
        )
    )
    keep, send = call(
        functools.partial(mask_grad_kernel, 2.0 * scale_psf),
        (idx, ids, got, *field_grad, con["m_back"], con["eighth"], pupil),
        (0, 1, 2),
        [(144, 256)] * 2,
        [
            pltpu.VMEM((2, 128, 512), F32),
            pltpu.VMEM((128, 512), F32),
            bf16_buffer(4, 512, 512),
            fetch_sems(1),
        ],
        (7,),
    )

    piece = 128 // lay.y
    blocks = call(
        functools.partial(cut_kernel, lay.y),
        (idx, keep, lay.move(send, swap)),
        (0,),
        [(piece + 16, 256)] * lay.y,
        [pltpu.VMEM((144, 256), F32)],
    )
    total = blocks[0]
    for d in range(1, lay.y):
        total = total + lay.move(
            blocks[d], lambda g, zh, y, c, s, d=d: (g, zh, y + d, c, s)
        )
    total = total + lay.move(total, lambda g, zh, y, c, s: (1 - g, zh, y, c, s))
    part = total
    for d in range(1, lay.zh):
        total = total + lay.move(part, lambda g, zh, y, c, s, d=d: (g, zh + d, y, c, s))
    part = total[:piece]
    near_part = lay.move(
        part, lambda g, zh, y, c, s: (g, zh, y, c, {0: 1, 3: 2}[s]) if s in (0, 3) else None
    )
    home = jnp.where(s == 1, jnp.stack([near_part, part]), jnp.stack([part, near_part]))
    near = lax.all_to_all(
        jnp.broadcast_to(home, (lay.y, 2, piece, 256)), "y", 0, 0, tiled=True
    )
    far = lay.move(
        near, lambda g, zh, y, c, s: (g, zh, y, 1 - c, s) if s in (1, 2) else None
    )
    mask_grad, w1_grad, b1_grad, w2_grad, loss = call(
        functools.partial(home_kernel, lay.y, pixel_count),
        (idx, total[piece:], near, far),
        (0,),
        [(N, 256), (32, 9), (1, 32), (9, 32), (1, 1)],
        [pltpu.VMEM((256, 512), F32)],
    )
    return mask_grad, w1_grad, b1_grad.reshape(32), w2_grad, loss.reshape(())


def solution(mesh):
    lay = Layout(mesh)
    images = ("zh", "y", "core")
    placed = (
        P(None, "sp"),
        P(None, None, "sp"),
        P(images),
        P(images),
        P(images, "sp", None),
        P(),
        P(),
        P(),
    )
    return jax.shard_map(
        functools.partial(on_device, lay),
        mesh=lay.mesh,
        in_specs=placed,
        out_specs=(P(None, "sp"), P(), P(), P(), P()),
        check_vma=False,
    )
```

```python
import functools
import itertools

import jax
import jax.numpy as jnp
import ml_dtypes
import numpy as np
from jax import lax
from jax.experimental import pallas as pl
from jax.experimental.pallas import tpu as pltpu
from jax.sharding import PartitionSpec as P

N = 1024
F32 = jnp.float32
BF16 = jnp.bfloat16
AXES = ("grp", "zh", "y", "core", "sp")
taps = ((-1, -1), (-1, 0), (-1, 1), (0, -1), (0, 0), (0, 1), (1, -1), (1, 0), (1, 1))


def halves(matrix):
    high = matrix.astype(ml_dtypes.bfloat16)
    low = (matrix - high.astype(np.float64)).astype(ml_dtypes.bfloat16)
    return high, low


def trig(rows, cols, length):
    angle = 2.0 * np.pi * (np.outer(rows, cols) % length) / length
    return np.cos(angle), np.sin(angle)


@functools.lru_cache(None)
def constants():
    half = np.arange(512)
    quarter = np.arange(256)
    fours = np.arange(4)
    spread = (np.arange(4)[:, None] * 256 + np.arange(128)).reshape(-1)
    cos_m, sin_m = trig(half, spread, N)
    cos_f, sin_f = trig(quarter, quarter, 256)
    cos_w, sin_w = trig(half, np.arange(N), N)
    sin_w = -sin_w
    sin_w[0] = (-1.0) ** np.arange(N)
    packed = np.concatenate([cos_w, sin_w])
    weight = np.full((N,), 2.0)
    weight[0] = 1.0
    weight[512] = 1.0
    unpack = (packed * weight[:, None]).T / (N * N)
    blocks = [np.r_[64 * q : 64 * q + 64, 512 + 64 * q : 576 + 64 * q] for q in range(8)]
    by_at = np.concatenate([blocks[2 * s + c] for c in range(2) for s in range(4)])
    near = packed[np.concatenate(blocks), 256:384].reshape(8, 128, 128).transpose(0, 2, 1)
    window = np.stack(halves(unpack[256:384, by_at].T))
    window = window.reshape(4, 2, 256, 128).transpose(0, 2, 1, 3).reshape(4, 256, 256)
    near = np.stack(halves(near)).reshape(4, 2, 2, 128, 128)
    near = near.transpose(0, 1, 3, 2, 4).reshape(4, 256, 256)
    cos_e, sin_e = trig([0, 1], half, 8)
    cos_t, sin_t = trig(quarter, fours, N)
    return {
        "m": np.stack(halves(cos_m) + halves(sin_m)),
        "m_back": np.stack(halves(cos_m.T) + halves(sin_m.T)),
        "f": np.concatenate([np.stack(halves(cos_f) + halves(sin_f)), window, near]),
        "pack": np.stack(halves(packed)),
        "eighth": np.stack([cos_e, sin_e], 1).astype(np.float32),
        "tw_col": np.concatenate([cos_t, sin_t], 1).astype(np.float32),
        "tw_row": np.concatenate([cos_t, sin_t], 1).T.astype(np.float32).copy(),
    }


def pupil_count(size_grid):
    coords = np.arange(size_grid) * 2 - size_grid + 1
    inside = (coords[:, None] ** 2 + coords[None, :] ** 2) * 4 <= size_grid * size_grid
    return float(np.sum(inside))


class Layout:
    def __init__(self, mesh):
        self.dp = mesh.shape["dp"]
        self.y = min(4, self.dp // 2)
        self.zh = self.dp // (2 * self.y)
        self.sp = mesh.shape["sp"]
        self.sizes = (2, self.zh, self.y, 2, self.sp)
        self.mesh = jax.sharding.Mesh(mesh.devices.reshape(self.sizes), AXES)

    def move(self, x, where):
        pairs = []
        for spot in itertools.product(*[range(n) for n in self.sizes]):
            goal = where(*spot)
            if goal is not None:
                pairs.append((self.flat(spot), self.flat(goal)))
        return lax.ppermute(x, AXES, pairs)

    def flat(self, spot):
        at = 0
        for place, size in zip(spot, self.sizes):
            at = at * size + place % size
        return at


def split(x):
    high = x.astype(BF16)
    return high, (x - high.astype(F32)).astype(BF16)


def dot(a, b):
    return lax.dot_general(a, b, (((1,), (0,)), ((), ())), preferred_element_type=F32)


def by_right(x, w_high, w_low):
    high, low = split(x)
    return dot(high, w_high) + (dot(high, w_low) + dot(low, w_high))


def by_left(w_high, w_low, x):
    high, low = split(x)
    return dot(w_high, high) + (dot(w_low, high) + dot(w_high, low))


def dft_right(re, im, mats, sign):
    rows = re.shape[0]
    both = jnp.concatenate([re, im], 0)
    by_cos = by_right(both, mats[0], mats[1])
    by_sin = by_right(both, mats[2], mats[3]) * sign
    return by_cos[:rows] - by_sin[rows:], by_cos[rows:] + by_sin[:rows]


def dft_left(re, im, mats, sign):
    cols = re.shape[1]
    both = jnp.concatenate([re, im], 1)
    by_cos = by_left(mats[0], mats[1], both)
    by_sin = by_left(mats[2], mats[3], both) * sign
    return by_cos[:, :cols] - by_sin[:, cols:], by_cos[:, cols:] + by_sin[:, :cols]


def turned(re, im, quarter_turns):
    quarter_turns %= 4
    if quarter_turns == 0:
        return re, im
    if quarter_turns == 1:
        return -im, re
    if quarter_turns == 2:
        return -re, -im
    return im, -re


def times(re, im, cos, sin):
    return re * cos - im * sin, re * sin + im * cos


def cos_sin(x):
    n = jnp.floor(x * (2.0 / np.pi) + 0.5)
    r = x - n * 1.5707963109016418
    r = r - n * 1.5893254712295857e-8
    q = n.astype(jnp.int32) & 3
    z = r * r
    sn = r + r * z * (-1.6666654611e-1 + z * (8.3321608736e-3 + z * -1.9515295891e-4))
    cs = 1.0 - 0.5 * z + z * z * (
        4.166664568298827e-2 + z * (-1.388731625493765e-3 + z * 2.443315711809948e-5)
    )
    odd = (q & 1) == 1
    c0 = jnp.where(odd, sn, cs)
    s0 = jnp.where(odd, cs, sn)
    cos = jnp.where((q == 1) | (q == 2), -c0, c0)
    sin = jnp.where(q >= 2, -s0, s0)
    return cos, sin


def spot_of(idx, d, e=0):
    return lax.rem(idx[0] + d, 4), lax.rem(idx[1] + e, 2)


def from_of(idx, d, e=0):
    return lax.rem(idx[0] + 4 - d, 4), lax.rem(idx[1] + 2 - e, 2)


def aligned(x, by):
    return pl.multiple_of(x * by, by)


def call(kernel, operands, in_smem, outs, scratch=(), apart=()):
    specs = []
    for at in range(len(operands)):
        space = pltpu.SMEM if at in in_smem else pltpu.VMEM
        specs.append(pl.BlockSpec(memory_space=pltpu.HBM if at in apart else space))
    return pl.pallas_call(
        kernel,
        out_shape=[jax.ShapeDtypeStruct(shape, F32) for shape in outs],
        in_specs=specs,
        out_specs=[pl.BlockSpec(memory_space=pltpu.VMEM) for _ in outs],
        scratch_shapes=list(scratch),
        compiler_params=pltpu.CompilerParams(vmem_limit_bytes=20 * 1024 * 1024),
    )(*operands)


relations = [(d, e) for e in range(2) for d in range(4)]


def ratio_of(wave):
    return 550.0 / (400.0 + 10.0 * jnp.full((8, 128), wave, jnp.int32).astype(F32))


def mats_of(ref):
    return ref[0], ref[1], ref[2], ref[3]


def phase_kernel(idx, phases, own0, own1, sent0, sent1, grid):
    grid[...] = jnp.transpose(phases[...])
    kept = aligned(jnp.where(idx[0] == 1, 1, 0), 128)
    given = aligned(jnp.where(idx[0] == 1, 0, 1), 128)
    own0[...] = grid[pl.ds(kept, 128), 0:256]
    own1[...] = grid[pl.ds(kept, 128), 256:512]
    sent0[...] = grid[pl.ds(given, 128), 0:256]
    sent1[...] = grid[pl.ds(given, 128), 256:512]


def scene_kernel(idx, scene, other, w, out, strip, edge, image, grid):
    owner = idx[2] == 1
    c = idx[1]
    rows = jnp.where(
        owner,
        scene[0, pl.ds(aligned(15 * c, 8), 136), :],
        other[...],
    )
    strip[...] = rows[:, 256:384]
    edge[...] = jnp.where(c == 0, rows[0:8, 256:384], rows[128:136, 256:384])
    image[...] = jnp.transpose(jnp.where(c == 0, rows[0:128], rows[8:136]))
    spectrum = by_left(w[0], w[1], image[...])
    grid[0] = spectrum[:512]
    grid[1] = spectrum[512:]
    eight_rows(out, grid)


def pupil_kernel(idx, *refs):
    m, e, o0, o1, o2, o3, pupil, grid = refs[8:]
    s = idx[0]
    c = idx[1]
    owner = idx[2] == 1
    central = (s == 1) | (s == 2)
    own = jnp.concatenate([refs[0][...], refs[1][...]], 1)
    got = jnp.concatenate([refs[2][...], refs[3][...]], 1)
    own_far = jnp.concatenate([refs[4][...], refs[5][...]], 1)
    got_far = jnp.concatenate([refs[6][...], refs[7][...]], 1)
    phase = jnp.where(central, jnp.where(owner, own, own_far), jnp.where(owner, got, got_far))
    rows = lax.broadcasted_iota(jnp.int32, (128, 512), 0) + s * 128
    cols = lax.broadcasted_iota(jnp.int32, (128, 512), 1)
    across = (rows + 256) * 2 - N + 1
    down = (cols + 256) * 2 - N + 1
    inside = (down * down + across * across) * 4 <= N * N
    cos, sin = cos_sin(phase)
    re = jnp.where(inside, cos, 0.0)
    im = jnp.where(inside, sin, 0.0)
    pupil[0] = re
    pupil[1] = im
    re, im = times(re, im, e[c, 0:1, :], -e[c, 1:2, :])
    out_re, out_im = dft_right(re, im, mats_of(m), -1.0)
    grid[0] = out_re
    grid[1] = out_im
    for d, out in enumerate((o0, o1, o2, o3)):
        to = spot_of(idx, d)[0]
        out[...] = grid[:, :, pl.ds(aligned(to, 128), 128)]


def eight_rows(out, grid):
    for c in range(2):
        for s in range(4):
            row = 128 * s + 64 * c
            out[4 * c + s, 0:2] = grid[:, row : row + 64, :]


def eight_columns(out, grid):
    for c in range(2):
        for s in range(4):
            col = 128 * (2 * s + c)
            out[4 * c + s] = grid[:, :, col : col + 128]


def optics_kernel(scale, idx, b0, b1, b2, b3, scene, *refs):
    f, tw, far, out, grid = refs
    for d, block in enumerate((b0, b1, b2, b3)):
        grid[:, pl.ds(aligned(from_of(idx, d)[0], 128), 128), :] = block[...]
    low = (grid[0, :256, :], grid[1, :256, :])
    high = (grid[0, 256:, :], grid[1, 256:, :])
    twists = [(tw[:, r : r + 1], tw[:, 4 + r : 5 + r]) for r in range(4)]
    res, ims = [], []
    for r in range(4):
        add = turned(high[0], high[1], -r)
        re, im = low[0] + add[0], low[1] + add[1]
        if r:
            re, im = times(re, im, twists[r][0], -twists[r][1])
        res.append(re)
        ims.append(im)
    mats = mats_of(f)
    far_re, far_im = dft_left(
        jnp.concatenate(res, 1), jnp.concatenate(ims, 1), mats, -1.0
    )
    far[0] = far_re
    far[1] = far_im
    psf = scale * (far_re * far_re + far_im * far_im)
    psf_high, psf_low = split(psf)
    z_re = dot(mats[0], psf_high) + (dot(mats[1], psf_high) + dot(mats[0], psf_low))
    z_im = -(dot(mats[2], psf_high) + (dot(mats[3], psf_high) + dot(mats[2], psf_low)))
    first = [None, None]
    second = [None, None]
    nyquist = None
    for r in range(4):
        re = z_re[:, r * 128 : r * 128 + 128]
        im = z_im[:, r * 128 : r * 128 + 128]
        top = re[0:1, :]
        nyquist = top if r == 0 else (nyquist + top if r % 2 == 0 else nyquist - top)
        if r:
            re, im = times(re, im, twists[r][0], -twists[r][1])
        more = turned(re, im, -r)
        first = [re, im] if r == 0 else [first[0] + re, first[1] + im]
        second = list(more) if r == 0 else [second[0] + more[0], second[1] + more[1]]
    row = lax.broadcasted_iota(jnp.int32, (256, 128), 0)
    grid[0, :256, :] = first[0]
    grid[1, :256, :] = jnp.where(row == 0, nyquist, first[1])
    grid[0, 256:, :] = second[0]
    grid[1, 256:, :] = second[1]
    eight_rows(out, grid)
    for at in range(8):
        out[at, 2:4] = scene[at]


def unpack_rows(idx, re, im, tail):
    rows = lax.broadcasted_iota(jnp.int32, re.shape, 0)
    first = (idx[0] + idx[1]) == 0
    nyquist = jnp.where(first, im[0:1, :], 0.0)
    tail_rows = lax.broadcasted_iota(jnp.int32, (tail, re.shape[1]), 0)
    extra = jnp.where(tail_rows == 0, nyquist, 0.0)
    im = jnp.where((rows == 0) & first, 0.0, im)
    return jnp.concatenate([re, extra], 0), jnp.concatenate([im, jnp.zeros_like(extra)], 0)


def repack_rows(idx, re, im):
    first = (idx[0] + idx[1]) == 0
    rows = lax.broadcasted_iota(jnp.int32, (64, re.shape[1]), 0)
    return re[:64], jnp.where((rows == 0) & first, re[64:65, :], im[:64])


def row_transform(idx, blocks, first, mats, tw, grid):
    for c in range(2):
        for s in range(4):
            col = 128 * (2 * s + c)
            grid[:, :, col : col + 128] = blocks[4 * c + s, first : first + 2]
    return rows_out(idx, grid[0], grid[1], mats, tw)


def rows_back(idx, re, im, mats, tw, grid):
    re, im = dft_right(re, im, mats, 1.0)
    parts = []
    for r in range(4):
        a, b = re[r * 72 : r * 72 + 72], im[r * 72 : r * 72 + 72]
        if r:
            a, b = times(a, b, tw[r : r + 1, :], tw[4 + r : 5 + r, :])
        parts.append((a, b))
    for q in range(4):
        a, b = parts[0]
        for r in range(1, 4):
            more = turned(parts[r][0], parts[r][1], q * r)
            a = a + more[0]
            b = b + more[1]
        a, b = repack_rows(idx, a, b)
        grid[0, :, q * 256 : q * 256 + 256] = a
        grid[1, :, q * 256 : q * 256 + 256] = b


def rows_out(idx, re, im, mats, tw):
    re, im = unpack_rows(idx, re, im, 8)
    quarters = [(re[:, q * 256 : q * 256 + 256], im[:, q * 256 : q * 256 + 256]) for q in range(4)]
    sum02 = [quarters[0][p] + quarters[2][p] for p in range(2)]
    dif02 = [quarters[0][p] - quarters[2][p] for p in range(2)]
    sum13 = [quarters[1][p] + quarters[3][p] for p in range(2)]
    dif13 = [quarters[1][p] - quarters[3][p] for p in range(2)]
    step = turned(dif13[0], dif13[1], -1)
    parts = [
        (sum02[0] + sum13[0], sum02[1] + sum13[1]),
        (dif02[0] + step[0], dif02[1] + step[1]),
        (sum02[0] - sum13[0], sum02[1] - sum13[1]),
        (dif02[0] - step[0], dif02[1] - step[1]),
    ]
    for r in range(1, 4):
        parts[r] = times(parts[r][0], parts[r][1], tw[r : r + 1, :], -tw[4 + r : 5 + r, :])
    return dft_right(
        jnp.concatenate([p[0] for p in parts], 0),
        jnp.concatenate([p[1] for p in parts], 0),
        mats,
        -1.0,
    )


def blur_kernel(idx, blocks, f, tw, out, spectrum, grid, turned_grid):
    mats = mats_of(f)
    re, im = row_transform(idx, blocks, 2, mats, tw, grid)
    spectrum[0] = re
    spectrum[1] = im
    re, im = row_transform(idx, blocks, 0, mats, tw, grid)
    re, im = times(re, im, spectrum[0], spectrum[1])
    rows_back(idx, re, im, mats, tw, grid)
    both = jnp.transpose(jnp.concatenate([grid[0], grid[1]], 0))
    turned_grid[8 : N + 8, :] = both
    turned_grid[0:8, :] = both[N - 8 :, :]
    turned_grid[N + 8 :, :] = both[:8, :]
    for c in range(2):
        for s in range(4):
            row = 128 * (2 * s + c)
            out[4 * c + s] = turned_grid[row : row + ROWS, :]


def moved_lanes(x, e, lanes):
    if e == 0:
        return x
    rolled = pltpu.roll(x, (-e) % 128, 1)
    return jnp.where(lanes == (127 if e > 0 else 0), 0.0, rolled)


def moved_rows(x, a):
    if a == 0:
        return x
    return pltpu.roll(x, (-a) % x.shape[0], 0)


ROWS = 144


def net_kernel(pixel_count, idx, w1, b1, w2, *refs):
    blocks, f, strip, edge, g_out, sums_out = refs[:6]
    win_taps, g_taps, hidden, sums, acc = refs[6:]
    target = jnp.where(
        idx[1] == 0,
        jnp.concatenate([edge[...], strip[...]], 0),
        jnp.concatenate([strip[...], edge[...]], 0),
    )
    window = None
    for at in range(4):
        part = by_right(
            jnp.concatenate([blocks[2 * at], blocks[2 * at + 1]], 1),
            f[4 + at // 2, :, 128 * (at % 2) : 128 * (at % 2) + 128],
            f[6 + at // 2, :, 128 * (at % 2) : 128 * (at % 2) + 128],
        )
        window = part if window is None else window + part
    rows = lax.broadcasted_iota(jnp.int32, (ROWS, 128), 0)
    lanes = lax.broadcasted_iota(jnp.int32, (ROWS, 128), 1)
    row_global = rows + (2 * idx[0] + idx[1]) * 128 - 8
    inside = (row_global >= 0) & (row_global < N)
    window = jnp.where(inside, window, 0.0)
    for e in (-1, 0, 1):
        side = moved_lanes(window, e, lanes)
        for a in (-1, 0, 1):
            win_taps[3 * (a + 1) + e + 1] = moved_rows(side, a)
    step = 24
    for k in range(ROWS // step):
        part = pl.ds(k * step, step)

        def forward(c, total, part=part):
            pre = w1[c, 0] * win_taps[0, part, :]
            for t in range(1, 9):
                pre = pre + w1[c, t] * win_taps[t, part, :]
            hid = jnp.maximum(pre + b1[c], 0.0)
            hidden[c, part, :] = hid
            return tuple(total[t] + w2[t, c] * hid for t in range(9))

        total = lax.fori_loop(
            0, 32, forward, tuple(jnp.zeros((step, 128), F32) for _ in range(9)), unroll=4
        )
        for t in range(9):
            sums[t, part, :] = total[t]
    restored = window
    for e in (-1, 0, 1):
        side = None
        for a in (-1, 0, 1):
            part = moved_rows(jnp.where(inside, sums[3 * (a + 1) + e + 1], 0.0), a)
            side = part if side is None else side + part
        restored = restored + moved_lanes(side, e, lanes)
    residual = jnp.where(inside, restored - target, 0.0)
    own = (rows >= 8) & (rows < 136)
    own_residual = jnp.where(own, residual, 0.0)
    loss = jnp.sum(own_residual * own_residual, 0, keepdims=True)
    g_restored = (2.0 / pixel_count) * residual
    for e in (-1, 0, 1):
        side = moved_lanes(g_restored, -e, lanes)
        for a in (-1, 0, 1):
            g_taps[3 * (a + 1) + e + 1] = jnp.where(inside, moved_rows(side, -a), 0.0)
    acc[...] = jnp.zeros_like(acc)

    def folded(x):
        total = x[:8]
        for row in range(8, x.shape[0], 8):
            total = total + x[row : row + 8]
        return total

    for start, step, mine in [(0, 8, False)] + [(8 + 32 * k, 32, True) for k in range(4)] + [
        (136, 8, False)
    ]:
        part = pl.ds(start, step)

        def backward(c, total, part=part, step=step, mine=mine):
            hid = hidden[c, part, :]
            gh = w2[0, c] * g_taps[0, part, :]
            for t in range(1, 9):
                gh = gh + w2[t, c] * g_taps[t, part, :]
            gp = jnp.where(hid > 0.0, gh, 0.0)
            if mine:
                for t in range(9):
                    acc[c, t] += folded(gp * win_taps[t, part, :])
                    acc[c, 9 + t] += folded(hid * g_taps[t, part, :])
                acc[c, 18] += folded(gp)
            return tuple(total[t] + w1[c, t] * gp for t in range(9))

        total = lax.fori_loop(
            0, 32, backward, tuple(jnp.zeros((step, 128), F32) for _ in range(9)), unroll=4
        )
        for t in range(9):
            sums[t, part, :] = total[t]
    g_window = g_restored
    for e in (-1, 0, 1):
        side = None
        for a in (-1, 0, 1):
            part = moved_rows(sums[3 * (a + 1) + e + 1], -a)
            side = part if side is None else side + part
        g_window = g_window + moved_lanes(side, -e, lanes)
    g_out[...] = g_window[8:136]
    for c in range(32):
        sums_out[c, 0:19, :] = jnp.sum(acc[c], 1)
        sums_out[c, 19:24, :] = jnp.broadcast_to(loss, (5, 128))


def otf_grad_kernel(idx, *refs):
    blocks = refs[:8]
    f, tw, spectrum, out, window, grid = refs[8:]
    for d, e in relations:
        s, c = from_of(idx, d, e)
        window[pl.ds(aligned(2 * s + c, 128), 128), :] = blocks[4 * e + d][...]
    rows = pl.ds(aligned(lax.rem(idx[0], 2), 128), 128)
    cols = pl.ds(aligned(idx[1], 128), 128)
    at = lax.div(idx[0], 2)
    packed = jnp.transpose(by_right(window[...], f[8 + at, rows, cols], f[10 + at, rows, cols]))
    mats = mats_of(f)
    re, im = rows_out(idx, packed[:64], packed[64:], mats, tw)
    re, im = times(re, im, spectrum[0], -spectrum[1])
    rows_back(idx, re, im, mats, tw, grid)
    eight_columns(out, grid)


def psf_grad_kernel(idx, blocks, far, f, tw, small, o0, o1, o2, o3, grid):
    for c in range(2):
        for s in range(4):
            grid[:, 128 * s + 64 * c : 128 * s + 64 * c + 64, :] = blocks[4 * c + s]
    row = lax.broadcasted_iota(jnp.int32, (256, 128), 0)
    zero_row = row == 0
    low_re, low_im = grid[0, :256, :], grid[1, :256, :]
    nyquist = jnp.where(zero_row, 0.5 * low_im, 0.0)
    low_re = jnp.where(zero_row, 0.5 * low_re, low_re)
    low_im = jnp.where(zero_row, 0.0, low_im)
    high = (grid[0, 256:, :], grid[1, 256:, :])
    twists = [(tw[:, r : r + 1], tw[:, 4 + r : 5 + r]) for r in range(4)]
    res, ims = [], []
    for r in range(4):
        add = turned(high[0], high[1], r)
        re, im = low_re + add[0], low_im + add[1]
        if r:
            re, im = times(re, im, twists[r][0], twists[r][1])
        re = re + nyquist if r % 2 == 0 else re - nyquist
        res.append(re)
        ims.append(im)
    mats = mats_of(f)
    g_psf = 2.0 * (
        by_left(mats[0], mats[1], jnp.concatenate(res, 1))
        - by_left(mats[2], mats[3], jnp.concatenate(ims, 1))
    )
    re, im = dft_left(g_psf * far[0], g_psf * far[1], mats, 1.0)
    first, second = None, None
    for r in range(4):
        a, b = re[:, r * 128 : r * 128 + 128], im[:, r * 128 : r * 128 + 128]
        if r:
            a, b = times(a, b, twists[r][0], twists[r][1])
        more = turned(a, b, r)
        first = [a, b] if r == 0 else [first[0] + a, first[1] + b]
        second = list(more) if r == 0 else [second[0] + more[0], second[1] + more[1]]
    for p in range(2):
        grid[p, :256, :] = first[p]
        grid[p, 256:, :] = second[p]
    for d, out in enumerate((o0, o1, o2, o3)):
        out[:, 0:128, :] = grid[:, pl.ds(aligned(spot_of(idx, d)[0], 128), 128), :]
        out[0, 128:136, :] = small[...]
        out[1, 128:136, :] = small[...]


def mask_grad_kernel(scale, idx, ids, got, *refs):
    b0, b1, b2, b3, m, e, pupil, keep, send, grid, whole = refs
    small = None
    for d, block in enumerate((b0, b1, b2, b3)):
        grid[:, :, pl.ds(aligned(from_of(idx, d)[0], 128), 128)] = block[:, 0:128, :]
        part = jnp.concatenate([block[0, 128:136, :], block[1, 128:136, :]], 1)
        small = part if small is None else small + part
    re, im = dft_right(grid[0], grid[1], mats_of(m), 1.0)
    re, im = times(re, im, e[idx[1], 0:1, :], e[idx[1], 1:2, :])
    factor = ratio_of(jnp.where(idx[2] == 1, ids[1], got[1]))[0:1, 0:1] * scale
    whole[...] = factor * (im * pupil[0] - re * pupil[1])
    keep[0:128, :] = whole[:, pl.ds(aligned(idx[1], 256), 256)]
    send[0:128, :] = whole[:, pl.ds(aligned(1 - idx[1], 256), 256)]
    keep[128:136, :] = small
    send[128:136, :] = small


def cut_kernel(ways, idx, keep, other, *refs):
    outs = refs[:ways]
    whole = refs[ways]
    whole[...] = keep[...] + other[...]
    piece = 128 // ways
    for d, out in enumerate(outs):
        to = lax.rem(idx[3] + d, ways)
        out[0:piece, :] = whole[pl.ds(aligned(to, piece), piece), :]
        out[piece : piece + 8, :] = whole[128:136, :]


def home_kernel(ways, pixel_count, idx, small, *refs):
    near, far, out, w1_out, b1_out, w2_out, loss_out, grid = refs
    piece = 128 // ways
    first = idx[1] == 0
    for y in range(ways):
        for h in range(2):
            row = 128 * h + piece * y
            a, b = near[y, h], far[y, h]
            grid[row : row + piece, 0:256] = jnp.where(first, a, b)
            grid[row : row + piece, 256:512] = jnp.where(first, b, a)
    central = (idx[0] == 1) | (idx[0] == 2)
    out[0:256, :] = jnp.zeros((256, 256), F32)
    out[768:1024, :] = jnp.zeros((256, 256), F32)
    out[256:768, :] = jnp.where(central, jnp.transpose(grid[...]), 0.0)
    flat = jnp.concatenate([small[:, 32 * g : 32 * g + 32] for g in range(3)], 0)
    w1_out[...] = flat[0:9, :]
    w2_out[...] = flat[9:18, :]
    b1_out[...] = flat[18:19, :]
    loss_out[...] = flat[19:20, 0:1] / pixel_count


def on_device(lay, phase_mask, height_offsets, sample_ids, wave_ids, scene, w1, b1, w2):
    con = constants()
    s = lax.axis_index("sp")
    c = lax.axis_index("core")
    y = lax.axis_index("y")
    owner = c == lax.axis_index("grp")
    pixel_count = float(lay.dp * N * 128)
    scale_psf = 1.0 / (N * N * pupil_count(N))
    idx = jnp.stack([s, c, owner.astype(jnp.int32), y]).astype(jnp.int32)

    def swap(g, zh, y, c, s):
        return (g, zh, y, 1 - c, s)

    def along_sp(blocks):
        return [blocks[0]] + [
            lay.move(blocks[d], lambda g, zh, y, c, s, d=d: (g, zh, y, c, s + d))
            for d in (1, 2, 3)
        ]

    def to_eight(blocks):
        return lax.all_to_all(blocks, ("core", "sp"), 0, 0, tiled=True)

    def gathered(block):
        near = along_sp([block] * 4)
        return near + [lay.move(part, swap) for part in near]

    ids = jnp.concatenate([sample_ids, wave_ids])
    got = lay.move(ids, swap)
    grabbed = lax.dynamic_slice(height_offsets, (ids[0], 256, 0), (1, 512, 256))[0]
    ratio = 550.0 / (400.0 + 10.0 * ids[1].astype(F32))
    phases = ratio * (phase_mask[256:768] + 0.1 * grabbed.astype(F32))

    mine = call(
        phase_kernel,
        (idx, phases),
        (0,),
        [(128, 256)] * 4,
        [pltpu.VMEM((256, 512), F32)],
    )
    pieces = list(mine[:2]) + [
        lay.move(
            block,
            lambda g, zh, y, c, s: (
                (g, zh, y, c, {1: 0, 2: 3}[s]) if s in (1, 2) and c == g else None
            ),
        )
        for block in mine[2:]
    ]
    pieces += [
        lay.move(
            block,
            lambda g, zh, y, c, s, inner=inner: (
                (g, zh, y, 1 - c, s) if c == g and (s in (1, 2)) == inner else None
            ),
        )
        for block, inner in zip(pieces, (True, True, False, False))
    ]

    scene, pieces[0] = lax.optimization_barrier((scene, pieces[0]))
    other = lay.move(lax.dynamic_slice_in_dim(scene[0], 120 * (1 - c), 136, 0), swap)

    *field, pupil = call(
        pupil_kernel,
        (idx, *pieces, con["m"], con["eighth"]),
        (0,),
        [(2, 128, 128)] * 4 + [(2, 128, 512)],
        [pltpu.VMEM((2, 128, 512), F32)],
    )
    field = along_sp(field)

    scene_part, strip, edge = call(
        scene_kernel,
        (idx, scene, other, con["pack"]),
        (0,),
        [(8, 2, 64, 128), (136, 128), (8, 128)],
        [
            pltpu.VMEM((N, 128), F32),
            pltpu.VMEM((2, 512, 128), F32),
        ],
    )
    edge = lay.move(
        edge,
        lambda g, zh, y, c, s: (
            (g, zh, y, 1 - c, s - 1 + 2 * c) if 0 <= s - 1 + 2 * c < 4 else None
        ),
    )
    far, parts = call(
        functools.partial(optics_kernel, scale_psf),
        (idx, *field, scene_part, con["f"], con["tw_col"]),
        (0,),
        [(2, 256, 512), (8, 4, 64, 128)],
        [
            pltpu.VMEM((2, 512, 128), F32),
        ],
    )
    parts, edge = lax.optimization_barrier((to_eight(parts), edge))
    blurred, spectrum = call(
        blur_kernel,
        (idx, parts, con["f"], con["tw_row"]),
        (0,),
        [(8, ROWS, 128), (2, 288, 256)],
        [
            pltpu.VMEM((2, 64, N), F32),
            pltpu.VMEM((N + 16, 128), F32),
        ],
    )
    blurred = to_eight(blurred)
    g_window, sums = call(
        functools.partial(net_kernel, pixel_count),
        (idx, w1, b1, w2, blurred, con["f"], strip, edge),
        (0, 1, 2, 3),
        [(128, 128), (32, 24, 128)],
        [
            pltpu.VMEM((9, ROWS, 128), F32),
            pltpu.VMEM((9, ROWS, 128), F32),
            pltpu.VMEM((32, ROWS, 128), F32),
            pltpu.VMEM((9, ROWS, 128), F32),
            pltpu.VMEM((32, 19, 8, 128), F32),
        ],
    )
    small = jnp.sum(sums, 2).reshape(32, 3, 8).transpose(2, 1, 0).reshape(8, 96)
    small = jnp.pad(small, ((0, 0), (0, 32)))
    g_parts = gathered(g_window)
    (otf_grad,) = call(
        otf_grad_kernel,
        (idx, *g_parts, con["f"], con["tw_row"], spectrum),
        (0,),
        [(8, 2, 64, 128)],
        [
            pltpu.VMEM((N, 128), F32),
            pltpu.VMEM((2, 64, N), F32),
        ],
    )
    otf_grad = to_eight(otf_grad)
    field_grad = along_sp(
        call(
            psf_grad_kernel,
            (idx, otf_grad, far, con["f"], con["tw_col"], small),
            (0,),
            [(2, 136, 128)] * 4,
            [
                pltpu.VMEM((2, 512, 128), F32),
            ],
        )
    )
    keep, send = call(
        functools.partial(mask_grad_kernel, 2.0 * scale_psf),
        (idx, ids, got, *field_grad, con["m_back"], con["eighth"], pupil),
        (0, 1, 2),
        [(136, 256)] * 2,
        [
            pltpu.VMEM((2, 128, 512), F32),
            pltpu.VMEM((128, 512), F32),
        ],
    )

    piece = 128 // lay.y
    blocks = call(
        functools.partial(cut_kernel, lay.y),
        (idx, keep, lay.move(send, swap)),
        (0,),
        [(piece + 8, 256)] * lay.y,
        [pltpu.VMEM((136, 256), F32)],
    )
    total = blocks[0]
    for d in range(1, lay.y):
        total = total + lay.move(
            blocks[d], lambda g, zh, y, c, s, d=d: (g, zh, y + d, c, s)
        )
    total = total + lay.move(total, lambda g, zh, y, c, s: (1 - g, zh, y, c, s))
    part = total
    for d in range(1, lay.zh):
        total = total + lay.move(part, lambda g, zh, y, c, s, d=d: (g, zh + d, y, c, s))
    part = total[:piece]
    near_part = lay.move(
        part, lambda g, zh, y, c, s: (g, zh, y, c, {0: 1, 3: 2}[s]) if s in (0, 3) else None
    )
    home = jnp.where(s == 1, jnp.stack([near_part, part]), jnp.stack([part, near_part]))
    near = lax.all_to_all(
        jnp.broadcast_to(home, (lay.y, 2, piece, 256)), "y", 0, 0, tiled=True
    )
    far = lay.move(
        near, lambda g, zh, y, c, s: (g, zh, y, 1 - c, s) if s in (1, 2) else None
    )
    mask_grad, w1_grad, b1_grad, w2_grad, loss = call(
        functools.partial(home_kernel, lay.y, pixel_count),
        (idx, total[piece:], near, far),
        (0,),
        [(N, 256), (9, 32), (1, 32), (9, 32), (1, 1)],
        [pltpu.VMEM((256, 512), F32)],
    )
    return mask_grad, w1_grad.T, b1_grad.reshape(32), w2_grad, loss.reshape(())


def solution(mesh):
    lay = Layout(mesh)
    images = ("zh", "y", "core")
    placed = (
        P(None, "sp"),
        P(None, None, "sp"),
        P(images),
        P(images),
        P(images, "sp", None),
        P(),
        P(),
        P(),
    )
    return jax.shard_map(
        functools.partial(on_device, lay),
        mesh=lay.mesh,
        in_specs=placed,
        out_specs=(P(None, "sp"), P(), P(), P(), P()),
        check_vma=False,
    )
```

```python
import functools
import itertools

import jax
import jax.numpy as jnp
import ml_dtypes
import numpy as np
from jax import lax
from jax.experimental import pallas as pl
from jax.experimental.pallas import tpu as pltpu
from jax.sharding import PartitionSpec as P

N = 1024
F32 = jnp.float32
BF16 = jnp.bfloat16
AXES = ("grp", "zh", "y", "core", "sp")
taps = ((-1, -1), (-1, 0), (-1, 1), (0, -1), (0, 0), (0, 1), (1, -1), (1, 0), (1, 1))


def halves(matrix):
    high = matrix.astype(ml_dtypes.bfloat16)
    low = (matrix - high.astype(np.float64)).astype(ml_dtypes.bfloat16)
    return high, low


def trig(rows, cols, length):
    angle = 2.0 * np.pi * (np.outer(rows, cols) % length) / length
    return np.cos(angle), np.sin(angle)


@functools.lru_cache(None)
def constants():
    half = np.arange(512)
    quarter = np.arange(256)
    fours = np.arange(4)
    spread = (np.arange(4)[:, None] * 256 + np.arange(128)).reshape(-1)
    cos_m, sin_m = trig(half, spread, N)
    cos_f, sin_f = trig(quarter, quarter, 256)
    cos_w, sin_w = trig(half, np.arange(N), N)
    sin_w = -sin_w
    sin_w[0] = (-1.0) ** np.arange(N)
    packed = np.concatenate([cos_w, sin_w])
    weight = np.full((N,), 2.0)
    weight[0] = 1.0
    weight[512] = 1.0
    unpack = (packed * weight[:, None]).T / (N * N)
    blocks = [np.r_[64 * q : 64 * q + 64, 512 + 64 * q : 576 + 64 * q] for q in range(8)]
    by_at = np.concatenate([blocks[2 * s + c] for c in range(2) for s in range(4)])
    near = packed[np.concatenate(blocks), 256:384].reshape(8, 128, 128).transpose(0, 2, 1)
    window = np.stack(halves(unpack[256:384, by_at].T))
    window = window.reshape(4, 2, 256, 128).transpose(0, 2, 1, 3).reshape(4, 256, 256)
    near = np.stack(halves(near)).reshape(4, 2, 2, 128, 128)
    near = near.transpose(0, 1, 3, 2, 4).reshape(4, 256, 256)
    cos_e, sin_e = trig([0, 1], half, 8)
    cos_t, sin_t = trig(quarter, fours, N)
    return {
        "m": np.stack(halves(cos_m) + halves(sin_m)),
        "m_back": np.stack(halves(cos_m.T) + halves(sin_m.T)),
        "f": np.concatenate([np.stack(halves(cos_f) + halves(sin_f)), window, near]),
        "pack": np.stack(halves(packed)),
        "eighth": np.stack([cos_e, sin_e], 1).astype(np.float32),
        "tw_col": np.concatenate([cos_t, sin_t], 1).astype(np.float32),
        "tw_row": np.concatenate([cos_t, sin_t], 1).T.astype(np.float32).copy(),
    }


def pupil_count(size_grid):
    coords = np.arange(size_grid) * 2 - size_grid + 1
    inside = (coords[:, None] ** 2 + coords[None, :] ** 2) * 4 <= size_grid * size_grid
    return float(np.sum(inside))


class Layout:
    def __init__(self, mesh):
        self.dp = mesh.shape["dp"]
        self.y = min(4, self.dp // 2)
        self.zh = self.dp // (2 * self.y)
        self.sp = mesh.shape["sp"]
        self.sizes = (2, self.zh, self.y, 2, self.sp)
        self.mesh = jax.sharding.Mesh(mesh.devices.reshape(self.sizes), AXES)

    def move(self, x, where):
        pairs = []
        for spot in itertools.product(*[range(n) for n in self.sizes]):
            goal = where(*spot)
            if goal is not None:
                pairs.append((self.flat(spot), self.flat(goal)))
        return lax.ppermute(x, AXES, pairs)

    def flat(self, spot):
        at = 0
        for place, size in zip(spot, self.sizes):
            at = at * size + place % size
        return at


def split(x):
    high = x.astype(BF16)
    return high, (x - high.astype(F32)).astype(BF16)


def dot(a, b):
    return lax.dot_general(a, b, (((1,), (0,)), ((), ())), preferred_element_type=F32)


def by_right(x, w_high, w_low):
    high, low = split(x)
    return dot(high, w_high) + (dot(high, w_low) + dot(low, w_high))


def by_left(w_high, w_low, x):
    high, low = split(x)
    return dot(w_high, high) + (dot(w_low, high) + dot(w_high, low))


def dft_right(re, im, mats, sign):
    rows = re.shape[0]
    both = jnp.concatenate([re, im], 0)
    by_cos = by_right(both, mats[0], mats[1])
    by_sin = by_right(both, mats[2], mats[3]) * sign
    return by_cos[:rows] - by_sin[rows:], by_cos[rows:] + by_sin[:rows]


def dft_left(re, im, mats, sign):
    cols = re.shape[1]
    both = jnp.concatenate([re, im], 1)
    by_cos = by_left(mats[0], mats[1], both)
    by_sin = by_left(mats[2], mats[3], both) * sign
    return by_cos[:, :cols] - by_sin[:, cols:], by_cos[:, cols:] + by_sin[:, :cols]


def turned(re, im, quarter_turns):
    quarter_turns %= 4
    if quarter_turns == 0:
        return re, im
    if quarter_turns == 1:
        return -im, re
    if quarter_turns == 2:
        return -re, -im
    return im, -re


def times(re, im, cos, sin):
    return re * cos - im * sin, re * sin + im * cos


def cos_sin(x):
    n = jnp.floor(x * (2.0 / np.pi) + 0.5)
    r = x - n * 1.5707963109016418
    r = r - n * 1.5893254712295857e-8
    q = n.astype(jnp.int32) & 3
    z = r * r
    sn = r + r * z * (-1.6666654611e-1 + z * (8.3321608736e-3 + z * -1.9515295891e-4))
    cs = 1.0 - 0.5 * z + z * z * (
        4.166664568298827e-2 + z * (-1.388731625493765e-3 + z * 2.443315711809948e-5)
    )
    odd = (q & 1) == 1
    c0 = jnp.where(odd, sn, cs)
    s0 = jnp.where(odd, cs, sn)
    cos = jnp.where((q == 1) | (q == 2), -c0, c0)
    sin = jnp.where(q >= 2, -s0, s0)
    return cos, sin


def spot_of(idx, d, e=0):
    return lax.rem(idx[0] + d, 4), lax.rem(idx[1] + e, 2)


def from_of(idx, d, e=0):
    return lax.rem(idx[0] + 4 - d, 4), lax.rem(idx[1] + 2 - e, 2)


def aligned(x, by):
    return pl.multiple_of(x * by, by)


def call(kernel, operands, in_smem, outs, scratch=(), apart=()):
    specs = []
    for at in range(len(operands)):
        space = pltpu.SMEM if at in in_smem else pltpu.VMEM
        specs.append(pl.BlockSpec(memory_space=pltpu.HBM if at in apart else space))
    return pl.pallas_call(
        kernel,
        out_shape=[jax.ShapeDtypeStruct(shape, F32) for shape in outs],
        in_specs=specs,
        out_specs=[pl.BlockSpec(memory_space=pltpu.VMEM) for _ in outs],
        scratch_shapes=list(scratch),
        compiler_params=pltpu.CompilerParams(vmem_limit_bytes=20 * 1024 * 1024),
    )(*operands)


relations = [(d, e) for e in range(2) for d in range(4)]


def ratio_of(wave):
    return 550.0 / (400.0 + 10.0 * jnp.full((8, 128), wave, jnp.int32).astype(F32))


def mats_of(ref):
    return ref[0], ref[1], ref[2], ref[3]


def phase_kernel(idx, phases, own0, own1, sent0, sent1, grid):
    grid[...] = jnp.transpose(phases[...])
    kept = aligned(jnp.where(idx[0] == 1, 1, 0), 128)
    given = aligned(jnp.where(idx[0] == 1, 0, 1), 128)
    own0[...] = grid[pl.ds(kept, 128), 0:256]
    own1[...] = grid[pl.ds(kept, 128), 256:512]
    sent0[...] = grid[pl.ds(given, 128), 0:256]
    sent1[...] = grid[pl.ds(given, 128), 256:512]


def scene_kernel(idx, scene, other, w, out, strip, edge, image, grid):
    owner = idx[2] == 1
    c = idx[1]
    part = pl.ds(aligned(15 * c, 8), 136)
    rows = jnp.where(owner, scene[0, part, :], other[0, part, :])
    strip[...] = rows[:, 256:384]
    edge[...] = jnp.where(c == 0, rows[0:8, 256:384], rows[128:136, 256:384])
    image[...] = jnp.transpose(jnp.where(c == 0, rows[0:128], rows[8:136]))
    spectrum = by_left(w[0], w[1], image[...])
    grid[0] = spectrum[:512]
    grid[1] = spectrum[512:]
    eight_rows(out, grid)


def pupil_kernel(idx, *refs):
    m, e, o0, o1, o2, o3, pupil, grid = refs[8:]
    s = idx[0]
    c = idx[1]
    owner = idx[2] == 1
    central = (s == 1) | (s == 2)
    own = jnp.concatenate([refs[0][...], refs[1][...]], 1)
    got = jnp.concatenate([refs[2][...], refs[3][...]], 1)
    own_far = jnp.concatenate([refs[4][...], refs[5][...]], 1)
    got_far = jnp.concatenate([refs[6][...], refs[7][...]], 1)
    phase = jnp.where(central, jnp.where(owner, own, own_far), jnp.where(owner, got, got_far))
    rows = lax.broadcasted_iota(jnp.int32, (128, 512), 0) + s * 128
    cols = lax.broadcasted_iota(jnp.int32, (128, 512), 1)
    across = (rows + 256) * 2 - N + 1
    down = (cols + 256) * 2 - N + 1
    inside = (down * down + across * across) * 4 <= N * N
    cos, sin = cos_sin(phase)
    re = jnp.where(inside, cos, 0.0)
    im = jnp.where(inside, sin, 0.0)
    pupil[0] = re
    pupil[1] = im
    re, im = times(re, im, e[c, 0:1, :], -e[c, 1:2, :])
    out_re, out_im = dft_right(re, im, mats_of(m), -1.0)
    grid[0] = out_re
    grid[1] = out_im
    for d, out in enumerate((o0, o1, o2, o3)):
        to = spot_of(idx, d)[0]
        out[...] = grid[:, :, pl.ds(aligned(to, 128), 128)]


def eight_rows(out, grid):
    for c in range(2):
        for s in range(4):
            row = 128 * s + 64 * c
            out[4 * c + s, 0:2] = grid[:, row : row + 64, :]


def eight_columns(out, grid):
    for c in range(2):
        for s in range(4):
            col = 128 * (2 * s + c)
            out[4 * c + s] = grid[:, :, col : col + 128]


def optics_kernel(scale, idx, b0, b1, b2, b3, scene, *refs):
    f, tw, far, out, grid = refs
    for d, block in enumerate((b0, b1, b2, b3)):
        grid[:, pl.ds(aligned(from_of(idx, d)[0], 128), 128), :] = block[...]
    low = (grid[0, :256, :], grid[1, :256, :])
    high = (grid[0, 256:, :], grid[1, 256:, :])
    twists = [(tw[:, r : r + 1], tw[:, 4 + r : 5 + r]) for r in range(4)]
    res, ims = [], []
    for r in range(4):
        add = turned(high[0], high[1], -r)
        re, im = low[0] + add[0], low[1] + add[1]
        if r:
            re, im = times(re, im, twists[r][0], -twists[r][1])
        res.append(re)
        ims.append(im)
    mats = mats_of(f)
    far_re, far_im = dft_left(
        jnp.concatenate(res, 1), jnp.concatenate(ims, 1), mats, -1.0
    )
    far[0] = far_re
    far[1] = far_im
    psf = scale * (far_re * far_re + far_im * far_im)
    psf_high, psf_low = split(psf)
    z_re = dot(mats[0], psf_high) + (dot(mats[1], psf_high) + dot(mats[0], psf_low))
    z_im = -(dot(mats[2], psf_high) + (dot(mats[3], psf_high) + dot(mats[2], psf_low)))
    first = [None, None]
    second = [None, None]
    nyquist = None
    for r in range(4):
        re = z_re[:, r * 128 : r * 128 + 128]
        im = z_im[:, r * 128 : r * 128 + 128]
        top = re[0:1, :]
        nyquist = top if r == 0 else (nyquist + top if r % 2 == 0 else nyquist - top)
        if r:
            re, im = times(re, im, twists[r][0], -twists[r][1])
        more = turned(re, im, -r)
        first = [re, im] if r == 0 else [first[0] + re, first[1] + im]
        second = list(more) if r == 0 else [second[0] + more[0], second[1] + more[1]]
    row = lax.broadcasted_iota(jnp.int32, (256, 128), 0)
    grid[0, :256, :] = first[0]
    grid[1, :256, :] = jnp.where(row == 0, nyquist, first[1])
    grid[0, 256:, :] = second[0]
    grid[1, 256:, :] = second[1]
    eight_rows(out, grid)
    for at in range(8):
        out[at, 2:4] = scene[at]


def unpack_rows(idx, re, im, tail):
    rows = lax.broadcasted_iota(jnp.int32, re.shape, 0)
    first = (idx[0] + idx[1]) == 0
    nyquist = jnp.where(first, im[0:1, :], 0.0)
    tail_rows = lax.broadcasted_iota(jnp.int32, (tail, re.shape[1]), 0)
    extra = jnp.where(tail_rows == 0, nyquist, 0.0)
    im = jnp.where((rows == 0) & first, 0.0, im)
    return jnp.concatenate([re, extra], 0), jnp.concatenate([im, jnp.zeros_like(extra)], 0)


def repack_rows(idx, re, im):
    first = (idx[0] + idx[1]) == 0
    rows = lax.broadcasted_iota(jnp.int32, (64, re.shape[1]), 0)
    return re[:64], jnp.where((rows == 0) & first, re[64:65, :], im[:64])


def row_transform(idx, blocks, first, mats, tw, grid):
    for c in range(2):
        for s in range(4):
            col = 128 * (2 * s + c)
            grid[:, :, col : col + 128] = blocks[4 * c + s, first : first + 2]
    return rows_out(idx, grid[0], grid[1], mats, tw)


def rows_back(idx, re, im, mats, tw, grid):
    re, im = dft_right(re, im, mats, 1.0)
    parts = []
    for r in range(4):
        a, b = re[r * 72 : r * 72 + 72], im[r * 72 : r * 72 + 72]
        if r:
            a, b = times(a, b, tw[r : r + 1, :], tw[4 + r : 5 + r, :])
        parts.append((a, b))
    for q in range(4):
        a, b = parts[0]
        for r in range(1, 4):
            more = turned(parts[r][0], parts[r][1], q * r)
            a = a + more[0]
            b = b + more[1]
        a, b = repack_rows(idx, a, b)
        grid[0, :, q * 256 : q * 256 + 256] = a
        grid[1, :, q * 256 : q * 256 + 256] = b


def rows_out(idx, re, im, mats, tw):
    re, im = unpack_rows(idx, re, im, 8)
    quarters = [(re[:, q * 256 : q * 256 + 256], im[:, q * 256 : q * 256 + 256]) for q in range(4)]
    sum02 = [quarters[0][p] + quarters[2][p] for p in range(2)]
    dif02 = [quarters[0][p] - quarters[2][p] for p in range(2)]
    sum13 = [quarters[1][p] + quarters[3][p] for p in range(2)]
    dif13 = [quarters[1][p] - quarters[3][p] for p in range(2)]
    step = turned(dif13[0], dif13[1], -1)
    parts = [
        (sum02[0] + sum13[0], sum02[1] + sum13[1]),
        (dif02[0] + step[0], dif02[1] + step[1]),
        (sum02[0] - sum13[0], sum02[1] - sum13[1]),
        (dif02[0] - step[0], dif02[1] - step[1]),
    ]
    for r in range(1, 4):
        parts[r] = times(parts[r][0], parts[r][1], tw[r : r + 1, :], -tw[4 + r : 5 + r, :])
    return dft_right(
        jnp.concatenate([p[0] for p in parts], 0),
        jnp.concatenate([p[1] for p in parts], 0),
        mats,
        -1.0,
    )


def blur_kernel(idx, blocks, f, tw, out, spectrum, grid, turned_grid):
    mats = mats_of(f)
    re, im = row_transform(idx, blocks, 2, mats, tw, grid)
    spectrum[0] = re
    spectrum[1] = im
    re, im = row_transform(idx, blocks, 0, mats, tw, grid)
    re, im = times(re, im, spectrum[0], spectrum[1])
    rows_back(idx, re, im, mats, tw, grid)
    both = jnp.transpose(jnp.concatenate([grid[0], grid[1]], 0))
    turned_grid[8 : N + 8, :] = both
    turned_grid[0:8, :] = both[N - 8 :, :]
    turned_grid[N + 8 :, :] = both[:8, :]
    for c in range(2):
        for s in range(4):
            row = 128 * (2 * s + c)
            out[4 * c + s] = turned_grid[row : row + ROWS, :]


def moved_lanes(x, e, lanes):
    if e == 0:
        return x
    rolled = pltpu.roll(x, (-e) % 128, 1)
    return jnp.where(lanes == (127 if e > 0 else 0), 0.0, rolled)


def moved_rows(x, a):
    if a == 0:
        return x
    return pltpu.roll(x, (-a) % x.shape[0], 0)


ROWS = 144


def row_pair(ref, row):
    parts = [ref[:, at : at + 8, :] for at in (row, row + 8)]
    return jnp.concatenate([part.reshape(part.shape[0] * 8, 128) for part in parts], 1)


def dot_rows(a, b):
    return lax.dot_general(a, b, (((1,), (1,)), ((), ())), preferred_element_type=F32)


def by_rows(a, b):
    a_high, a_low = split(a)
    b_high, b_low = split(b)
    return dot_rows(a_high, b_high) + (dot_rows(a_high, b_low) + dot_rows(a_low, b_high))


def same_rows(x):
    rows = lax.broadcasted_iota(jnp.int32, x.shape, 0)
    cols = lax.broadcasted_iota(jnp.int32, x.shape, 1)
    kept = jnp.where((rows & 7) == (cols & 7), x, 0.0)
    return jnp.sum(kept.reshape(32, 8, x.shape[1]), 1)


def net_kernel(pixel_count, idx, w1, b1, w2, *refs):
    blocks, f, strip, edge, g_out, sums_out = refs[:6]
    win_taps, g_taps, hidden, sums, g_pre = refs[6:]
    target = jnp.where(
        idx[1] == 0,
        jnp.concatenate([edge[...], strip[...]], 0),
        jnp.concatenate([strip[...], edge[...]], 0),
    )
    window = None
    for at in range(4):
        part = by_right(
            jnp.concatenate([blocks[2 * at], blocks[2 * at + 1]], 1),
            f[4 + at // 2, :, 128 * (at % 2) : 128 * (at % 2) + 128],
            f[6 + at // 2, :, 128 * (at % 2) : 128 * (at % 2) + 128],
        )
        window = part if window is None else window + part
    rows = lax.broadcasted_iota(jnp.int32, (ROWS, 128), 0)
    lanes = lax.broadcasted_iota(jnp.int32, (ROWS, 128), 1)
    row_global = rows + (2 * idx[0] + idx[1]) * 128 - 8
    inside = (row_global >= 0) & (row_global < N)
    window = jnp.where(inside, window, 0.0)
    for e in (-1, 0, 1):
        side = moved_lanes(window, e, lanes)
        for a in (-1, 0, 1):
            win_taps[3 * (a + 1) + e + 1] = moved_rows(side, a)
    step = 24
    for k in range(ROWS // step):
        part = pl.ds(k * step, step)

        def forward(c, total, part=part):
            pre = w1[c, 0] * win_taps[0, part, :]
            for t in range(1, 9):
                pre = pre + w1[c, t] * win_taps[t, part, :]
            hid = jnp.maximum(pre + b1[c], 0.0)
            hidden[c, part, :] = hid
            return tuple(total[t] + w2[t, c] * hid for t in range(9))

        total = lax.fori_loop(
            0, 32, forward, tuple(jnp.zeros((step, 128), F32) for _ in range(9)), unroll=4
        )
        for t in range(9):
            sums[t, part, :] = total[t]
    restored = window
    for e in (-1, 0, 1):
        side = None
        for a in (-1, 0, 1):
            part = moved_rows(jnp.where(inside, sums[3 * (a + 1) + e + 1], 0.0), a)
            side = part if side is None else side + part
        restored = restored + moved_lanes(side, e, lanes)
    residual = jnp.where(inside, restored - target, 0.0)
    own = (rows >= 8) & (rows < 136)
    own_residual = jnp.where(own, residual, 0.0)
    loss = jnp.sum(own_residual * own_residual, keepdims=True)
    g_restored = (2.0 / pixel_count) * residual
    for e in (-1, 0, 1):
        side = moved_lanes(g_restored, -e, lanes)
        for a in (-1, 0, 1):
            g_taps[3 * (a + 1) + e + 1] = jnp.where(inside, moved_rows(side, -a), 0.0)
    for k in range(ROWS // step):
        part = pl.ds(k * step, step)

        def backward(c, total, part=part):
            gh = w2[0, c] * g_taps[0, part, :]
            for t in range(1, 9):
                gh = gh + w2[t, c] * g_taps[t, part, :]
            gp = jnp.where(hidden[c, part, :] > 0.0, gh, 0.0)
            g_pre[c, part, :] = gp
            return tuple(total[t] + w1[c, t] * gp for t in range(9))

        total = lax.fori_loop(
            0, 32, backward, tuple(jnp.zeros((step, 128), F32) for _ in range(9)), unroll=4
        )
        for t in range(9):
            sums[t, part, :] = total[t]
    g_window = g_restored
    for e in (-1, 0, 1):
        side = None
        for a in (-1, 0, 1):
            part = moved_rows(sums[3 * (a + 1) + e + 1], -a)
            side = part if side is None else side + part
        g_window = g_window + moved_lanes(side, -e, lanes)
    g_out[...] = g_window[8:136]
    first, second = None, None
    for row in range(0, 128, 16):
        with_taps = jnp.concatenate(
            [row_pair(win_taps, row + 8), jnp.ones((8, 256), F32)], 0
        )
        one = by_rows(row_pair(g_pre, row + 8), with_taps)
        two = by_rows(row_pair(hidden, row + 8), row_pair(g_taps, row + 8))
        first = one if first is None else first + one
        second = two if second is None else second + two
    sums_out[...] = jnp.zeros_like(sums_out)
    sums_out[:, 0:80] = same_rows(first)
    sums_out[:, 80:88] = jnp.broadcast_to(loss * 0.125, (32, 8))
    sums_out[:, 128:200] = same_rows(second)


def otf_grad_kernel(idx, *refs):
    blocks = refs[:8]
    f, tw, spectrum, out, window, grid = refs[8:]
    for d, e in relations:
        s, c = from_of(idx, d, e)
        window[pl.ds(aligned(2 * s + c, 128), 128), :] = blocks[4 * e + d][...]
    rows = pl.ds(aligned(lax.rem(idx[0], 2), 128), 128)
    cols = pl.ds(aligned(idx[1], 128), 128)
    at = lax.div(idx[0], 2)
    packed = jnp.transpose(by_right(window[...], f[8 + at, rows, cols], f[10 + at, rows, cols]))
    mats = mats_of(f)
    re, im = rows_out(idx, packed[:64], packed[64:], mats, tw)
    re, im = times(re, im, spectrum[0], -spectrum[1])
    rows_back(idx, re, im, mats, tw, grid)
    eight_columns(out, grid)


def psf_grad_kernel(idx, blocks, far, f, tw, small, o0, o1, o2, o3, grid):
    for c in range(2):
        for s in range(4):
            grid[:, 128 * s + 64 * c : 128 * s + 64 * c + 64, :] = blocks[4 * c + s]
    row = lax.broadcasted_iota(jnp.int32, (256, 128), 0)
    zero_row = row == 0
    low_re, low_im = grid[0, :256, :], grid[1, :256, :]
    nyquist = jnp.where(zero_row, 0.5 * low_im, 0.0)
    low_re = jnp.where(zero_row, 0.5 * low_re, low_re)
    low_im = jnp.where(zero_row, 0.0, low_im)
    high = (grid[0, 256:, :], grid[1, 256:, :])
    twists = [(tw[:, r : r + 1], tw[:, 4 + r : 5 + r]) for r in range(4)]
    res, ims = [], []
    for r in range(4):
        add = turned(high[0], high[1], r)
        re, im = low_re + add[0], low_im + add[1]
        if r:
            re, im = times(re, im, twists[r][0], twists[r][1])
        re = re + nyquist if r % 2 == 0 else re - nyquist
        res.append(re)
        ims.append(im)
    mats = mats_of(f)
    g_psf = 2.0 * (
        by_left(mats[0], mats[1], jnp.concatenate(res, 1))
        - by_left(mats[2], mats[3], jnp.concatenate(ims, 1))
    )
    re, im = dft_left(g_psf * far[0], g_psf * far[1], mats, 1.0)
    first, second = None, None
    for r in range(4):
        a, b = re[:, r * 128 : r * 128 + 128], im[:, r * 128 : r * 128 + 128]
        if r:
            a, b = times(a, b, twists[r][0], twists[r][1])
        more = turned(a, b, r)
        first = [a, b] if r == 0 else [first[0] + a, first[1] + b]
        second = list(more) if r == 0 else [second[0] + more[0], second[1] + more[1]]
    for p in range(2):
        grid[p, :256, :] = first[p]
        grid[p, 256:, :] = second[p]
    for d, out in enumerate((o0, o1, o2, o3)):
        out[:, 0:128, :] = grid[:, pl.ds(aligned(spot_of(idx, d)[0], 128), 128), :]
        out[0, 128:136, :] = small[...]
        out[1, 128:136, :] = small[...]


def mask_grad_kernel(scale, idx, ids, got, *refs):
    b0, b1, b2, b3, m, e, pupil, keep, send, grid, whole = refs
    small = None
    for d, block in enumerate((b0, b1, b2, b3)):
        grid[:, :, pl.ds(aligned(from_of(idx, d)[0], 128), 128)] = block[:, 0:128, :]
        part = jnp.concatenate([block[0, 128:136, :], block[1, 128:136, :]], 1)
        small = part if small is None else small + part
    re, im = dft_right(grid[0], grid[1], mats_of(m), 1.0)
    re, im = times(re, im, e[idx[1], 0:1, :], e[idx[1], 1:2, :])
    factor = ratio_of(jnp.where(idx[2] == 1, ids[1], got[1]))[0:1, 0:1] * scale
    whole[...] = factor * (im * pupil[0] - re * pupil[1])
    keep[0:128, :] = whole[:, pl.ds(aligned(idx[1], 256), 256)]
    send[0:128, :] = whole[:, pl.ds(aligned(1 - idx[1], 256), 256)]
    keep[128:136, :] = small
    send[128:136, :] = small


def cut_kernel(ways, idx, keep, other, *refs):
    outs = refs[:ways]
    whole = refs[ways]
    whole[...] = keep[...] + other[...]
    piece = 128 // ways
    for d, out in enumerate(outs):
        to = lax.rem(idx[3] + d, ways)
        out[0:piece, :] = whole[pl.ds(aligned(to, piece), piece), :]
        out[piece : piece + 8, :] = whole[128:136, :]


def home_kernel(ways, pixel_count, idx, small, *refs):
    near, far, out, w1_out, b1_out, w2_out, loss_out, grid = refs
    piece = 128 // ways
    first = idx[1] == 0
    for y in range(ways):
        for h in range(2):
            row = 128 * h + piece * y
            a, b = near[y, h], far[y, h]
            grid[row : row + piece, 0:256] = jnp.where(first, a, b)
            grid[row : row + piece, 256:512] = jnp.where(first, b, a)
    central = (idx[0] == 1) | (idx[0] == 2)
    out[0:256, :] = jnp.zeros((256, 256), F32)
    out[768:1024, :] = jnp.zeros((256, 256), F32)
    out[256:768, :] = jnp.where(central, jnp.transpose(grid[...]), 0.0)
    flat = jnp.concatenate([small[:, 32 * g : 32 * g + 32] for g in range(4)], 0)
    w1_out[...] = flat[0:9, :]
    w2_out[...] = flat[16:25, :]
    b1_out[...] = flat[9:10, :]
    loss_out[...] = flat[10:11, 0:1] / pixel_count


def on_device(lay, phase_mask, height_offsets, sample_ids, wave_ids, scene, w1, b1, w2):
    con = constants()
    s = lax.axis_index("sp")
    c = lax.axis_index("core")
    y = lax.axis_index("y")
    owner = c == lax.axis_index("grp")
    pixel_count = float(lay.dp * N * 128)
    scale_psf = 1.0 / (N * N * pupil_count(N))
    idx = jnp.stack([s, c, owner.astype(jnp.int32), y]).astype(jnp.int32)

    def swap(g, zh, y, c, s):
        return (g, zh, y, 1 - c, s)

    def along_sp(blocks):
        return [blocks[0]] + [
            lay.move(blocks[d], lambda g, zh, y, c, s, d=d: (g, zh, y, c, s + d))
            for d in (1, 2, 3)
        ]

    def to_eight(blocks):
        return lax.all_to_all(blocks, ("core", "sp"), 0, 0, tiled=True)

    def gathered(block):
        near = along_sp([block] * 4)
        return near + [lay.move(part, swap) for part in near]

    ids = jnp.concatenate([sample_ids, wave_ids])
    got = lay.move(ids, swap)
    grabbed = lax.dynamic_slice(height_offsets, (ids[0], 256, 0), (1, 512, 256))[0]
    ratio = 550.0 / (400.0 + 10.0 * ids[1].astype(F32))
    phases = ratio * (phase_mask[256:768] + 0.1 * grabbed.astype(F32))

    mine = call(
        phase_kernel,
        (idx, phases),
        (0,),
        [(128, 256)] * 4,
        [pltpu.VMEM((256, 512), F32)],
    )
    pieces = list(mine[:2]) + [
        lay.move(
            block,
            lambda g, zh, y, c, s: (
                (g, zh, y, c, {1: 0, 2: 3}[s]) if s in (1, 2) and c == g else None
            ),
        )
        for block in mine[2:]
    ]
    pieces += [
        lay.move(
            block,
            lambda g, zh, y, c, s, inner=inner: (
                (g, zh, y, 1 - c, s) if c == g and (s in (1, 2)) == inner else None
            ),
        )
        for block, inner in zip(pieces, (True, True, False, False))
    ]

    other = lay.move(
        scene, lambda g, zh, y, c, s: (g, zh, y, 1 - c, s) if c == g else None
    )

    *field, pupil = call(
        pupil_kernel,
        (idx, *pieces, con["m"], con["eighth"]),
        (0,),
        [(2, 128, 128)] * 4 + [(2, 128, 512)],
        [pltpu.VMEM((2, 128, 512), F32)],
    )
    field = along_sp(field)

    scene_part, strip, edge = call(
        scene_kernel,
        (idx, scene, other, con["pack"]),
        (0,),
        [(8, 2, 64, 128), (136, 128), (8, 128)],
        [
            pltpu.VMEM((N, 128), F32),
            pltpu.VMEM((2, 512, 128), F32),
        ],
    )
    edge = lay.move(
        edge,
        lambda g, zh, y, c, s: (
            (g, zh, y, 1 - c, s - 1 + 2 * c) if 0 <= s - 1 + 2 * c < 4 else None
        ),
    )
    far, parts = call(
        functools.partial(optics_kernel, scale_psf),
        (idx, *field, scene_part, con["f"], con["tw_col"]),
        (0,),
        [(2, 256, 512), (8, 4, 64, 128)],
        [
            pltpu.VMEM((2, 512, 128), F32),
        ],
    )
    parts, edge = lax.optimization_barrier((to_eight(parts), edge))
    blurred, spectrum = call(
        blur_kernel,
        (idx, parts, con["f"], con["tw_row"]),
        (0,),
        [(8, ROWS, 128), (2, 288, 256)],
        [
            pltpu.VMEM((2, 64, N), F32),
            pltpu.VMEM((N + 16, 128), F32),
        ],
    )
    blurred = to_eight(blurred)
    g_window, sums = call(
        functools.partial(net_kernel, pixel_count),
        (idx, w1, b1, w2, blurred, con["f"], strip, edge),
        (0, 1, 2, 3),
        [(128, 128), (32, 256)],
        [
            pltpu.VMEM((9, ROWS, 128), F32),
            pltpu.VMEM((9, ROWS, 128), F32),
            pltpu.VMEM((32, ROWS, 128), F32),
            pltpu.VMEM((9, ROWS, 128), F32),
            pltpu.VMEM((32, ROWS, 128), F32),
        ],
    )
    small = jnp.sum(sums.reshape(32, 4, 8, 8), 3).transpose(2, 1, 0).reshape(8, 128)
    g_parts = gathered(g_window)
    (otf_grad,) = call(
        otf_grad_kernel,
        (idx, *g_parts, con["f"], con["tw_row"], spectrum),
        (0,),
        [(8, 2, 64, 128)],
        [
            pltpu.VMEM((N, 128), F32),
            pltpu.VMEM((2, 64, N), F32),
        ],
    )
    otf_grad = to_eight(otf_grad)
    field_grad = along_sp(
        call(
            psf_grad_kernel,
            (idx, otf_grad, far, con["f"], con["tw_col"], small),
            (0,),
            [(2, 136, 128)] * 4,
            [
                pltpu.VMEM((2, 512, 128), F32),
            ],
        )
    )
    keep, send = call(
        functools.partial(mask_grad_kernel, 2.0 * scale_psf),
        (idx, ids, got, *field_grad, con["m_back"], con["eighth"], pupil),
        (0, 1, 2),
        [(136, 256)] * 2,
        [
            pltpu.VMEM((2, 128, 512), F32),
            pltpu.VMEM((128, 512), F32),
        ],
    )

    piece = 128 // lay.y
    blocks = call(
        functools.partial(cut_kernel, lay.y),
        (idx, keep, lay.move(send, swap)),
        (0,),
        [(piece + 8, 256)] * lay.y,
        [pltpu.VMEM((136, 256), F32)],
    )
    total = blocks[0]
    for d in range(1, lay.y):
        total = total + lay.move(
            blocks[d], lambda g, zh, y, c, s, d=d: (g, zh, y + d, c, s)
        )
    total = total + lay.move(total, lambda g, zh, y, c, s: (1 - g, zh, y, c, s))
    part = total
    for d in range(1, lay.zh):
        total = total + lay.move(part, lambda g, zh, y, c, s, d=d: (g, zh + d, y, c, s))
    part = total[:piece]
    near_part = lay.move(
        part, lambda g, zh, y, c, s: (g, zh, y, c, {0: 1, 3: 2}[s]) if s in (0, 3) else None
    )
    home = jnp.where(s == 1, jnp.stack([near_part, part]), jnp.stack([part, near_part]))
    near = lax.all_to_all(
        jnp.broadcast_to(home, (lay.y, 2, piece, 256)), "y", 0, 0, tiled=True
    )
    far = lay.move(
        near, lambda g, zh, y, c, s: (g, zh, y, 1 - c, s) if s in (1, 2) else None
    )
    mask_grad, w1_grad, b1_grad, w2_grad, loss = call(
        functools.partial(home_kernel, lay.y, pixel_count),
        (idx, total[piece:], near, far),
        (0,),
        [(N, 256), (9, 32), (1, 32), (9, 32), (1, 1)],
        [pltpu.VMEM((256, 512), F32)],
    )
    return mask_grad, w1_grad.T, b1_grad.reshape(32), w2_grad, loss.reshape(())


def solution(mesh):
    lay = Layout(mesh)
    images = ("zh", "y", "core")
    placed = (
        P(None, "sp"),
        P(None, None, "sp"),
        P(images),
        P(images),
        P(images, "sp", None),
        P(),
        P(),
        P(),
    )
    return jax.shard_map(
        functools.partial(on_device, lay),
        mesh=lay.mesh,
        in_specs=placed,
        out_specs=(P(None, "sp"), P(), P(), P(), P()),
        check_vma=False,
    )
```

```python
import functools
import itertools

import jax
import jax.numpy as jnp
import ml_dtypes
import numpy as np
from jax import lax
from jax.experimental import pallas as pl
from jax.experimental.pallas import tpu as pltpu
from jax.sharding import PartitionSpec as P

N = 1024
F32 = jnp.float32
BF16 = jnp.bfloat16
AXES = ("grp", "zh", "y", "core", "sp")
taps = ((-1, -1), (-1, 0), (-1, 1), (0, -1), (0, 0), (0, 1), (1, -1), (1, 0), (1, 1))


def halves(matrix):
    high = matrix.astype(ml_dtypes.bfloat16)
    low = (matrix - high.astype(np.float64)).astype(ml_dtypes.bfloat16)
    return high, low


def trig(rows, cols, length):
    angle = 2.0 * np.pi * (np.outer(rows, cols) % length) / length
    return np.cos(angle), np.sin(angle)


@functools.lru_cache(None)
def constants():
    half = np.arange(512)
    quarter = np.arange(256)
    fours = np.arange(4)
    spread = (np.arange(4)[:, None] * 256 + np.arange(128)).reshape(-1)
    cos_m, sin_m = trig(half, spread, N)
    cos_f, sin_f = trig(quarter, quarter, 256)
    cos_w, sin_w = trig(half, np.arange(N), N)
    sin_w = -sin_w
    sin_w[0] = (-1.0) ** np.arange(N)
    packed = np.concatenate([cos_w, sin_w])
    weight = np.full((N,), 2.0)
    weight[0] = 1.0
    weight[512] = 1.0
    unpack = (packed * weight[:, None]).T / (N * N)
    blocks = [np.r_[64 * q : 64 * q + 64, 512 + 64 * q : 576 + 64 * q] for q in range(8)]
    by_at = np.concatenate([blocks[2 * s + c] for c in range(2) for s in range(4)])
    near = packed[np.concatenate(blocks), 256:384].reshape(8, 128, 128).transpose(0, 2, 1)
    window = np.stack(halves(unpack[256:384, by_at].T))
    window = window.reshape(4, 2, 256, 128).transpose(0, 2, 1, 3).reshape(4, 256, 256)
    near = np.stack(halves(near)).reshape(4, 2, 2, 128, 128)
    near = near.transpose(0, 1, 3, 2, 4).reshape(4, 256, 256)
    cos_e, sin_e = trig([0, 1], half, 8)
    cos_t, sin_t = trig(quarter, fours, N)
    return {
        "m": np.stack(halves(cos_m) + halves(sin_m)),
        "m_back": np.stack(halves(cos_m.T) + halves(sin_m.T)),
        "f": np.concatenate([np.stack(halves(cos_f) + halves(sin_f)), window, near]),
        "pack": np.stack(halves(packed)),
        "eighth": np.stack([cos_e, sin_e], 1).astype(np.float32),
        "tw_col": np.concatenate([cos_t, sin_t], 1).astype(np.float32),
        "tw_row": np.concatenate([cos_t, sin_t], 1).T.astype(np.float32).copy(),
    }


def pupil_count(size_grid):
    coords = np.arange(size_grid) * 2 - size_grid + 1
    inside = (coords[:, None] ** 2 + coords[None, :] ** 2) * 4 <= size_grid * size_grid
    return float(np.sum(inside))


class Layout:
    def __init__(self, mesh):
        self.dp = mesh.shape["dp"]
        self.y = min(4, self.dp // 2)
        self.zh = self.dp // (2 * self.y)
        self.sp = mesh.shape["sp"]
        self.sizes = (2, self.zh, self.y, 2, self.sp)
        self.mesh = jax.sharding.Mesh(mesh.devices.reshape(self.sizes), AXES)

    def move(self, x, where):
        pairs = []
        for spot in itertools.product(*[range(n) for n in self.sizes]):
            goal = where(*spot)
            if goal is not None:
                pairs.append((self.flat(spot), self.flat(goal)))
        return lax.ppermute(x, AXES, pairs)

    def flat(self, spot):
        at = 0
        for place, size in zip(spot, self.sizes):
            at = at * size + place % size
        return at


def split(x):
    high = x.astype(BF16)
    return high, (x - high.astype(F32)).astype(BF16)


def dot(a, b):
    return lax.dot_general(a, b, (((1,), (0,)), ((), ())), preferred_element_type=F32)


def by_right(x, w_high, w_low):
    high, low = split(x)
    return dot(high, w_high) + (dot(high, w_low) + dot(low, w_high))


def by_left(w_high, w_low, x):
    high, low = split(x)
    return dot(w_high, high) + (dot(w_low, high) + dot(w_high, low))


def dft_right(re, im, mats, sign):
    rows = re.shape[0]
    both = jnp.concatenate([re, im], 0)
    by_cos = by_right(both, mats[0], mats[1])
    by_sin = by_right(both, mats[2], mats[3]) * sign
    return by_cos[:rows] - by_sin[rows:], by_cos[rows:] + by_sin[:rows]


def dft_left(re, im, mats, sign):
    cols = re.shape[1]
    both = jnp.concatenate([re, im], 1)
    by_cos = by_left(mats[0], mats[1], both)
    by_sin = by_left(mats[2], mats[3], both) * sign
    return by_cos[:, :cols] - by_sin[:, cols:], by_cos[:, cols:] + by_sin[:, :cols]


def turned(re, im, quarter_turns):
    quarter_turns %= 4
    if quarter_turns == 0:
        return re, im
    if quarter_turns == 1:
        return -im, re
    if quarter_turns == 2:
        return -re, -im
    return im, -re


def times(re, im, cos, sin):
    return re * cos - im * sin, re * sin + im * cos


def cos_sin(x):
    n = jnp.floor(x * (2.0 / np.pi) + 0.5)
    r = x - n * 1.5707963109016418
    r = r - n * 1.5893254712295857e-8
    q = n.astype(jnp.int32) & 3
    z = r * r
    sn = r + r * z * (-1.6666654611e-1 + z * (8.3321608736e-3 + z * -1.9515295891e-4))
    cs = 1.0 - 0.5 * z + z * z * (
        4.166664568298827e-2 + z * (-1.388731625493765e-3 + z * 2.443315711809948e-5)
    )
    odd = (q & 1) == 1
    c0 = jnp.where(odd, sn, cs)
    s0 = jnp.where(odd, cs, sn)
    cos = jnp.where((q == 1) | (q == 2), -c0, c0)
    sin = jnp.where(q >= 2, -s0, s0)
    return cos, sin


def spot_of(idx, d, e=0):
    return lax.rem(idx[0] + d, 4), lax.rem(idx[1] + e, 2)


def from_of(idx, d, e=0):
    return lax.rem(idx[0] + 4 - d, 4), lax.rem(idx[1] + 2 - e, 2)


def aligned(x, by):
    return pl.multiple_of(x * by, by)


def call(kernel, operands, in_smem, outs, scratch=(), apart=()):
    specs = []
    for at in range(len(operands)):
        space = pltpu.SMEM if at in in_smem else pltpu.VMEM
        specs.append(pl.BlockSpec(memory_space=pltpu.HBM if at in apart else space))
    return pl.pallas_call(
        kernel,
        out_shape=[jax.ShapeDtypeStruct(shape, F32) for shape in outs],
        in_specs=specs,
        out_specs=[pl.BlockSpec(memory_space=pltpu.VMEM) for _ in outs],
        scratch_shapes=list(scratch),
        compiler_params=pltpu.CompilerParams(vmem_limit_bytes=20 * 1024 * 1024),
    )(*operands)


relations = [(d, e) for e in range(2) for d in range(4)]


def ratio_of(wave):
    return 550.0 / (400.0 + 10.0 * jnp.full((8, 128), wave, jnp.int32).astype(F32))


def mats_of(ref):
    return ref[0], ref[1], ref[2], ref[3]


def phase_kernel(idx, phases, own0, own1, sent0, sent1, grid):
    grid[...] = jnp.transpose(phases[...])
    kept = aligned(jnp.where(idx[0] == 1, 1, 0), 128)
    given = aligned(jnp.where(idx[0] == 1, 0, 1), 128)
    own0[...] = grid[pl.ds(kept, 128), 0:256]
    own1[...] = grid[pl.ds(kept, 128), 256:512]
    sent0[...] = grid[pl.ds(given, 128), 0:256]
    sent1[...] = grid[pl.ds(given, 128), 256:512]


def scene_kernel(idx, scene, other, w, out, strip, edge, image, grid):
    owner = idx[2] == 1
    c = idx[1]
    part = pl.ds(aligned(15 * c, 8), 136)
    rows = jnp.where(owner, scene[0, part, :], other[0, part, :])
    strip[...] = rows[:, 256:384]
    edge[...] = jnp.where(c == 0, rows[0:8, 256:384], rows[128:136, 256:384])
    image[...] = jnp.transpose(jnp.where(c == 0, rows[0:128], rows[8:136]))
    spectrum = by_left(w[0], w[1], image[...])
    grid[0] = spectrum[:512]
    grid[1] = spectrum[512:]
    eight_rows(out, grid)


def pupil_kernel(idx, *refs):
    m, e, o0, o1, o2, o3, pupil, grid = refs[8:]
    s = idx[0]
    c = idx[1]
    owner = idx[2] == 1
    central = (s == 1) | (s == 2)
    own = jnp.concatenate([refs[0][...], refs[1][...]], 1)
    got = jnp.concatenate([refs[2][...], refs[3][...]], 1)
    own_far = jnp.concatenate([refs[4][...], refs[5][...]], 1)
    got_far = jnp.concatenate([refs[6][...], refs[7][...]], 1)
    phase = jnp.where(central, jnp.where(owner, own, own_far), jnp.where(owner, got, got_far))
    rows = lax.broadcasted_iota(jnp.int32, (128, 512), 0) + s * 128
    cols = lax.broadcasted_iota(jnp.int32, (128, 512), 1)
    across = (rows + 256) * 2 - N + 1
    down = (cols + 256) * 2 - N + 1
    inside = (down * down + across * across) * 4 <= N * N
    cos, sin = cos_sin(phase)
    re = jnp.where(inside, cos, 0.0)
    im = jnp.where(inside, sin, 0.0)
    pupil[0] = re
    pupil[1] = im
    re, im = times(re, im, e[c, 0:1, :], -e[c, 1:2, :])
    out_re, out_im = dft_right(re, im, mats_of(m), -1.0)
    grid[0] = out_re
    grid[1] = out_im
    for d, out in enumerate((o0, o1, o2, o3)):
        to = spot_of(idx, d)[0]
        out[...] = grid[:, :, pl.ds(aligned(to, 128), 128)]


def eight_rows(out, grid):
    for c in range(2):
        for s in range(4):
            row = 128 * s + 64 * c
            out[4 * c + s, 0:2] = grid[:, row : row + 64, :]


def eight_columns(out, grid):
    for c in range(2):
        for s in range(4):
            col = 128 * (2 * s + c)
            out[4 * c + s] = grid[:, :, col : col + 128]


def optics_kernel(scale, idx, b0, b1, b2, b3, scene, *refs):
    f, tw, far, out, grid = refs
    for d, block in enumerate((b0, b1, b2, b3)):
        grid[:, pl.ds(aligned(from_of(idx, d)[0], 128), 128), :] = block[...]
    low = (grid[0, :256, :], grid[1, :256, :])
    high = (grid[0, 256:, :], grid[1, 256:, :])
    twists = [(tw[:, r : r + 1], tw[:, 4 + r : 5 + r]) for r in range(4)]
    res, ims = [], []
    for r in range(4):
        add = turned(high[0], high[1], -r)
        re, im = low[0] + add[0], low[1] + add[1]
        if r:
            re, im = times(re, im, twists[r][0], -twists[r][1])
        res.append(re)
        ims.append(im)
    mats = mats_of(f)
    far_re, far_im = dft_left(
        jnp.concatenate(res, 1), jnp.concatenate(ims, 1), mats, -1.0
    )
    far[0] = far_re
    far[1] = far_im
    psf = scale * (far_re * far_re + far_im * far_im)
    psf_high, psf_low = split(psf)
    z_re = dot(mats[0], psf_high) + (dot(mats[1], psf_high) + dot(mats[0], psf_low))
    z_im = -(dot(mats[2], psf_high) + (dot(mats[3], psf_high) + dot(mats[2], psf_low)))
    first = [None, None]
    second = [None, None]
    nyquist = None
    for r in range(4):
        re = z_re[:, r * 128 : r * 128 + 128]
        im = z_im[:, r * 128 : r * 128 + 128]
        top = re[0:1, :]
        nyquist = top if r == 0 else (nyquist + top if r % 2 == 0 else nyquist - top)
        if r:
            re, im = times(re, im, twists[r][0], -twists[r][1])
        more = turned(re, im, -r)
        first = [re, im] if r == 0 else [first[0] + re, first[1] + im]
        second = list(more) if r == 0 else [second[0] + more[0], second[1] + more[1]]
    row = lax.broadcasted_iota(jnp.int32, (256, 128), 0)
    grid[0, :256, :] = first[0]
    grid[1, :256, :] = jnp.where(row == 0, nyquist, first[1])
    grid[0, 256:, :] = second[0]
    grid[1, 256:, :] = second[1]
    eight_rows(out, grid)
    for at in range(8):
        out[at, 2:4] = scene[at]


def unpack_rows(idx, re, im, tail):
    rows = lax.broadcasted_iota(jnp.int32, re.shape, 0)
    first = (idx[0] + idx[1]) == 0
    nyquist = jnp.where(first, im[0:1, :], 0.0)
    tail_rows = lax.broadcasted_iota(jnp.int32, (tail, re.shape[1]), 0)
    extra = jnp.where(tail_rows == 0, nyquist, 0.0)
    im = jnp.where((rows == 0) & first, 0.0, im)
    return jnp.concatenate([re, extra], 0), jnp.concatenate([im, jnp.zeros_like(extra)], 0)


def repack_rows(idx, re, im):
    first = (idx[0] + idx[1]) == 0
    rows = lax.broadcasted_iota(jnp.int32, (64, re.shape[1]), 0)
    return re[:64], jnp.where((rows == 0) & first, re[64:65, :], im[:64])


def row_transform(idx, blocks, first, mats, tw, grid):
    for c in range(2):
        for s in range(4):
            col = 128 * (2 * s + c)
            grid[:, :, col : col + 128] = blocks[4 * c + s, first : first + 2]
    return rows_out(idx, grid[0], grid[1], mats, tw)


def rows_back(idx, re, im, mats, tw, grid):
    re, im = dft_right(re, im, mats, 1.0)
    parts = []
    for r in range(4):
        a, b = re[r * 72 : r * 72 + 72], im[r * 72 : r * 72 + 72]
        if r:
            a, b = times(a, b, tw[r : r + 1, :], tw[4 + r : 5 + r, :])
        parts.append((a, b))
    for q in range(4):
        a, b = parts[0]
        for r in range(1, 4):
            more = turned(parts[r][0], parts[r][1], q * r)
            a = a + more[0]
            b = b + more[1]
        a, b = repack_rows(idx, a, b)
        grid[0, :, q * 256 : q * 256 + 256] = a
        grid[1, :, q * 256 : q * 256 + 256] = b


def rows_out(idx, re, im, mats, tw):
    re, im = unpack_rows(idx, re, im, 8)
    quarters = [(re[:, q * 256 : q * 256 + 256], im[:, q * 256 : q * 256 + 256]) for q in range(4)]
    sum02 = [quarters[0][p] + quarters[2][p] for p in range(2)]
    dif02 = [quarters[0][p] - quarters[2][p] for p in range(2)]
    sum13 = [quarters[1][p] + quarters[3][p] for p in range(2)]
    dif13 = [quarters[1][p] - quarters[3][p] for p in range(2)]
    step = turned(dif13[0], dif13[1], -1)
    parts = [
        (sum02[0] + sum13[0], sum02[1] + sum13[1]),
        (dif02[0] + step[0], dif02[1] + step[1]),
        (sum02[0] - sum13[0], sum02[1] - sum13[1]),
        (dif02[0] - step[0], dif02[1] - step[1]),
    ]
    for r in range(1, 4):
        parts[r] = times(parts[r][0], parts[r][1], tw[r : r + 1, :], -tw[4 + r : 5 + r, :])
    return dft_right(
        jnp.concatenate([p[0] for p in parts], 0),
        jnp.concatenate([p[1] for p in parts], 0),
        mats,
        -1.0,
    )


def blur_kernel(idx, blocks, f, tw, out, spectrum, grid, turned_grid):
    mats = mats_of(f)
    re, im = row_transform(idx, blocks, 2, mats, tw, grid)
    spectrum[0] = re
    spectrum[1] = im
    re, im = row_transform(idx, blocks, 0, mats, tw, grid)
    re, im = times(re, im, spectrum[0], spectrum[1])
    rows_back(idx, re, im, mats, tw, grid)
    both = jnp.transpose(jnp.concatenate([grid[0], grid[1]], 0))
    turned_grid[8 : N + 8, :] = both
    turned_grid[0:8, :] = both[N - 8 :, :]
    turned_grid[N + 8 :, :] = both[:8, :]
    for c in range(2):
        for s in range(4):
            row = 128 * (2 * s + c)
            out[4 * c + s] = turned_grid[row : row + ROWS, :]


def moved_lanes(x, e, lanes):
    if e == 0:
        return x
    rolled = pltpu.roll(x, (-e) % 128, 1)
    return jnp.where(lanes == (127 if e > 0 else 0), 0.0, rolled)


def moved_rows(x, a):
    if a == 0:
        return x
    return pltpu.roll(x, (-a) % x.shape[0], 0)


ROWS = 144


def row_pair(ref, row):
    parts = [ref[:, at : at + 8, :] for at in (row, row + 8)]
    return jnp.concatenate([part.reshape(part.shape[0] * 8, 128) for part in parts], 1)


def dot_rows(a, b):
    return lax.dot_general(a, b, (((1,), (1,)), ((), ())), preferred_element_type=F32)


def by_rows(a, b):
    a_high, a_low = split(a)
    b_high, b_low = split(b)
    return dot_rows(a_high, b_high) + (dot_rows(a_high, b_low) + dot_rows(a_low, b_high))


def same_rows(x):
    rows = lax.broadcasted_iota(jnp.int32, x.shape, 0)
    cols = lax.broadcasted_iota(jnp.int32, x.shape, 1)
    kept = jnp.where((rows & 7) == (cols & 7), x, 0.0)
    return jnp.sum(kept.reshape(32, 8, x.shape[1]), 1)


def net_kernel(pixel_count, idx, w1, b1, w2, *refs):
    blocks, f, strip, edge, g_out, sums_out = refs[:6]
    win_taps, g_taps, hidden, sums, g_pre = refs[6:]
    target = jnp.where(
        idx[1] == 0,
        jnp.concatenate([edge[...], strip[...]], 0),
        jnp.concatenate([strip[...], edge[...]], 0),
    )
    window = None
    for at in range(4):
        part = by_right(
            jnp.concatenate([blocks[2 * at], blocks[2 * at + 1]], 1),
            f[4 + at // 2, :, 128 * (at % 2) : 128 * (at % 2) + 128],
            f[6 + at // 2, :, 128 * (at % 2) : 128 * (at % 2) + 128],
        )
        window = part if window is None else window + part
    rows = lax.broadcasted_iota(jnp.int32, (ROWS, 128), 0)
    lanes = lax.broadcasted_iota(jnp.int32, (ROWS, 128), 1)
    row_global = rows + (2 * idx[0] + idx[1]) * 128 - 8
    inside = (row_global >= 0) & (row_global < N)
    window = jnp.where(inside, window, 0.0)
    for e in (-1, 0, 1):
        side = moved_lanes(window, e, lanes)
        for a in (-1, 0, 1):
            win_taps[3 * (a + 1) + e + 1] = moved_rows(side, a)
    step = 48
    for k in range(ROWS // step):
        part = pl.ds(k * step, step)

        def forward(c, total, part=part):
            pre = w1[c, 0] * win_taps[0, part, :]
            for t in range(1, 9):
                pre = pre + w1[c, t] * win_taps[t, part, :]
            hid = jnp.maximum(pre + b1[c], 0.0)
            hidden[c, part, :] = hid
            return tuple(total[t] + w2[t, c] * hid for t in range(9))

        total = lax.fori_loop(
            0, 32, forward, tuple(jnp.zeros((step, 128), F32) for _ in range(9)), unroll=32
        )
        for t in range(9):
            sums[t, part, :] = total[t]
    restored = window
    for e in (-1, 0, 1):
        side = None
        for a in (-1, 0, 1):
            part = moved_rows(jnp.where(inside, sums[3 * (a + 1) + e + 1], 0.0), a)
            side = part if side is None else side + part
        restored = restored + moved_lanes(side, e, lanes)
    residual = jnp.where(inside, restored - target, 0.0)
    own = (rows >= 8) & (rows < 136)
    own_residual = jnp.where(own, residual, 0.0)
    loss = jnp.sum(own_residual * own_residual, keepdims=True)
    g_restored = (2.0 / pixel_count) * residual
    for e in (-1, 0, 1):
        side = moved_lanes(g_restored, -e, lanes)
        for a in (-1, 0, 1):
            g_taps[3 * (a + 1) + e + 1] = jnp.where(inside, moved_rows(side, -a), 0.0)
    for k in range(ROWS // step):
        part = pl.ds(k * step, step)

        def backward(c, total, part=part):
            gh = w2[0, c] * g_taps[0, part, :]
            for t in range(1, 9):
                gh = gh + w2[t, c] * g_taps[t, part, :]
            gp = jnp.where(hidden[c, part, :] > 0.0, gh, 0.0)
            g_pre[c, part, :] = gp
            return tuple(total[t] + w1[c, t] * gp for t in range(9))

        total = lax.fori_loop(
            0, 32, backward, tuple(jnp.zeros((step, 128), F32) for _ in range(9)), unroll=32
        )
        for t in range(9):
            sums[t, part, :] = total[t]
    g_window = g_restored
    for e in (-1, 0, 1):
        side = None
        for a in (-1, 0, 1):
            part = moved_rows(sums[3 * (a + 1) + e + 1], -a)
            side = part if side is None else side + part
        g_window = g_window + moved_lanes(side, -e, lanes)
    g_out[...] = g_window[8:136]
    first, second = None, None
    for row in range(0, 128, 16):
        with_taps = jnp.concatenate(
            [row_pair(win_taps, row + 8), jnp.ones((8, 256), F32)], 0
        )
        one = by_rows(row_pair(g_pre, row + 8), with_taps)
        two = by_rows(row_pair(hidden, row + 8), row_pair(g_taps, row + 8))
        first = one if first is None else first + one
        second = two if second is None else second + two
    sums_out[...] = jnp.zeros_like(sums_out)
    sums_out[:, 0:80] = same_rows(first)
    sums_out[:, 80:88] = jnp.broadcast_to(loss * 0.125, (32, 8))
    sums_out[:, 128:200] = same_rows(second)


def otf_grad_kernel(idx, *refs):
    blocks = refs[:8]
    f, tw, spectrum, out, window, grid = refs[8:]
    for d, e in relations:
        s, c = from_of(idx, d, e)
        window[pl.ds(aligned(2 * s + c, 128), 128), :] = blocks[4 * e + d][...]
    rows = pl.ds(aligned(lax.rem(idx[0], 2), 128), 128)
    cols = pl.ds(aligned(idx[1], 128), 128)
    at = lax.div(idx[0], 2)
    packed = jnp.transpose(by_right(window[...], f[8 + at, rows, cols], f[10 + at, rows, cols]))
    mats = mats_of(f)
    re, im = rows_out(idx, packed[:64], packed[64:], mats, tw)
    re, im = times(re, im, spectrum[0], -spectrum[1])
    rows_back(idx, re, im, mats, tw, grid)
    eight_columns(out, grid)


def psf_grad_kernel(idx, blocks, far, f, tw, small, o0, o1, o2, o3, grid):
    for c in range(2):
        for s in range(4):
            grid[:, 128 * s + 64 * c : 128 * s + 64 * c + 64, :] = blocks[4 * c + s]
    row = lax.broadcasted_iota(jnp.int32, (256, 128), 0)
    zero_row = row == 0
    low_re, low_im = grid[0, :256, :], grid[1, :256, :]
    nyquist = jnp.where(zero_row, 0.5 * low_im, 0.0)
    low_re = jnp.where(zero_row, 0.5 * low_re, low_re)
    low_im = jnp.where(zero_row, 0.0, low_im)
    high = (grid[0, 256:, :], grid[1, 256:, :])
    twists = [(tw[:, r : r + 1], tw[:, 4 + r : 5 + r]) for r in range(4)]
    res, ims = [], []
    for r in range(4):
        add = turned(high[0], high[1], r)
        re, im = low_re + add[0], low_im + add[1]
        if r:
            re, im = times(re, im, twists[r][0], twists[r][1])
        re = re + nyquist if r % 2 == 0 else re - nyquist
        res.append(re)
        ims.append(im)
    mats = mats_of(f)
    g_psf = 2.0 * (
        by_left(mats[0], mats[1], jnp.concatenate(res, 1))
        - by_left(mats[2], mats[3], jnp.concatenate(ims, 1))
    )
    re, im = dft_left(g_psf * far[0], g_psf * far[1], mats, 1.0)
    first, second = None, None
    for r in range(4):
        a, b = re[:, r * 128 : r * 128 + 128], im[:, r * 128 : r * 128 + 128]
        if r:
            a, b = times(a, b, twists[r][0], twists[r][1])
        more = turned(a, b, r)
        first = [a, b] if r == 0 else [first[0] + a, first[1] + b]
        second = list(more) if r == 0 else [second[0] + more[0], second[1] + more[1]]
    for p in range(2):
        grid[p, :256, :] = first[p]
        grid[p, 256:, :] = second[p]
    for d, out in enumerate((o0, o1, o2, o3)):
        out[:, 0:128, :] = grid[:, pl.ds(aligned(spot_of(idx, d)[0], 128), 128), :]
        out[0, 128:136, :] = small[...]
        out[1, 128:136, :] = small[...]


def mask_grad_kernel(scale, idx, ids, got, *refs):
    b0, b1, b2, b3, m, e, pupil, keep, send, grid, whole = refs
    small = None
    for d, block in enumerate((b0, b1, b2, b3)):
        grid[:, :, pl.ds(aligned(from_of(idx, d)[0], 128), 128)] = block[:, 0:128, :]
        part = jnp.concatenate([block[0, 128:136, :], block[1, 128:136, :]], 1)
        small = part if small is None else small + part
    re, im = dft_right(grid[0], grid[1], mats_of(m), 1.0)
    re, im = times(re, im, e[idx[1], 0:1, :], e[idx[1], 1:2, :])
    factor = ratio_of(jnp.where(idx[2] == 1, ids[1], got[1]))[0:1, 0:1] * scale
    whole[...] = factor * (im * pupil[0] - re * pupil[1])
    keep[0:128, :] = whole[:, pl.ds(aligned(idx[1], 256), 256)]
    send[0:128, :] = whole[:, pl.ds(aligned(1 - idx[1], 256), 256)]
    keep[128:136, :] = small
    send[128:136, :] = small


def cut_kernel(ways, idx, keep, other, *refs):
    outs = refs[:ways]
    whole = refs[ways]
    whole[...] = keep[...] + other[...]
    piece = 128 // ways
    for d, out in enumerate(outs):
        to = lax.rem(idx[3] + d, ways)
        out[0:piece, :] = whole[pl.ds(aligned(to, piece), piece), :]
        out[piece : piece + 8, :] = whole[128:136, :]


def home_kernel(ways, pixel_count, idx, small, *refs):
    near, far, out, w1_out, b1_out, w2_out, loss_out, grid = refs
    piece = 128 // ways
    first = idx[1] == 0
    for y in range(ways):
        for h in range(2):
            row = 128 * h + piece * y
            a, b = near[y, h], far[y, h]
            grid[row : row + piece, 0:256] = jnp.where(first, a, b)
            grid[row : row + piece, 256:512] = jnp.where(first, b, a)
    central = (idx[0] == 1) | (idx[0] == 2)
    out[0:256, :] = jnp.zeros((256, 256), F32)
    out[768:1024, :] = jnp.zeros((256, 256), F32)
    out[256:768, :] = jnp.where(central, jnp.transpose(grid[...]), 0.0)
    flat = jnp.concatenate([small[:, 32 * g : 32 * g + 32] for g in range(4)], 0)
    w1_out[...] = flat[0:9, :]
    w2_out[...] = flat[16:25, :]
    b1_out[...] = flat[9:10, :]
    loss_out[...] = flat[10:11, 0:1] / pixel_count


def on_device(lay, phase_mask, height_offsets, sample_ids, wave_ids, scene, w1, b1, w2):
    con = constants()
    s = lax.axis_index("sp")
    c = lax.axis_index("core")
    y = lax.axis_index("y")
    owner = c == lax.axis_index("grp")
    pixel_count = float(lay.dp * N * 128)
    scale_psf = 1.0 / (N * N * pupil_count(N))
    idx = jnp.stack([s, c, owner.astype(jnp.int32), y]).astype(jnp.int32)

    def swap(g, zh, y, c, s):
        return (g, zh, y, 1 - c, s)

    def along_sp(blocks):
        return [blocks[0]] + [
            lay.move(blocks[d], lambda g, zh, y, c, s, d=d: (g, zh, y, c, s + d))
            for d in (1, 2, 3)
        ]

    def to_eight(blocks):
        return lax.all_to_all(blocks, ("core", "sp"), 0, 0, tiled=True)

    def gathered(block):
        near = along_sp([block] * 4)
        return near + [lay.move(part, swap) for part in near]

    ids = jnp.concatenate([sample_ids, wave_ids])
    got = lay.move(ids, swap)
    grabbed = lax.dynamic_slice(height_offsets, (ids[0], 256, 0), (1, 512, 256))[0]
    ratio = 550.0 / (400.0 + 10.0 * ids[1].astype(F32))
    phases = ratio * (phase_mask[256:768] + 0.1 * grabbed.astype(F32))

    mine = call(
        phase_kernel,
        (idx, phases),
        (0,),
        [(128, 256)] * 4,
        [pltpu.VMEM((256, 512), F32)],
    )
    pieces = list(mine[:2]) + [
        lay.move(
            block,
            lambda g, zh, y, c, s: (
                (g, zh, y, c, {1: 0, 2: 3}[s]) if s in (1, 2) and c == g else None
            ),
        )
        for block in mine[2:]
    ]
    pieces += [
        lay.move(
            block,
            lambda g, zh, y, c, s, inner=inner: (
                (g, zh, y, 1 - c, s) if c == g and (s in (1, 2)) == inner else None
            ),
        )
        for block, inner in zip(pieces, (True, True, False, False))
    ]


    *field, pupil = call(
        pupil_kernel,
        (idx, *pieces, con["m"], con["eighth"]),
        (0,),
        [(2, 128, 128)] * 4 + [(2, 128, 512)],
        [pltpu.VMEM((2, 128, 512), F32)],
    )
    scene, pupil = lax.optimization_barrier((scene, pupil))
    other = lay.move(
        scene, lambda g, zh, y, c, s: (g, zh, y, 1 - c, s) if c == g else None
    )
    field = along_sp(field)

    scene_part, strip, edge = call(
        scene_kernel,
        (idx, scene, other, con["pack"]),
        (0,),
        [(8, 2, 64, 128), (136, 128), (8, 128)],
        [
            pltpu.VMEM((N, 128), F32),
            pltpu.VMEM((2, 512, 128), F32),
        ],
    )
    edge = lay.move(
        edge,
        lambda g, zh, y, c, s: (
            (g, zh, y, 1 - c, s - 1 + 2 * c) if 0 <= s - 1 + 2 * c < 4 else None
        ),
    )
    far, parts = call(
        functools.partial(optics_kernel, scale_psf),
        (idx, *field, scene_part, con["f"], con["tw_col"]),
        (0,),
        [(2, 256, 512), (8, 4, 64, 128)],
        [
            pltpu.VMEM((2, 512, 128), F32),
        ],
    )
    parts, edge = lax.optimization_barrier((to_eight(parts), edge))
    blurred, spectrum = call(
        blur_kernel,
        (idx, parts, con["f"], con["tw_row"]),
        (0,),
        [(8, ROWS, 128), (2, 288, 256)],
        [
            pltpu.VMEM((2, 64, N), F32),
            pltpu.VMEM((N + 16, 128), F32),
        ],
    )
    blurred = to_eight(blurred)
    g_window, sums = call(
        functools.partial(net_kernel, pixel_count),
        (idx, w1, b1, w2, blurred, con["f"], strip, edge),
        (0, 1, 2, 3),
        [(128, 128), (32, 256)],
        [
            pltpu.VMEM((9, ROWS, 128), F32),
            pltpu.VMEM((9, ROWS, 128), F32),
            pltpu.VMEM((32, ROWS, 128), F32),
            pltpu.VMEM((9, ROWS, 128), F32),
            pltpu.VMEM((32, ROWS, 128), F32),
        ],
    )
    small = jnp.sum(sums.reshape(32, 4, 8, 8), 3).transpose(2, 1, 0).reshape(8, 128)
    g_parts = gathered(g_window)
    (otf_grad,) = call(
        otf_grad_kernel,
        (idx, *g_parts, con["f"], con["tw_row"], spectrum),
        (0,),
        [(8, 2, 64, 128)],
        [
            pltpu.VMEM((N, 128), F32),
            pltpu.VMEM((2, 64, N), F32),
        ],
    )
    otf_grad = to_eight(otf_grad)
    field_grad = along_sp(
        call(
            psf_grad_kernel,
            (idx, otf_grad, far, con["f"], con["tw_col"], small),
            (0,),
            [(2, 136, 128)] * 4,
            [
                pltpu.VMEM((2, 512, 128), F32),
            ],
        )
    )
    keep, send = call(
        functools.partial(mask_grad_kernel, 2.0 * scale_psf),
        (idx, ids, got, *field_grad, con["m_back"], con["eighth"], pupil),
        (0, 1, 2),
        [(136, 256)] * 2,
        [
            pltpu.VMEM((2, 128, 512), F32),
            pltpu.VMEM((128, 512), F32),
        ],
    )

    piece = 128 // lay.y
    blocks = call(
        functools.partial(cut_kernel, lay.y),
        (idx, keep, lay.move(send, swap)),
        (0,),
        [(piece + 8, 256)] * lay.y,
        [pltpu.VMEM((136, 256), F32)],
    )
    total = blocks[0]
    for d in range(1, lay.y):
        total = total + lay.move(
            blocks[d], lambda g, zh, y, c, s, d=d: (g, zh, y + d, c, s)
        )
    total = total + lay.move(total, lambda g, zh, y, c, s: (1 - g, zh, y, c, s))
    part = total
    for d in range(1, lay.zh):
        total = total + lay.move(part, lambda g, zh, y, c, s, d=d: (g, zh + d, y, c, s))
    part = total[:piece]
    near_part = lay.move(
        part, lambda g, zh, y, c, s: (g, zh, y, c, {0: 1, 3: 2}[s]) if s in (0, 3) else None
    )
    home = jnp.where(s == 1, jnp.stack([near_part, part]), jnp.stack([part, near_part]))
    near = lax.all_to_all(
        jnp.broadcast_to(home, (lay.y, 2, piece, 256)), "y", 0, 0, tiled=True
    )
    far = lay.move(
        near, lambda g, zh, y, c, s: (g, zh, y, 1 - c, s) if s in (1, 2) else None
    )
    mask_grad, w1_grad, b1_grad, w2_grad, loss = call(
        functools.partial(home_kernel, lay.y, pixel_count),
        (idx, total[piece:], near, far),
        (0,),
        [(N, 256), (9, 32), (1, 32), (9, 32), (1, 1)],
        [pltpu.VMEM((256, 512), F32)],
    )
    return mask_grad, w1_grad.T, b1_grad.reshape(32), w2_grad, loss.reshape(())


def solution(mesh):
    lay = Layout(mesh)
    images = ("zh", "y", "core")
    placed = (
        P(None, "sp"),
        P(None, None, "sp"),
        P(images),
        P(images),
        P(images, "sp", None),
        P(),
        P(),
        P(),
    )
    return jax.shard_map(
        functools.partial(on_device, lay),
        mesh=lay.mesh,
        in_specs=placed,
        out_specs=(P(None, "sp"), P(), P(), P(), P()),
        check_vma=False,
    )
```

```python
import functools
import itertools

import jax
import jax.numpy as jnp
import ml_dtypes
import numpy as np
from jax import lax
from jax.experimental import pallas as pl
from jax.experimental.pallas import tpu as pltpu
from jax.sharding import PartitionSpec as P

N = 1024
F32 = jnp.float32
BF16 = jnp.bfloat16
AXES = ("grp", "zh", "y", "core", "sp")
taps = ((-1, -1), (-1, 0), (-1, 1), (0, -1), (0, 0), (0, 1), (1, -1), (1, 0), (1, 1))


def halves(matrix):
    high = matrix.astype(ml_dtypes.bfloat16)
    low = (matrix - high.astype(np.float64)).astype(ml_dtypes.bfloat16)
    return high, low


def trig(rows, cols, length):
    angle = 2.0 * np.pi * (np.outer(rows, cols) % length) / length
    return np.cos(angle), np.sin(angle)


@functools.lru_cache(None)
def constants():
    half = np.arange(512)
    quarter = np.arange(256)
    fours = np.arange(4)
    spread = (np.arange(4)[:, None] * 256 + np.arange(128)).reshape(-1)
    cos_m, sin_m = trig(half, spread, N)
    cos_f, sin_f = trig(quarter, quarter, 256)
    cos_w, sin_w = trig(half, np.arange(N), N)
    sin_w = -sin_w
    sin_w[0] = (-1.0) ** np.arange(N)
    packed = np.concatenate([cos_w, sin_w])
    weight = np.full((N,), 2.0)
    weight[0] = 1.0
    weight[512] = 1.0
    unpack = (packed * weight[:, None]).T / (N * N)
    blocks = [np.r_[64 * q : 64 * q + 64, 512 + 64 * q : 576 + 64 * q] for q in range(8)]
    by_at = np.concatenate([blocks[2 * s + c] for c in range(2) for s in range(4)])
    near = packed[np.concatenate(blocks), 256:384].reshape(8, 128, 128).transpose(0, 2, 1)
    window = np.stack(halves(unpack[256:384, by_at].T))
    window = window.reshape(4, 2, 256, 128).transpose(0, 2, 1, 3).reshape(4, 256, 256)
    near = np.stack(halves(near)).reshape(4, 2, 2, 128, 128)
    near = near.transpose(0, 1, 3, 2, 4).reshape(4, 256, 256)
    cos_t, sin_t = trig(quarter, fours, N)
    return {
        "m": np.stack(halves(cos_m) + halves(sin_m)),
        "m_back": np.stack(halves(cos_m.T) + halves(sin_m.T)),
        "f": np.concatenate([np.stack(halves(cos_f) + halves(sin_f)), window, near]),
        "pack": np.stack(halves(packed)),
        "tw_col": np.concatenate([cos_t, sin_t], 1).astype(np.float32),
        "tw_row": np.concatenate([cos_t, sin_t], 1).T.astype(np.float32).copy(),
    }


def pupil_count(size_grid):
    coords = np.arange(size_grid) * 2 - size_grid + 1
    inside = (coords[:, None] ** 2 + coords[None, :] ** 2) * 4 <= size_grid * size_grid
    return float(np.sum(inside))


class Layout:
    def __init__(self, mesh):
        self.dp = mesh.shape["dp"]
        self.y = min(4, self.dp // 2)
        self.zh = self.dp // (2 * self.y)
        self.sp = mesh.shape["sp"]
        self.sizes = (2, self.zh, self.y, 2, self.sp)
        self.mesh = jax.sharding.Mesh(mesh.devices.reshape(self.sizes), AXES)

    def move(self, x, where):
        pairs = []
        for spot in itertools.product(*[range(n) for n in self.sizes]):
            goal = where(*spot)
            if goal is not None:
                pairs.append((self.flat(spot), self.flat(goal)))
        return lax.ppermute(x, AXES, pairs)

    def flat(self, spot):
        at = 0
        for place, size in zip(spot, self.sizes):
            at = at * size + place % size
        return at


def split(x):
    high = x.astype(BF16)
    return high, (x - high.astype(F32)).astype(BF16)


def dot(a, b):
    return lax.dot_general(a, b, (((1,), (0,)), ((), ())), preferred_element_type=F32)


def by_right(x, w_high, w_low):
    high, low = split(x)
    return dot(high, w_high) + (dot(high, w_low) + dot(low, w_high))


def by_left(w_high, w_low, x):
    high, low = split(x)
    return dot(w_high, high) + (dot(w_low, high) + dot(w_high, low))


def dft_right(re, im, mats, sign):
    rows = re.shape[0]
    both = jnp.concatenate([re, im], 0)
    by_cos = by_right(both, mats[0], mats[1])
    by_sin = by_right(both, mats[2], mats[3]) * sign
    return by_cos[:rows] - by_sin[rows:], by_cos[rows:] + by_sin[:rows]


def dft_left(re, im, mats, sign):
    cols = re.shape[1]
    both = jnp.concatenate([re, im], 1)
    by_cos = by_left(mats[0], mats[1], both)
    by_sin = by_left(mats[2], mats[3], both) * sign
    return by_cos[:, :cols] - by_sin[:, cols:], by_cos[:, cols:] + by_sin[:, :cols]


def turned(re, im, quarter_turns):
    quarter_turns %= 4
    if quarter_turns == 0:
        return re, im
    if quarter_turns == 1:
        return -im, re
    if quarter_turns == 2:
        return -re, -im
    return im, -re


def times(re, im, cos, sin):
    return re * cos - im * sin, re * sin + im * cos


def cos_sin(x):
    n = jnp.floor(x * (2.0 / np.pi) + 0.5)
    r = x - n * 1.5707963109016418
    r = r - n * 1.5893254712295857e-8
    q = n.astype(jnp.int32) & 3
    z = r * r
    sn = r + r * z * (-1.6666654611e-1 + z * (8.3321608736e-3 + z * -1.9515295891e-4))
    cs = 1.0 - 0.5 * z + z * z * (
        4.166664568298827e-2 + z * (-1.388731625493765e-3 + z * 2.443315711809948e-5)
    )
    odd = (q & 1) == 1
    c0 = jnp.where(odd, sn, cs)
    s0 = jnp.where(odd, cs, sn)
    cos = jnp.where((q == 1) | (q == 2), -c0, c0)
    sin = jnp.where(q >= 2, -s0, s0)
    return cos, sin


def eighth_turns(c):
    step = (lax.broadcasted_iota(jnp.int32, (8, 512), 1) & 7) * c
    side = 0.5**0.5
    cos = jnp.where(step == 0, 1.0, jnp.where(step == 4, -1.0, 0.0))
    cos = jnp.where((step == 1) | (step == 7), side, cos)
    cos = jnp.where((step == 3) | (step == 5), -side, cos)
    sin = jnp.where(step == 2, 1.0, jnp.where(step == 6, -1.0, 0.0))
    sin = jnp.where((step == 1) | (step == 3), side, sin)
    sin = jnp.where((step == 5) | (step == 7), -side, sin)
    return cos[0:1, :], sin[0:1, :]


def spot_of(idx, d, e=0):
    return lax.rem(idx[0] + d, 4), lax.rem(idx[1] + e, 2)


def from_of(idx, d, e=0):
    return lax.rem(idx[0] + 4 - d, 4), lax.rem(idx[1] + 2 - e, 2)


def aligned(x, by):
    return pl.multiple_of(x * by, by)


def call(kernel, operands, in_smem, outs, scratch=(), apart=()):
    specs = []
    for at in range(len(operands)):
        space = pltpu.SMEM if at in in_smem else pltpu.VMEM
        specs.append(pl.BlockSpec(memory_space=pltpu.HBM if at in apart else space))
    return pl.pallas_call(
        kernel,
        out_shape=[jax.ShapeDtypeStruct(shape, F32) for shape in outs],
        in_specs=specs,
        out_specs=[pl.BlockSpec(memory_space=pltpu.VMEM) for _ in outs],
        scratch_shapes=list(scratch),
        compiler_params=pltpu.CompilerParams(vmem_limit_bytes=20 * 1024 * 1024),
    )(*operands)


relations = [(d, e) for e in range(2) for d in range(4)]


def ratio_of(wave):
    return 550.0 / (400.0 + 10.0 * jnp.full((8, 128), wave, jnp.int32).astype(F32))


def mats_of(ref):
    return ref[0], ref[1], ref[2], ref[3]


def phase_kernel(idx, phases, own, sent, grid):
    grid[...] = jnp.transpose(phases[...])
    kept = aligned(jnp.where(idx[0] == 1, 1, 0), 128)
    given = aligned(jnp.where(idx[0] == 1, 0, 1), 128)
    own[...] = grid[pl.ds(kept, 128), :]
    sent[...] = grid[pl.ds(given, 128), :]


def scene_kernel(idx, scene, other, w, out, strip, edge, image, grid):
    owner = idx[2] == 1
    c = idx[1]
    part = pl.ds(aligned(15 * c, 8), 136)
    rows = jnp.where(owner, scene[0, part, :], other[0, part, :])
    strip[...] = rows[:, 256:384]
    edge[...] = jnp.where(c == 0, rows[0:8, 256:384], rows[128:136, 256:384])
    image[...] = jnp.transpose(jnp.where(c == 0, rows[0:128], rows[8:136]))
    spectrum = by_left(w[0], w[1], image[...])
    grid[0] = spectrum[:512]
    grid[1] = spectrum[512:]
    eight_rows(out, grid)


def pupil_kernel(idx, *refs):
    m, o0, o1, o2, o3, pupil, grid = refs[4:]
    s = idx[0]
    c = idx[1]
    owner = idx[2] == 1
    central = (s == 1) | (s == 2)
    own, got, own_far, got_far = [ref[...] for ref in refs[:4]]
    phase = jnp.where(central, jnp.where(owner, own, own_far), jnp.where(owner, got, got_far))
    rows = lax.broadcasted_iota(jnp.int32, (128, 512), 0) + s * 128
    cols = lax.broadcasted_iota(jnp.int32, (128, 512), 1)
    across = (rows + 256) * 2 - N + 1
    down = (cols + 256) * 2 - N + 1
    inside = (down * down + across * across) * 4 <= N * N
    cos, sin = cos_sin(phase)
    re = jnp.where(inside, cos, 0.0)
    im = jnp.where(inside, sin, 0.0)
    pupil[0] = re
    pupil[1] = im
    turn_cos, turn_sin = eighth_turns(c)
    re, im = times(re, im, turn_cos, -turn_sin)
    out_re, out_im = dft_right(re, im, mats_of(m), -1.0)
    grid[0] = out_re
    grid[1] = out_im
    for d, out in enumerate((o0, o1, o2, o3)):
        to = spot_of(idx, d)[0]
        out[...] = grid[:, :, pl.ds(aligned(to, 128), 128)]


def eight_rows(out, grid):
    for c in range(2):
        for s in range(4):
            row = 128 * s + 64 * c
            out[4 * c + s, 0:2] = grid[:, row : row + 64, :]


def eight_columns(out, grid):
    for c in range(2):
        for s in range(4):
            col = 128 * (2 * s + c)
            out[4 * c + s] = grid[:, :, col : col + 128]


def optics_kernel(scale, idx, b0, b1, b2, b3, scene, *refs):
    f, tw, far, out, grid = refs
    for d, block in enumerate((b0, b1, b2, b3)):
        grid[:, pl.ds(aligned(from_of(idx, d)[0], 128), 128), :] = block[...]
    low = (grid[0, :256, :], grid[1, :256, :])
    high = (grid[0, 256:, :], grid[1, 256:, :])
    twists = [(tw[:, r : r + 1], tw[:, 4 + r : 5 + r]) for r in range(4)]
    res, ims = [], []
    for r in range(4):
        add = turned(high[0], high[1], -r)
        re, im = low[0] + add[0], low[1] + add[1]
        if r:
            re, im = times(re, im, twists[r][0], -twists[r][1])
        res.append(re)
        ims.append(im)
    mats = mats_of(f)
    far_re, far_im = dft_left(
        jnp.concatenate(res, 1), jnp.concatenate(ims, 1), mats, -1.0
    )
    far[0] = far_re
    far[1] = far_im
    psf = scale * (far_re * far_re + far_im * far_im)
    psf_high, psf_low = split(psf)
    z_re = dot(mats[0], psf_high) + (dot(mats[1], psf_high) + dot(mats[0], psf_low))
    z_im = -(dot(mats[2], psf_high) + (dot(mats[3], psf_high) + dot(mats[2], psf_low)))
    first = [None, None]
    second = [None, None]
    nyquist = None
    for r in range(4):
        re = z_re[:, r * 128 : r * 128 + 128]
        im = z_im[:, r * 128 : r * 128 + 128]
        top = re[0:1, :]
        nyquist = top if r == 0 else (nyquist + top if r % 2 == 0 else nyquist - top)
        if r:
            re, im = times(re, im, twists[r][0], -twists[r][1])
        more = turned(re, im, -r)
        first = [re, im] if r == 0 else [first[0] + re, first[1] + im]
        second = list(more) if r == 0 else [second[0] + more[0], second[1] + more[1]]
    row = lax.broadcasted_iota(jnp.int32, (256, 128), 0)
    grid[0, :256, :] = first[0]
    grid[1, :256, :] = jnp.where(row == 0, nyquist, first[1])
    grid[0, 256:, :] = second[0]
    grid[1, 256:, :] = second[1]
    eight_rows(out, grid)
    for at in range(8):
        out[at, 2:4] = scene[at]


def unpack_rows(idx, re, im, tail):
    rows = lax.broadcasted_iota(jnp.int32, re.shape, 0)
    first = (idx[0] + idx[1]) == 0
    nyquist = jnp.where(first, im[0:1, :], 0.0)
    tail_rows = lax.broadcasted_iota(jnp.int32, (tail, re.shape[1]), 0)
    extra = jnp.where(tail_rows == 0, nyquist, 0.0)
    im = jnp.where((rows == 0) & first, 0.0, im)
    return jnp.concatenate([re, extra], 0), jnp.concatenate([im, jnp.zeros_like(extra)], 0)


def repack_rows(idx, re, im):
    first = (idx[0] + idx[1]) == 0
    rows = lax.broadcasted_iota(jnp.int32, (64, re.shape[1]), 0)
    return re[:64], jnp.where((rows == 0) & first, re[64:65, :], im[:64])


def row_transform(idx, blocks, first, mats, tw, grid):
    for c in range(2):
        for s in range(4):
            col = 128 * (2 * s + c)
            grid[:, :, col : col + 128] = blocks[4 * c + s, first : first + 2]
    return rows_out(idx, grid[0], grid[1], mats, tw)


def rows_back(idx, re, im, mats, tw, grid):
    re, im = dft_right(re, im, mats, 1.0)
    parts = []
    for r in range(4):
        a, b = re[r * 72 : r * 72 + 72], im[r * 72 : r * 72 + 72]
        if r:
            a, b = times(a, b, tw[r : r + 1, :], tw[4 + r : 5 + r, :])
        parts.append((a, b))
    for q in range(4):
        a, b = parts[0]
        for r in range(1, 4):
            more = turned(parts[r][0], parts[r][1], q * r)
            a = a + more[0]
            b = b + more[1]
        a, b = repack_rows(idx, a, b)
        grid[0, :, q * 256 : q * 256 + 256] = a
        grid[1, :, q * 256 : q * 256 + 256] = b


def rows_out(idx, re, im, mats, tw):
    re, im = unpack_rows(idx, re, im, 8)
    quarters = [(re[:, q * 256 : q * 256 + 256], im[:, q * 256 : q * 256 + 256]) for q in range(4)]
    sum02 = [quarters[0][p] + quarters[2][p] for p in range(2)]
    dif02 = [quarters[0][p] - quarters[2][p] for p in range(2)]
    sum13 = [quarters[1][p] + quarters[3][p] for p in range(2)]
    dif13 = [quarters[1][p] - quarters[3][p] for p in range(2)]
    step = turned(dif13[0], dif13[1], -1)
    parts = [
        (sum02[0] + sum13[0], sum02[1] + sum13[1]),
        (dif02[0] + step[0], dif02[1] + step[1]),
        (sum02[0] - sum13[0], sum02[1] - sum13[1]),
        (dif02[0] - step[0], dif02[1] - step[1]),
    ]
    for r in range(1, 4):
        parts[r] = times(parts[r][0], parts[r][1], tw[r : r + 1, :], -tw[4 + r : 5 + r, :])
    return dft_right(
        jnp.concatenate([p[0] for p in parts], 0),
        jnp.concatenate([p[1] for p in parts], 0),
        mats,
        -1.0,
    )


def blur_kernel(idx, blocks, f, tw, out, spectrum, grid, turned_grid):
    mats = mats_of(f)
    re, im = row_transform(idx, blocks, 2, mats, tw, grid)
    spectrum[0] = re
    spectrum[1] = im
    re, im = row_transform(idx, blocks, 0, mats, tw, grid)
    re, im = times(re, im, spectrum[0], spectrum[1])
    rows_back(idx, re, im, mats, tw, grid)
    both = jnp.transpose(jnp.concatenate([grid[0], grid[1]], 0))
    turned_grid[8 : N + 8, :] = both
    turned_grid[0:8, :] = both[N - 8 :, :]
    turned_grid[N + 8 :, :] = both[:8, :]
    for c in range(2):
        for s in range(4):
            row = 128 * (2 * s + c)
            out[4 * c + s] = turned_grid[row : row + ROWS, :]


def moved_lanes(x, e, lanes):
    if e == 0:
        return x
    rolled = pltpu.roll(x, (-e) % 128, 1)
    return jnp.where(lanes == (127 if e > 0 else 0), 0.0, rolled)


def moved_rows(x, a):
    if a == 0:
        return x
    return pltpu.roll(x, (-a) % x.shape[0], 0)


ROWS = 144


def row_pair(ref, row):
    parts = [ref[:, at : at + 8, :] for at in (row, row + 8)]
    return jnp.concatenate([part.reshape(part.shape[0] * 8, 128) for part in parts], 1)


def dot_rows(a, b):
    return lax.dot_general(a, b, (((1,), (1,)), ((), ())), preferred_element_type=F32)


def by_rows(a, b):
    a_high, a_low = split(a)
    b_high, b_low = split(b)
    return dot_rows(a_high, b_high) + (dot_rows(a_high, b_low) + dot_rows(a_low, b_high))


def same_rows(x):
    rows = lax.broadcasted_iota(jnp.int32, x.shape, 0)
    cols = lax.broadcasted_iota(jnp.int32, x.shape, 1)
    kept = jnp.where((rows & 7) == (cols & 7), x, 0.0)
    return jnp.sum(kept.reshape(32, 8, x.shape[1]), 1)


def net_kernel(pixel_count, idx, w1, b1, w2, *refs):
    blocks, f, strip, edge, g_out, sums_out = refs[:6]
    win_taps, g_taps, hidden, sums, g_pre = refs[6:]
    target = jnp.where(
        idx[1] == 0,
        jnp.concatenate([edge[...], strip[...]], 0),
        jnp.concatenate([strip[...], edge[...]], 0),
    )
    window = None
    for at in range(4):
        part = by_right(
            jnp.concatenate([blocks[2 * at], blocks[2 * at + 1]], 1),
            f[4 + at // 2, :, 128 * (at % 2) : 128 * (at % 2) + 128],
            f[6 + at // 2, :, 128 * (at % 2) : 128 * (at % 2) + 128],
        )
        window = part if window is None else window + part
    rows = lax.broadcasted_iota(jnp.int32, (ROWS, 128), 0)
    lanes = lax.broadcasted_iota(jnp.int32, (ROWS, 128), 1)
    row_global = rows + (2 * idx[0] + idx[1]) * 128 - 8
    inside = (row_global >= 0) & (row_global < N)
    window = jnp.where(inside, window, 0.0)
    for e in (-1, 0, 1):
        side = moved_lanes(window, e, lanes)
        for a in (-1, 0, 1):
            win_taps[3 * (a + 1) + e + 1] = moved_rows(side, a)
    step = 48
    for k in range(ROWS // step):
        part = pl.ds(k * step, step)

        def forward(c, total, part=part):
            pre = w1[c, 0] * win_taps[0, part, :]
            for t in range(1, 9):
                pre = pre + w1[c, t] * win_taps[t, part, :]
            hid = jnp.maximum(pre + b1[c], 0.0)
            hidden[c, part, :] = hid
            return tuple(total[t] + w2[t, c] * hid for t in range(9))

        total = lax.fori_loop(
            0, 32, forward, tuple(jnp.zeros((step, 128), F32) for _ in range(9)), unroll=32
        )
        for t in range(9):
            sums[t, part, :] = total[t]
    restored = window
    for e in (-1, 0, 1):
        side = None
        for a in (-1, 0, 1):
            part = moved_rows(jnp.where(inside, sums[3 * (a + 1) + e + 1], 0.0), a)
            side = part if side is None else side + part
        restored = restored + moved_lanes(side, e, lanes)
    residual = jnp.where(inside, restored - target, 0.0)
    own = (rows >= 8) & (rows < 136)
    own_residual = jnp.where(own, residual, 0.0)
    loss = jnp.sum(own_residual * own_residual, keepdims=True)
    g_restored = (2.0 / pixel_count) * residual
    for e in (-1, 0, 1):
        side = moved_lanes(g_restored, -e, lanes)
        for a in (-1, 0, 1):
            g_taps[3 * (a + 1) + e + 1] = jnp.where(inside, moved_rows(side, -a), 0.0)
    for k in range(ROWS // step):
        part = pl.ds(k * step, step)

        def backward(c, total, part=part):
            gh = w2[0, c] * g_taps[0, part, :]
            for t in range(1, 9):
                gh = gh + w2[t, c] * g_taps[t, part, :]
            gp = jnp.where(hidden[c, part, :] > 0.0, gh, 0.0)
            g_pre[c, part, :] = gp
            return tuple(total[t] + w1[c, t] * gp for t in range(9))

        total = lax.fori_loop(
            0, 32, backward, tuple(jnp.zeros((step, 128), F32) for _ in range(9)), unroll=32
        )
        for t in range(9):
            sums[t, part, :] = total[t]
    g_window = g_restored
    for e in (-1, 0, 1):
        side = None
        for a in (-1, 0, 1):
            part = moved_rows(sums[3 * (a + 1) + e + 1], -a)
            side = part if side is None else side + part
        g_window = g_window + moved_lanes(side, -e, lanes)
    g_out[...] = g_window[8:136]
    first, second = None, None
    for row in range(0, 128, 16):
        with_taps = jnp.concatenate(
            [row_pair(win_taps, row + 8), jnp.ones((8, 256), F32)], 0
        )
        one = by_rows(row_pair(g_pre, row + 8), with_taps)
        two = by_rows(row_pair(hidden, row + 8), row_pair(g_taps, row + 8))
        first = one if first is None else first + one
        second = two if second is None else second + two
    sums_out[...] = jnp.zeros_like(sums_out)
    sums_out[:, 0:80] = same_rows(first)
    sums_out[:, 80:88] = jnp.broadcast_to(loss * 0.125, (32, 8))
    sums_out[:, 128:200] = same_rows(second)


def otf_grad_kernel(idx, *refs):
    blocks = refs[:8]
    f, tw, spectrum, out, window, grid = refs[8:]
    for d, e in relations:
        s, c = from_of(idx, d, e)
        window[pl.ds(aligned(2 * s + c, 128), 128), :] = blocks[4 * e + d][...]
    rows = pl.ds(aligned(lax.rem(idx[0], 2), 128), 128)
    cols = pl.ds(aligned(idx[1], 128), 128)
    at = lax.div(idx[0], 2)
    packed = jnp.transpose(by_right(window[...], f[8 + at, rows, cols], f[10 + at, rows, cols]))
    mats = mats_of(f)
    re, im = rows_out(idx, packed[:64], packed[64:], mats, tw)
    re, im = times(re, im, spectrum[0], -spectrum[1])
    rows_back(idx, re, im, mats, tw, grid)
    eight_columns(out, grid)


def psf_grad_kernel(idx, blocks, far, f, tw, small, o0, o1, o2, o3, grid):
    for c in range(2):
        for s in range(4):
            grid[:, 128 * s + 64 * c : 128 * s + 64 * c + 64, :] = blocks[4 * c + s]
    row = lax.broadcasted_iota(jnp.int32, (256, 128), 0)
    zero_row = row == 0
    low_re, low_im = grid[0, :256, :], grid[1, :256, :]
    nyquist = jnp.where(zero_row, 0.5 * low_im, 0.0)
    low_re = jnp.where(zero_row, 0.5 * low_re, low_re)
    low_im = jnp.where(zero_row, 0.0, low_im)
    high = (grid[0, 256:, :], grid[1, 256:, :])
    twists = [(tw[:, r : r + 1], tw[:, 4 + r : 5 + r]) for r in range(4)]
    res, ims = [], []
    for r in range(4):
        add = turned(high[0], high[1], r)
        re, im = low_re + add[0], low_im + add[1]
        if r:
            re, im = times(re, im, twists[r][0], twists[r][1])
        re = re + nyquist if r % 2 == 0 else re - nyquist
        res.append(re)
        ims.append(im)
    mats = mats_of(f)
    g_psf = 2.0 * (
        by_left(mats[0], mats[1], jnp.concatenate(res, 1))
        - by_left(mats[2], mats[3], jnp.concatenate(ims, 1))
    )
    re, im = dft_left(g_psf * far[0], g_psf * far[1], mats, 1.0)
    first, second = None, None
    for r in range(4):
        a, b = re[:, r * 128 : r * 128 + 128], im[:, r * 128 : r * 128 + 128]
        if r:
            a, b = times(a, b, twists[r][0], twists[r][1])
        more = turned(a, b, r)
        first = [a, b] if r == 0 else [first[0] + a, first[1] + b]
        second = list(more) if r == 0 else [second[0] + more[0], second[1] + more[1]]
    for p in range(2):
        grid[p, :256, :] = first[p]
        grid[p, 256:, :] = second[p]
    for d, out in enumerate((o0, o1, o2, o3)):
        out[:, 0:128, :] = grid[:, pl.ds(aligned(spot_of(idx, d)[0], 128), 128), :]
        out[0, 128:136, :] = small[...]
        out[1, 128:136, :] = small[...]


def mask_grad_kernel(scale, idx, ids, got, *refs):
    b0, b1, b2, b3, m, pupil, keep, send, grid, whole = refs
    small = None
    for d, block in enumerate((b0, b1, b2, b3)):
        grid[:, :, pl.ds(aligned(from_of(idx, d)[0], 128), 128)] = block[:, 0:128, :]
        part = jnp.concatenate([block[0, 128:136, :], block[1, 128:136, :]], 1)
        small = part if small is None else small + part
    re, im = dft_right(grid[0], grid[1], mats_of(m), 1.0)
    turn_cos, turn_sin = eighth_turns(idx[1])
    re, im = times(re, im, turn_cos, turn_sin)
    factor = ratio_of(jnp.where(idx[2] == 1, ids[1], got[1]))[0:1, 0:1] * scale
    whole[...] = factor * (im * pupil[0] - re * pupil[1])
    keep[0:128, :] = whole[:, pl.ds(aligned(idx[1], 256), 256)]
    send[0:128, :] = whole[:, pl.ds(aligned(1 - idx[1], 256), 256)]
    keep[128:136, :] = small
    send[128:136, :] = small


def cut_kernel(ways, idx, keep, other, *refs):
    outs = refs[:ways]
    whole = refs[ways]
    whole[...] = keep[...] + other[...]
    piece = 128 // ways
    for d, out in enumerate(outs):
        to = lax.rem(idx[3] + d, ways)
        out[0:piece, :] = whole[pl.ds(aligned(to, piece), piece), :]
        out[piece : piece + 8, :] = whole[128:136, :]


def home_kernel(ways, pixel_count, idx, small, *refs):
    near, far, out, w1_out, b1_out, w2_out, loss_out, grid = refs
    piece = 128 // ways
    first = idx[1] == 0
    for y in range(ways):
        for h in range(2):
            row = 128 * h + piece * y
            a, b = near[y, h], far[y, h]
            grid[row : row + piece, 0:256] = jnp.where(first, a, b)
            grid[row : row + piece, 256:512] = jnp.where(first, b, a)
    central = (idx[0] == 1) | (idx[0] == 2)
    out[0:256, :] = jnp.zeros((256, 256), F32)
    out[768:1024, :] = jnp.zeros((256, 256), F32)
    out[256:768, :] = jnp.where(central, jnp.transpose(grid[...]), 0.0)
    flat = jnp.concatenate([small[:, 32 * g : 32 * g + 32] for g in range(4)], 0)
    w1_out[...] = flat[0:9, :]
    w2_out[...] = flat[16:25, :]
    b1_out[...] = flat[9:10, :]
    loss_out[...] = flat[10:11, 0:1] / pixel_count


def on_device(lay, phase_mask, height_offsets, sample_ids, wave_ids, scene, w1, b1, w2):
    con = constants()
    s = lax.axis_index("sp")
    c = lax.axis_index("core")
    y = lax.axis_index("y")
    owner = c == lax.axis_index("grp")
    pixel_count = float(lay.dp * N * 128)
    scale_psf = 1.0 / (N * N * pupil_count(N))
    idx = jnp.stack([s, c, owner.astype(jnp.int32), y]).astype(jnp.int32)

    def swap(g, zh, y, c, s):
        return (g, zh, y, 1 - c, s)

    def along_sp(blocks):
        return [blocks[0]] + [
            lay.move(blocks[d], lambda g, zh, y, c, s, d=d: (g, zh, y, c, s + d))
            for d in (1, 2, 3)
        ]

    def to_eight(blocks):
        return lax.all_to_all(blocks, ("core", "sp"), 0, 0, tiled=True)

    def gathered(block):
        near = along_sp([block] * 4)
        return near + [lay.move(part, swap) for part in near]

    ids = jnp.concatenate([sample_ids, wave_ids])
    got = lay.move(ids, swap)
    grabbed = lax.dynamic_slice(height_offsets, (ids[0], 256, 0), (1, 512, 256))[0]
    ratio = 550.0 / (400.0 + 10.0 * ids[1].astype(F32))
    phases = ratio * (phase_mask[256:768] + 0.1 * grabbed.astype(F32))

    mine = call(
        phase_kernel,
        (idx, phases),
        (0,),
        [(128, 512)] * 2,
        [pltpu.VMEM((256, 512), F32)],
    )
    pieces = list(mine[:1]) + [
        lay.move(
            block,
            lambda g, zh, y, c, s: (
                (g, zh, y, c, {1: 0, 2: 3}[s]) if s in (1, 2) and c == g else None
            ),
        )
        for block in mine[1:]
    ]
    pieces += [
        lay.move(
            block,
            lambda g, zh, y, c, s, inner=inner: (
                (g, zh, y, 1 - c, s) if c == g and (s in (1, 2)) == inner else None
            ),
        )
        for block, inner in zip(pieces, (True, False))
    ]


    *field, pupil = call(
        pupil_kernel,
        (idx, *pieces, con["m"]),
        (0,),
        [(2, 128, 128)] * 4 + [(2, 128, 512)],
        [pltpu.VMEM((2, 128, 512), F32)],
    )
    scene, pupil = lax.optimization_barrier((scene, pupil))
    other = lay.move(
        scene, lambda g, zh, y, c, s: (g, zh, y, 1 - c, s) if c == g else None
    )
    field = along_sp(field)

    scene_part, strip, edge = call(
        scene_kernel,
        (idx, scene, other, con["pack"]),
        (0,),
        [(8, 2, 64, 128), (136, 128), (8, 128)],
        [
            pltpu.VMEM((N, 128), F32),
            pltpu.VMEM((2, 512, 128), F32),
        ],
    )
    edge = lay.move(
        edge,
        lambda g, zh, y, c, s: (
            (g, zh, y, 1 - c, s - 1 + 2 * c) if 0 <= s - 1 + 2 * c < 4 else None
        ),
    )
    far, parts = call(
        functools.partial(optics_kernel, scale_psf),
        (idx, *field, scene_part, con["f"], con["tw_col"]),
        (0,),
        [(2, 256, 512), (8, 4, 64, 128)],
        [
            pltpu.VMEM((2, 512, 128), F32),
        ],
    )
    parts, edge = lax.optimization_barrier((to_eight(parts), edge))
    blurred, spectrum = call(
        blur_kernel,
        (idx, parts, con["f"], con["tw_row"]),
        (0,),
        [(8, ROWS, 128), (2, 288, 256)],
        [
            pltpu.VMEM((2, 64, N), F32),
            pltpu.VMEM((N + 16, 128), F32),
        ],
    )
    blurred = to_eight(blurred)
    g_window, sums = call(
        functools.partial(net_kernel, pixel_count),
        (idx, w1, b1, w2, blurred, con["f"], strip, edge),
        (0, 1, 2, 3),
        [(128, 128), (32, 256)],
        [
            pltpu.VMEM((9, ROWS, 128), F32),
            pltpu.VMEM((9, ROWS, 128), F32),
            pltpu.VMEM((32, ROWS, 128), F32),
            pltpu.VMEM((9, ROWS, 128), F32),
            pltpu.VMEM((32, ROWS, 128), F32),
        ],
    )
    small = jnp.sum(sums.reshape(32, 4, 8, 8), 3).transpose(2, 1, 0).reshape(8, 128)
    g_parts = gathered(g_window)
    (otf_grad,) = call(
        otf_grad_kernel,
        (idx, *g_parts, con["f"], con["tw_row"], spectrum),
        (0,),
        [(8, 2, 64, 128)],
        [
            pltpu.VMEM((N, 128), F32),
            pltpu.VMEM((2, 64, N), F32),
        ],
    )
    otf_grad = to_eight(otf_grad)
    field_grad = along_sp(
        call(
            psf_grad_kernel,
            (idx, otf_grad, far, con["f"], con["tw_col"], small),
            (0,),
            [(2, 136, 128)] * 4,
            [
                pltpu.VMEM((2, 512, 128), F32),
            ],
        )
    )
    keep, send = call(
        functools.partial(mask_grad_kernel, 2.0 * scale_psf),
        (idx, ids, got, *field_grad, con["m_back"], pupil),
        (0, 1, 2),
        [(136, 256)] * 2,
        [
            pltpu.VMEM((2, 128, 512), F32),
            pltpu.VMEM((128, 512), F32),
        ],
    )

    piece = 128 // lay.y
    blocks = call(
        functools.partial(cut_kernel, lay.y),
        (idx, keep, lay.move(send, swap)),
        (0,),
        [(piece + 8, 256)] * lay.y,
        [pltpu.VMEM((136, 256), F32)],
    )
    total = blocks[0]
    for d in range(1, lay.y):
        total = total + lay.move(
            blocks[d], lambda g, zh, y, c, s, d=d: (g, zh, y + d, c, s)
        )
    total = total + lay.move(total, lambda g, zh, y, c, s: (1 - g, zh, y, c, s))
    part = total
    for d in range(1, lay.zh):
        total = total + lay.move(part, lambda g, zh, y, c, s, d=d: (g, zh + d, y, c, s))
    part = total[:piece]
    near_part = lay.move(
        part, lambda g, zh, y, c, s: (g, zh, y, c, {0: 1, 3: 2}[s]) if s in (0, 3) else None
    )
    home = jnp.where(s == 1, jnp.stack([near_part, part]), jnp.stack([part, near_part]))
    near = lax.all_to_all(
        jnp.broadcast_to(home, (lay.y, 2, piece, 256)), "y", 0, 0, tiled=True
    )
    far = lay.move(
        near, lambda g, zh, y, c, s: (g, zh, y, 1 - c, s) if s in (1, 2) else None
    )
    mask_grad, w1_grad, b1_grad, w2_grad, loss = call(
        functools.partial(home_kernel, lay.y, pixel_count),
        (idx, total[piece:], near, far),
        (0,),
        [(N, 256), (9, 32), (1, 32), (9, 32), (1, 1)],
        [pltpu.VMEM((256, 512), F32)],
    )
    return mask_grad, w1_grad.T, b1_grad.reshape(32), w2_grad, loss.reshape(())


def solution(mesh):
    lay = Layout(mesh)
    images = ("zh", "y", "core")
    placed = (
        P(None, "sp"),
        P(None, None, "sp"),
        P(images),
        P(images),
        P(images, "sp", None),
        P(),
        P(),
        P(),
    )
    return jax.shard_map(
        functools.partial(on_device, lay),
        mesh=lay.mesh,
        in_specs=placed,
        out_specs=(P(None, "sp"), P(), P(), P(), P()),
        check_vma=False,
    )
```
